32 devices in a mesh: dp: 8 (over z, y), seq: 4 (over x, core).
Axes of the slice: x: 2, y: 2, z: 4, core: 2. Of those that a mesh axis runs over, the one named last changes fastest.
Arguments:
- layer_input: bfloat16 [16, 2048, 768], P('dp', 'seq'), may hold values from -10 to 10
- cotangent: bfloat16 [16, 2048, 768], P('dp', 'seq'), may hold values from -6 to 6
- attn_master: float32 [768, 4, 768], P('dp'), may hold values from -2.309401 to 2.309401
- up_master: float32 [768, 3072], P('dp'), may hold values from -0.21875 to 0.21875
- down_master: float32 [3072, 768], P('dp'), may hold values from -0.109375 to 0.109375
- norm_params: float32 [4, 768], replicated, may hold values from -1.5 to 2.4
- attn_first: float32 [768, 4, 768], P('dp'), may hold values from -0.005859375 to 0.005859375
- up_first: float32 [768, 3072], P('dp'), may hold values from -0.005859375 to 0.005859375
- down_first: float32 [3072, 768], P('dp'), may hold values from -0.005859375 to 0.005859375
- norm_first: float32 [4, 768], replicated, may hold values from -0.005859375 to 0.005859375
- attn_second: float32 [768, 4, 768], P('dp'), may hold values from 1.4128508e-07 to 5.6514034e-07
- up_second: float32 [768, 3072], P('dp'), may hold values from 1.4128508e-07 to 5.6514034e-07
- down_second: float32 [3072, 768], P('dp'), may hold values from 1.4128508e-07 to 5.6514034e-07
- norm_second: float32 [4, 768], replicated, may hold values from 1.4128508e-07 to 5.6514034e-07
Outputs:
- layer_output: bfloat16 [16, 2048, 768], P('dp', 'seq')
- input_grad: float32 [16, 2048, 768], P('dp', 'seq')
- attn_grad: float32 [768, 4, 768], P('dp')
- up_grad: float32 [768, 3072], P('dp')
- down_grad: float32 [3072, 768], P('dp')
- norm_grad: float32 [4, 768], replicated
- grad_norm: float32 [], replicated
- attn_new: float32 [768, 4, 768], P('dp')
- up_new: float32 [768, 3072], P('dp')
- down_new: float32 [3072, 768], P('dp')
- norm_new: float32 [4, 768], replicated
- attn_first_new: float32 [768, 4, 768], P('dp')
- up_first_new: float32 [768, 3072], P('dp')
- down_first_new: float32 [3072, 768], P('dp')
- norm_first_new: float32 [4, 768], replicated
- attn_second_new: float32 [768, 4, 768], P('dp')
- up_second_new: float32 [768, 3072], P('dp')
- down_second_new: float32 [3072, 768], P('dp')
- norm_second_new: float32 [4, 768], replicated
The draws below stay inside these ranges and needn't reach their ends.
All inputs are finite; a program needn't handle non-finite values.
Results may differ from the reference program's by a relative error of at most 0.018.
Values may be sent and summed in bfloat16 or wider, within the bound.
A program may use at most 256 MiB of HBM per device.

```python
import math
import jax
import jax.numpy as jnp
from jax import lax

D = 768
HEADS = 12
HEAD = 64
FF = 3072
STEP = 5
SEQLEN = 2048
SEQS = 16
N_SEQ = 4


def draw_layer_input(key, part):
    key = jax.random.fold_in(key, 11)
    feature = jnp.arange(D, dtype=jnp.float32) / (D - 1)
    feature_scale = 0.6 + 1.2 * feature
    random_part = jnp.clip(jax.random.normal(key, (SEQS, SEQLEN, D), jnp.float32), -5.5, 5.5)
    return (random_part * feature_scale).astype(jnp.bfloat16)


def draw_attn_master(key, part):
    key = jax.random.fold_in(key, 12)
    standard = jnp.clip(jax.random.normal(key, (D, 4, D), jnp.float32), -4.0, 4.0)
    column = jnp.array([1.0, 1.0, 1.0, (SEQLEN // 8) ** 0.5], jnp.float32)
    return standard * column[None, :, None] * D ** (-0.5)


def draw_norm_params(key, part):
    key = jax.random.fold_in(key, 13)
    first_key, second_key = jax.random.split(key)
    feature = jnp.arange(D, dtype=jnp.float32) / (D - 1)
    rising = 0.6 + 1.2 * feature
    jitter = jnp.clip(0.1 * jax.random.normal(first_key, (2, D), jnp.float32), -0.3, 0.3)
    offsets = jnp.clip(0.3 * jax.random.normal(second_key, (2, D), jnp.float32), -1.5, 1.5)
    gain_rows = rising[None, :] * (1.0 + jitter)
    return jnp.stack([gain_rows[0], offsets[0], gain_rows[1], offsets[1]])


def levels(own_key, dims, cuts, low, top_value):
    factor_of = 1.0
    for position, shards_of in cuts:
        heights = jax.random.uniform(jax.random.fold_in(jax.random.fold_in(own_key, 6), position), (shards_of,), jnp.float32, low / len(cuts), top_value / len(cuts))
        factor_of = factor_of * jnp.repeat(jnp.exp(heights), dims[position] // shards_of).reshape((-1,) + (1,) * (len(dims) - 1 - position))
    return factor_of


def bell_draw(own_key, shape, deviation, bound, pieces=(), kind=jnp.bfloat16):
    values = deviation * jax.random.normal(own_key, shape, jnp.float32)
    if pieces:
        values = values * levels(own_key, shape, pieces, -0.22, 0.18)
    return jnp.clip(values, -bound, bound).astype(kind)


def setup_inputs(seed: int = 0) -> dict:
    arg_keys = jax.random.split(jax.random.key(seed), 15)
    layer_input = draw_layer_input(jax.random.fold_in(arg_keys[14], 71), 0)
    cotangent = bell_draw(arg_keys[1], (SEQS, SEQLEN, D), 1.0, 6.0, ((0, 8), (1, 4)))
    attn_master = draw_attn_master(jax.random.fold_in(arg_keys[14], 71), 0)
    up_master = bell_draw(arg_keys[3], (D, FF), D ** -0.5, 0.21875, ((0, 8),), jnp.float32)
    down_master = bell_draw(arg_keys[4], (FF, D), FF ** -0.5, 0.109375, ((0, 8),), jnp.float32)
    norm_params = draw_norm_params(jax.random.fold_in(arg_keys[14], 71), 0)
    attn_first = bell_draw(arg_keys[6], (D, 4, D), ((4 * D * D + 2 * D * FF) ** -0.5), 0.005859375, ((0, 8),), jnp.float32)
    up_first = bell_draw(arg_keys[7], (D, FF), ((4 * D * D + 2 * D * FF) ** -0.5), 0.005859375, ((0, 8),), jnp.float32)
    down_first = bell_draw(arg_keys[8], (FF, D), ((4 * D * D + 2 * D * FF) ** -0.5), 0.005859375, ((0, 8),), jnp.float32)
    norm_first = bell_draw(arg_keys[9], (4, D), ((4 * D * D + 2 * D * FF) ** -0.5), 0.005859375, (), jnp.float32)
    attn_second = jnp.clip(jnp.exp(math.log(5.651403398587718e-07) - 1.3862944 * jax.random.uniform(arg_keys[10], (D, 4, D), jnp.float32) ** levels(arg_keys[10], (D, 4, D), ((0, 8),), -0.2, 0.2)), 1.4128508496469294e-07, 5.651403398587718e-07)
    up_second = jnp.clip(jnp.exp(math.log(5.651403398587718e-07) - 1.3862944 * jax.random.uniform(arg_keys[11], (D, FF), jnp.float32) ** levels(arg_keys[11], (D, FF), ((0, 8),), -0.2, 0.2)), 1.4128508496469294e-07, 5.651403398587718e-07)
    down_second = jnp.clip(jnp.exp(math.log(5.651403398587718e-07) - 1.3862944 * jax.random.uniform(arg_keys[12], (FF, D), jnp.float32) ** levels(arg_keys[12], (FF, D), ((0, 8),), -0.2, 0.2)), 1.4128508496469294e-07, 5.651403398587718e-07)
    norm_second = jnp.clip(jnp.exp(jax.random.uniform(arg_keys[13], (4, D), jnp.float32, math.log(1.4128508496469294e-07), math.log(5.651403398587718e-07))), 1.4128508496469294e-07, 5.651403398587718e-07)
    return {"layer_input": layer_input, "cotangent": cotangent, "attn_master": attn_master, "up_master": up_master, "down_master": down_master, "norm_params": norm_params, "attn_first": attn_first, "up_first": up_first, "down_first": down_first, "norm_first": norm_first, "attn_second": attn_second, "up_second": up_second, "down_second": down_second, "norm_second": norm_second}


highest = lax.Precision.HIGHEST
beta_one = 0.5
beta_two = 0.5
learn_rate = 0.02
gain_rate = 0.2
epsilon = 1e-08
weight_decay = 0.01
norm_eps = 1e-05
clip_limit = 1.0

@jax.custom_vjp
def low(v):
    return lax.optimization_barrier(v.astype(jnp.bfloat16)).astype(jnp.float32)

@jax.custom_vjp
def low_back(v):
    return v

def low_keep(v):
    return (low(v), None)

def low_pass(kept, grad):
    return (grad,)

def back_keep(v):
    return (v, None)

def back_low(kept, grad):
    return (low(grad),)
low.defvjp(low_keep, low_pass)
low_back.defvjp(back_keep, back_low)

def matmul(left, right):
    return jnp.dot(left, right, precision=highest, preferred_element_type=jnp.float32)

def layer_norm(values, gain_row, bias_row):
    centered = values - lax.optimization_barrier(jnp.mean(values, axis=-1, keepdims=True))
    spread = lax.optimization_barrier(jnp.mean(centered * centered, axis=-1, keepdims=True))
    return centered * lax.rsqrt(spread + norm_eps) * gain_row + bias_row

def piece_step(states, inputs):
    state_cos, state_sin, total_cos, total_sin = states
    query_cos, query_sin, key_cos, key_sin, values = inputs
    length = query_cos.shape[0]
    scores = jnp.einsum('ihe,jhe->hij', query_cos, key_cos, precision=highest)
    scores = scores + jnp.einsum('ihe,jhe->hij', query_sin, key_sin, precision=highest)
    causal = jnp.arange(length)[:, None] >= jnp.arange(length)[None, :]
    scores = low_back(jnp.where(causal[None], scores, 0.0))
    numerator = jnp.einsum('hij,jhe->ihe', low(scores), values, precision=highest)
    numerator = numerator + jnp.einsum('ihe,hef->ihf', query_cos, state_cos, precision=highest)
    numerator = numerator + jnp.einsum('ihe,hef->ihf', query_sin, state_sin, precision=highest)
    denominator = lax.optimization_barrier(jnp.sum(scores, axis=-1)).T
    denominator = denominator + jnp.einsum('ihe,he->ih', query_cos, total_cos, precision=highest)
    denominator = denominator + jnp.einsum('ihe,he->ih', query_sin, total_sin, precision=highest)
    attended = low_back(numerator) / denominator[:, :, None]
    state_cos = state_cos + jnp.einsum('jhe,jhf->hef', key_cos, values, precision=highest)
    state_sin = state_sin + jnp.einsum('jhe,jhf->hef', key_sin, values, precision=highest)
    total_cos = total_cos + lax.optimization_barrier(jnp.sum(key_cos, axis=0))
    total_sin = total_sin + lax.optimization_barrier(jnp.sum(key_sin, axis=0))
    return ((state_cos, state_sin, total_cos, total_sin), attended)

def sequence_layer(tokens, weights):
    attn_weight, up_weight, down_weight, norm_rows = weights
    length = tokens.shape[0]
    query_pre = low_back(matmul(tokens, attn_weight[:, 0, :]))
    key_pre = low_back(matmul(tokens, attn_weight[:, 1, :]))
    value_pre = low_back(matmul(tokens, attn_weight[:, 2, :]))
    phase_angle = math.pi / 2 * jnp.arange(length, dtype=jnp.float32) / length
    cosine_weight = jnp.cos(phase_angle)[:, None]
    sine_weight = jnp.sin(phase_angle)[:, None]
    query_feat = jax.nn.softplus(query_pre)
    key_feat = jax.nn.softplus(key_pre)
    query_cos = low(query_feat * cosine_weight)
    query_sin = low(query_feat * sine_weight)
    key_cos = low(key_feat * cosine_weight)
    key_sin = low(key_feat * sine_weight)
    values = low(value_pre)

    def by_piece(array):
        return array.reshape(N_SEQ, length // N_SEQ, HEADS, HEAD)
    start_states = (jnp.zeros((HEADS, HEAD, HEAD), jnp.float32), jnp.zeros((HEADS, HEAD, HEAD), jnp.float32), jnp.zeros((HEADS, HEAD), jnp.float32), jnp.zeros((HEADS, HEAD), jnp.float32))
    final_states, attended = lax.scan(jax.checkpoint(piece_step), start_states, (by_piece(query_cos), by_piece(query_sin), by_piece(key_cos), by_piece(key_sin), by_piece(values)))
    attended = attended.reshape(length, D)
    branch_one = low_back(matmul(low(attended), attn_weight[:, 3, :]))
    first_norm = layer_norm(tokens + branch_one, norm_rows[0], norm_rows[1])
    hidden = low_back(matmul(low(first_norm), up_weight))
    branch_two = low_back(matmul(low(jax.nn.gelu(hidden)), down_weight))
    return layer_norm(first_norm + branch_two, norm_rows[2], norm_rows[3])

def adamw(weight, gradient, first_moment, second, step_rate):
    first_new = beta_one * first_moment + (1.0 - beta_one) * gradient
    second_new = beta_two * second + (1.0 - beta_two) * gradient * gradient
    first_hat = first_new / (1.0 - beta_one ** STEP)
    second_hat = second_new / (1.0 - beta_two ** STEP)
    weight_new = weight - step_rate * (first_hat / (jnp.sqrt(second_hat) + epsilon) + weight_decay * weight)
    return (weight_new, first_new, second_new)

def reference(layer_input, cotangent, attn_master, up_master, down_master, norm_params, attn_first, up_first, down_first, norm_first, attn_second, up_second, down_second, norm_second):
    weights = (low(attn_master), low(up_master), low(down_master), norm_params)

    def one_sequence(totals, pair):
        tokens, backward = pair
        result, pullback = jax.vjp(sequence_layer, tokens.astype(jnp.float32), weights)
        grad_tokens, grad_weights = pullback(backward.astype(jnp.float32))
        totals = jax.tree.map(jnp.add, totals, grad_weights)
        return (totals, (result.astype(jnp.bfloat16), grad_tokens))
    zero_totals = jax.tree.map(jnp.zeros_like, weights)
    totals, outputs = lax.scan(one_sequence, zero_totals, (layer_input, cotangent))
    layer_output, input_grad = outputs
    square = jnp.float32(0.0)
    for gradient in totals:
        square = square + jnp.sum(gradient * gradient)
    grad_norm = jnp.sqrt(square)
    clip_scale = clip_limit / jnp.maximum(grad_norm, clip_limit)
    attn_grad = totals[0] * clip_scale
    up_grad = totals[1] * clip_scale
    down_grad = totals[2] * clip_scale
    norm_grad = totals[3] * clip_scale
    attn_rate = learn_rate * jnp.array([1.0, 1.0, 1.0, math.sqrt(SEQLEN // 8)], jnp.float32)[None, :, None]
    attn_new, attn_first_new, attn_second_new = adamw(attn_master, attn_grad, attn_first, attn_second, attn_rate)
    up_new, up_first_new, up_second_new = adamw(up_master, up_grad, up_first, up_second, learn_rate)
    down_new, down_first_new, down_second_new = adamw(down_master, down_grad, down_first, down_second, learn_rate * math.sqrt(D / FF))
    norm_new, norm_first_new, norm_second_new = adamw(norm_params, norm_grad, norm_first, norm_second, gain_rate)
    return (layer_output, input_grad, attn_grad, up_grad, down_grad, norm_grad, grad_norm, attn_new, up_new, down_new, norm_new, attn_first_new, up_first_new, down_first_new, norm_first_new, attn_second_new, up_second_new, down_second_new, norm_second_new)
```

```python
import functools
import math

import jax
import jax.numpy as jnp
import numpy as np
from jax import lax
from jax.experimental import pallas as pl
from jax.experimental.pallas import tpu as pltpu
from jax.sharding import PartitionSpec as P

D = 768
HEAD = 64
FF = 3072
STEP = 5


highest = lax.Precision.HIGHEST
beta_one = 0.5
beta_two = 0.5
learn_rate = 0.02
gain_rate = 0.2
epsilon = 1e-08
weight_decay = 0.01
norm_eps = 1e-05
clip_limit = 1.0


MESH = pl.DeviceIdType.MESH
f32, bf16 = jnp.float32, jnp.bfloat16
PIECE = 512
PAIR = 2 * HEAD
PLANES = 4
VMEM_BYTES = 63 * 1024 * 1024


def dot(left, right):
    return jnp.dot(left, right, preferred_element_type=f32)


def dot_nt(left, right):
    return lax.dot_general(left, right, (((1,), (1,)), ((), ())), preferred_element_type=f32)


def dot_tn(left, right):
    return lax.dot_general(left, right, (((0,), (0,)), ((), ())), preferred_element_type=f32)


def first_half(shape):
    return lax.broadcasted_iota(jnp.int32, shape, 1) < HEAD


def top_half(shape):
    return lax.broadcasted_iota(jnp.int32, shape, 0) < HEAD


def own_head(value, head):
    mask = first_half(value.shape)
    zero = jnp.zeros_like(value)
    return jnp.where(mask, value, zero) if head == 0 else jnp.where(mask, zero, value)


def two_heads(first, second):
    return jnp.where(first_half(first.shape), first, second)


def pair_mask(shape):
    return (lax.broadcasted_iota(jnp.int32, shape, 1) & (PAIR - 1)) < HEAD


def stack_heads(value):
    mask, zero = pair_mask(value.shape), jnp.zeros_like(value)
    return jnp.concatenate([jnp.where(mask, value, zero), jnp.where(mask, zero, value)], axis=0)


def join_heads(stacked):
    first, second = stacked[: stacked.shape[0] // 2], stacked[stacked.shape[0] // 2 :]
    return jnp.where(pair_mask(first.shape), first, second)


def side_by_side(wide):
    half = wide.shape[1] // 2
    return jnp.concatenate([wide[:, :half], wide[:, half:]], axis=0)


def fill_triangles(tri_s):
    half = tri_s.shape[1]
    row = lax.broadcasted_iota(jnp.int32, (half, half), 0)
    col = lax.broadcasted_iota(jnp.int32, (half, half), 1)
    tri_s[0:half] = (row >= col).astype(f32).astype(bf16)
    tri_s[half:] = (row <= col).astype(f32).astype(bf16)


def causal_product(own, other, right, tri_s):
    half = PIECE // 2
    tri = jnp.concatenate([tri_s[0:half], tri_s[0:half]], axis=0)
    tops, lows = stack_heads(own[0:half]), stack_heads(own[half:])
    first = dot_nt(jnp.concatenate([tops, lows], axis=0), other[0:half]).astype(bf16)
    near = dot_nt(lows, other[half:]).astype(bf16) * tri
    first = jnp.concatenate([first[:PIECE] * tri, first[PIECE:]], axis=0)
    out = dot(first, right[0:half])
    low = out[PIECE:] + dot(near, right[half:])
    return jnp.concatenate([join_heads(out[:PIECE]), join_heads(low)], axis=0)


def causal_transposed(own, other, right, tri_s):
    half = PIECE // 2
    tri = jnp.concatenate([tri_s[half:], tri_s[half:]], axis=1)
    top = dot_nt(other[0:half], stack_heads(own[0:half])).astype(bf16) * tri
    low = dot_nt(other, stack_heads(own[half:])).astype(bf16)
    low = jnp.concatenate([low[0:half], low[half:] * tri], axis=0)
    out = dot(side_by_side(low), right[half:])
    more = dot(side_by_side(top), right[0:half])
    first = jnp.concatenate([out[0:half] + more[0:half], out[half:PIECE]], axis=0)
    second = jnp.concatenate([out[PIECE : PIECE + half] + more[half:], out[PIECE + half :]], axis=0)
    return jnp.where(pair_mask(first.shape), first, second)


def with_ones(value):
    return jnp.concatenate([value, jnp.ones_like(value)], axis=1)


def turned(value, trig):
    wide = value.astype(f32)
    cos, sin = trig[:, :PAIR], trig[:, PAIR:]
    return jnp.concatenate([(wide * cos).astype(bf16), (wide * sin).astype(bf16)], axis=1)


def squeeze_state(state, totals):
    cos = two_heads(state[0:HEAD], state[HEAD : 2 * HEAD])
    sin = two_heads(state[2 * HEAD : 3 * HEAD], state[3 * HEAD :])
    row = lax.broadcasted_iota(jnp.int32, (16, PAIR), 0)
    sums = jnp.where(row == 0, totals[:, :PAIR], totals[:, PAIR:])
    return jnp.concatenate([cos, sin, sums], axis=0)


def spread_state(packed):
    cos, sin = packed[0:HEAD], packed[HEAD:PAIR]
    state = jnp.concatenate(
        [own_head(cos, 0), own_head(cos, 1), own_head(sin, 0), own_head(sin, 1)], axis=0
    )
    row = lax.broadcasted_iota(jnp.int32, (16, PAIR), 0)
    sums = packed[PAIR:]
    ones = jnp.ones((16, PAIR), bf16)
    blocks = []
    for kind in range(2):
        column = dot_tn(jnp.where(row == kind, sums, jnp.zeros_like(sums)), ones).astype(bf16)
        blocks += [own_head(column[0:HEAD], 0), own_head(column[HEAD:], 1)]
    return jnp.concatenate([state, jnp.concatenate(blocks, axis=0)], axis=1)


def normed(value):
    centered = value - jnp.mean(value, axis=-1, keepdims=True)
    rstd = lax.rsqrt(jnp.mean(centered * centered, axis=-1, keepdims=True) + norm_eps)
    return centered * rstd, rstd


def norm_back(grad, unit, rstd):
    mean = jnp.mean(grad, axis=-1, keepdims=True)
    along = jnp.mean(grad * unit, axis=-1, keepdims=True)
    return rstd * (grad - mean - unit * along)


class Place:
    def __init__(self):
        dp, seq = lax.axis_index("dp"), lax.axis_index("seq")
        self.z, self.y, self.x, self.c = dp // 2, dp % 2, seq // 2, seq % 2
        self.shard = dp

    def device(self, z=None, y=None, x=None, c=None):
        z = self.z if z is None else z
        y = self.y if y is None else y
        x = self.x if x is None else x
        c = self.c if c is None else c
        return {"dp": z * 2 + y, "seq": x * 2 + c}

    def plane(self, shift):
        return lax.rem(self.z + shift + PLANES, PLANES)

    def across_y(self):
        return self.device(y=1 - self.y)

    def across_x(self):
        return self.device(x=1 - self.x)

    def across_c(self):
        return self.device(c=1 - self.c)

    def neighbours(self):
        planes = [self.device(z=self.plane(step)) for step in range(1, PLANES)]
        return planes + [self.across_y(), self.across_x(), self.across_c()]

    def corners(self):
        y, x, c = 1 - self.y, 1 - self.x, 1 - self.c
        return [
            self.device(x=x, c=c), self.device(y=y, c=c),
            self.device(y=y, x=x), self.device(y=y, x=x, c=c),
        ]

    def in_plane(self):
        return (self.y * 2 + self.x) * 2 + self.c


def greet(place, corners=False):
    barrier = pltpu.get_barrier_semaphore()
    peers = place.neighbours() + (place.corners() if corners else [])
    for peer in peers:
        pl.semaphore_signal(barrier, inc=1, device_id=peer, device_id_type=MESH)
    pl.semaphore_wait(barrier, len(peers))


class Engine:
    RATES = {"x": 30e3, "y": 30e3, "z": 23e3, "c": 200e3}

    def __init__(self, pace=1.0):
        self.now, self.free, self.pace = 0.0, dict.fromkeys(self.RATES, 0.0), pace
        self.eta, self.tasks, self.done = {}, [], set()

    def sent(self, key, link, size):
        self.now += 0.04
        start = max(self.now, self.free[link])
        self.free[link] = start + size / (self.pace * self.RATES[link])
        self.eta[key] = self.free[link] + 1.5

    def add(self, needs, act, mark=None, cost=0.05):
        self.tasks.append((needs, act, mark, cost))

    def due(self, task):
        return max((self.eta.get(key, math.inf) for key in task[0]), default=0.0)

    def run(self, task):
        self.tasks.remove(task)
        self.now = max(self.now, self.due(task)) + task[3]
        task[1]()
        if task[2] is not None:
            self.done.add(task[2])

    def tick(self, cost):
        self.now += cost
        while self.tasks:
            task = min(self.tasks, key=self.due)
            if self.due(task) > self.now:
                return
            self.run(task)

    def until(self, *marks):
        while not self.done.issuperset(marks):
            self.run(min(self.tasks, key=self.due))

    def rest(self):
        while self.tasks:
            self.run(min(self.tasks, key=self.due))


class Gather:
    def __init__(self, place, engine, chunks, send, recv, ready):
        self.place, self.engine, self.chunks = place, engine, chunks
        self.send, self.recv, self.sent, self.ready = send, recv, [], ready
        for k in range(len(chunks)):
            self.plan(k)

    def piece(self, k, z, y, x, c):
        ref, stride, base, height, column, width = self.chunks[k]
        row = (z * 2 + y) * stride + base + c * height
        return ref.at[
            pl.ds(pl.multiple_of(row, 16), height),
            pl.ds(pl.multiple_of(column + x * width, 128), width),
        ]

    def copy(self, k, index, ref, device):
        return pltpu.make_async_remote_copy(
            src_ref=ref,
            dst_ref=ref,
            send_sem=self.send.at[k, index],
            recv_sem=self.recv.at[k, index],
            device_id=device,
            device_id_type=MESH,
        )

    def push(self, k, index, ref, device, link):
        copy = self.copy(k, index, ref, device)
        copy.start()
        self.sent.append(copy)
        self.engine.sent((k, index), link, 2 * self.chunks[k][3] * self.chunks[k][5])

    def pull(self, k, index, ref):
        self.copy(k, index, ref, self.place.across_c()).wait_recv()

    def twin(self, k, index, ref):
        self.push(k, 14 + index, ref, self.place.across_c(), "c")

    def begin(self, k):
        p = self.place
        self.ready(k)
        own = self.piece(k, p.z, p.y, p.x, p.c)
        for step in (1, 3, 2):
            self.push(k, step - 1, own, p.device(z=p.plane(step)), "z")
        self.push(k, 3, own, p.across_y(), "y")
        other = self.piece(k, p.z, p.y, 1 - p.x, p.c)
        self.push(k, 10, other, p.across_y(), "y")
        self.push(k, 7, other, p.device(z=p.plane(1)), "z")

    def from_plane(self, k, step):
        p = self.place
        ref = self.piece(k, p.plane(-step), p.y, p.x, p.c)
        self.pull(k, step - 1, ref)
        self.push(k, 3 + step, ref, p.across_y(), "y")
        if step != 1:
            self.push(k, 6 + step, ref, p.across_x(), "x")
        self.twin(k, step - 1, ref)

    def by_y(self, k):
        return (1, 3) if k == 6 else ()

    def from_y(self, k, step):
        p = self.place
        ref = self.piece(k, p.plane(-step), 1 - p.y, p.x, p.c)
        self.pull(k, 3 + step, ref)
        if step and step not in self.by_y(k):
            self.push(k, 10 + step, ref, p.across_x(), "x")
        self.twin(k, 3 + step, ref)

    def from_x(self, k, step):
        p = self.place
        ref = self.piece(k, p.plane(-step), p.y, 1 - p.x, p.c)
        self.pull(k, 6 + step, ref)
        if step in self.by_y(k):
            self.push(k, 10 + step, ref, p.across_y(), "y")
        self.twin(k, 6 + step, ref)

    def corner(self, k, step):
        p = self.place
        ref = self.piece(k, p.plane(-step), 1 - p.y, 1 - p.x, p.c)
        self.pull(k, 10 + step, ref)
        self.twin(k, 10 + step, ref)

    def finish(self, k):
        p = self.place
        far = 1 - p.c
        for step in range(PLANES):
            z = p.plane(-step)
            if step:
                self.pull(k, 14 + step - 1, self.piece(k, z, p.y, p.x, far))
                self.pull(k, 20 + step, self.piece(k, z, p.y, 1 - p.x, far))
            self.pull(k, 17 + step, self.piece(k, z, 1 - p.y, p.x, far))
            self.pull(k, 24 + step, self.piece(k, z, 1 - p.y, 1 - p.x, far))

    def plan(self, k):
        before = [(k - 2, at) for at in range(3)] if k > 1 else []
        add = self.engine.add
        add(before, functools.partial(self.begin, k))
        for step in (1, 3, 2):
            add([(k, step - 1)], functools.partial(self.from_plane, k, step))
            add([(k, 6 + step)], functools.partial(self.from_x, k, step))
        for step in (0, 1, 3, 2):
            add([(k, 3 + step)], functools.partial(self.from_y, k, step))
            add([(k, 10 + step)], functools.partial(self.corner, k, step))
        add([(k, 14 + at) for at in range(14)], functools.partial(self.finish, k), k, 0.3)

    def drain(self):
        for copy in self.sent:
            copy.wait_send()


def ds(start, size, unit):
    return pl.ds(pl.multiple_of(start, unit), size)


def turn_over(source, target):
    for at in range(0, source.shape[0], 256):
        target[:, at : at + 256] = source[at : at + 256, :].T


def block_of(b):
    return ds((b // 6) * PIECE, PIECE, PIECE), ds(lax.rem(b, 6) * PAIR, PAIR, PAIR)


def forward_kernel(
    x_h, attn_h, up_h, down_h, norm_h, trig_h,
    wqkv_o, wo_o, wup_o, wdn_o, q_o, k_o, v_o, att_o, rden_o, xhat_o, rstd_o, xt_o, att_t_o,
    low_t_o, act_o, slope_o, state_o,
    wqkv, wo, wup, wdn, attn_st, up_st, down_st, x_s, norm_s, trig_s, tri_s,
    q_s, k_s, v_s, num_s, den_s, att_s, xhat_s, rstd_s, low_s, act_s, slope_a, slope_b, hid_a, hid_b,
    x_t_s, att_t_s, low_t_s, st_own, st_twin, st_chip, st_prior,
    load_sem, store_sem, tile_sem, g_send, g_recv, st_send, st_recv,
):
    place = Place()
    shard, x, c = place.shard, place.x, place.c
    groups = x_s.shape[0] // PIECE
    blocks = groups * 6
    loads = []
    for at, (src, dst) in enumerate(
        [
            (attn_h, attn_st), (up_h, up_st), (down_h, down_st), (x_h, x_s), (norm_h, norm_s),
            (trig_h.at[ds((x * 2 + c) * PIECE, PIECE, PIECE), :], trig_s),
        ]
    ):
        copy = pltpu.make_async_copy(src, dst, load_sem.at[at])
        copy.start()
        loads.append(copy)
    stores = []

    def store(src, dst):
        copy = pltpu.make_async_copy(src, dst, store_sem.at[len(stores)])
        copy.start()
        stores.append(copy)

    thin, thick = attn_st.shape[0], down_st.shape[0]
    chunks = [
        (wqkv, thin, 0, thin // 2, D, D),
        (wqkv, thin, 0, thin // 2, 0, D // 2),
        (wo, thin, 0, thin // 2, 0, D // 2),
        (wup, thin, 0, thin // 2, 0, FF // 4),
        (wup, thin, 0, thin // 2, FF // 2, FF // 4),
        (wdn, thick, 0, thick // 4, 0, D // 2),
        (wdn, thick, thick // 2, thick // 4, 0, D // 2),
    ]
    def ready(k):
        narrow = ds(shard * thin, thin, 32)
        if k == 0:
            loads[0].wait()
            for j in range(3):
                wqkv[narrow, j * D : (j + 1) * D] = attn_st[:, j, :].astype(bf16)
        elif k == 2:
            wo[narrow, :] = attn_st[:, 3, :].astype(bf16)
        elif k == 3:
            loads[1].wait()
            wup[narrow, :] = up_st[...].astype(bf16)
        elif k == 5:
            loads[2].wait()
            wdn[ds(shard * thick, thick, 128), :] = down_st[...].astype(bf16)

    engine = Engine()
    gather = Gather(place, engine, chunks, g_send, g_recv, ready)
    greet(place)
    engine.tick(0.0)
    fill_triangles(tri_s)
    for copy in loads[3:]:
        copy.wait()
    turn_over(x_s, x_t_s)
    store(x_t_s, xt_o)
    engine.tick(3.0)
    engine.until(0)

    hidden = (hid_a, hid_b)

    def chain(products, finish, cost):
        hidden[0][...] = products[0]()
        for t in range(len(products)):
            if t + 1 < len(products):
                hidden[(t + 1) % 2][...] = products[t + 1]()
            finish(t, hidden[t % 2])
            engine.tick(cost)

    def project(parts):
        tiles = [(target, column, t, soft) for target, column, soft in parts for t in range(3)]

        def product(target, column, t, soft):
            return dot(x_s[...], wqkv[:, column + 256 * t : column + 256 * t + 256])

        def finish(at, pre):
            target, _, t, soft = tiles[at]
            pre = pre[...]
            if soft:
                pre = jnp.maximum(pre, 0.0) + jnp.log1p(jnp.exp(-jnp.abs(pre)))
            target[:, 256 * t : 256 * t + 256] = pre.astype(bf16)

        chain([functools.partial(product, *tile) for tile in tiles], finish, 0.7)

    project([(k_s, D, True), (v_s, 2 * D, False)])

    def local(b, carry):
        rows, cols = ds((b // 6) * PIECE, PIECE, PIECE), ds(lax.rem(b, 6) * PAIR, PAIR, PAIR)
        keys = turned(k_s[rows, cols], trig_s[...])
        state = dot_tn(keys, v_s[rows, cols])
        totals = dot(jnp.ones((16, PIECE), bf16), keys)
        st_own[b] = squeeze_state(state, totals).astype(bf16)
        return carry

    for part in range(0, blocks, 4):
        lax.fori_loop(part, part + 4, local, 0)
        engine.tick(1.4)
    state = StateSum(place, engine, st_send, st_recv, st_own, st_twin, st_chip, st_prior, False)
    engine.tick(0.0)
    engine.until(1)
    project([(q_s, 0, True)])
    store(wqkv, wqkv_o)
    store(q_s, q_o)
    store(k_s, k_o)
    store(v_s, v_o)

    def intra(i, carry):
        spots = [block_of(2 * i), block_of(2 * i + 1)]
        taken = [(q_s[at], k_s[at], v_s[at]) for at in spots]
        outs = [
            causal_product(
                turned(q, trig_s[...]), turned(k, trig_s[...]), with_ones(v), tri_s
            )
            for q, k, v in taken
        ]
        for at, out in zip(spots, outs):
            num_s[at] = out[:, :PAIR]
            den_s[at] = out[:, PAIR:]
        return carry

    for part in range(blocks // 2):
        lax.fori_loop(part, part + 1, intra, 0)
        engine.tick(1.6)
    engine.until("state")

    def inter(i, carry):
        spots = [block_of(2 * i), block_of(2 * i + 1)]
        states = [state.total(2 * i + at).astype(bf16) for at in range(2)]
        taken = [(q_s[at], num_s[at], den_s[at]) for at in spots]
        outs = []
        for (q, num, den), packed in zip(taken, states):
            more = dot(turned(q, trig_s[...]), spread_state(packed))
            recip = 1.0 / (den + more[:, PAIR:])
            outs.append((((num + more[:, :PAIR]) * recip).astype(bf16), recip))
        for at, (attended, recip) in zip(spots, outs):
            att_s[at] = attended
            den_s[at] = recip
        for at, packed in enumerate(states):
            st_chip[2 * i + at] = packed
        return carry

    for part in range(0, blocks // 2, 2):
        lax.fori_loop(part, part + 2, inter, 0)
        engine.tick(1.6)
    store(att_s, att_o)
    store(den_s, rden_o)
    turn_over(att_s, att_t_s)
    store(att_t_s, att_t_o)
    store(st_chip, state_o)
    engine.tick(1.0)
    engine.until(2)
    store(wo, wo_o)

    gain_one, bias_one = norm_s[0:1, :], norm_s[1:2, :]
    tile = 256

    def join(t, carry):
        cols = ds(t * tile, tile, tile)
        xhat_s[:, cols] = x_s[:, cols].astype(f32) + dot(att_s[...], wo[:, cols])
        return carry

    def join_norm(t, carry):
        rows = ds(t * tile, tile, tile)
        unit, rstd = normed(xhat_s[rows, :])
        xhat_s[rows, :] = unit
        rstd_s[rows, :] = jnp.broadcast_to(rstd, (tile, 128))
        low_s[rows, :] = (unit * gain_one + bias_one).astype(bf16)
        return carry

    for t in range(D // tile):
        lax.fori_loop(t, t + 1, join, 0)
        engine.tick(0.7)
    for part in range(x_s.shape[0] // tile):
        lax.fori_loop(part, part + 1, join_norm, 0)
        engine.tick(0.4)
    store(xhat_s, xhat_o)
    store(rstd_s, rstd_o)
    turn_over(low_s, low_t_s)
    store(low_t_s, low_t_o)
    engine.tick(1.0)
    engine.until(3)

    slopes, scale = (slope_a, slope_b), math.sqrt(2.0 / math.pi)

    def slope_copy(t):
        return pltpu.make_async_copy(
            slopes[t % 2], slope_o.at[:, 256 * t : 256 * t + 256], tile_sem.at[t % 2]
        )

    def expand(t, value):
        if t >= 2:
            slope_copy(t - 2).wait()
        value = value[...]
        squared = value * value
        curve = jnp.tanh(value * (scale + (scale * 0.044715) * squared))
        half = 0.5 + 0.5 * curve
        active = value * half
        slope = half + active * (1.0 - curve) * (scale + (3.0 * scale * 0.044715) * squared)
        act_s[:, 256 * t : 256 * t + 256] = active.astype(bf16)
        slopes[t % 2][...] = slope.astype(bf16)
        slope_copy(t).start()

    def raised(t):
        if t == 6:
            engine.until(4)
            store(wup, wup_o)
        return dot(low_s[...], wup[:, 256 * t : 256 * t + 256])

    chain([functools.partial(raised, t) for t in range(FF // 256)], expand, 1.1)
    store(act_s, act_o)
    engine.until(5, 6)
    store(wdn, wdn_o)
    for copy in stores + [slope_copy(10), slope_copy(11)]:
        copy.wait()
    gather.drain()
    state.drain()


def forward_call(tokens, attn_master, up_master, down_master, norm_params, seq_count):
    rows = tokens.shape[0]
    blocks = rows // PIECE * 6
    thin, thick = attn_master.shape[0], down_master.shape[0]
    trig = turning_table(seq_count)
    shapes = dict(
        wqkv=((D, 3 * D), bf16), wo=((D, D), bf16), wup=((D, FF), bf16), wdn=((FF, D), bf16),
        q=((rows, D), bf16), k=((rows, D), bf16), v=((rows, D), bf16), att=((rows, D), bf16),
        rden=((rows, D), f32), xhat=((rows, D), f32), rstd=((rows, 128), f32),
        x_t=((D, rows), bf16), att_t=((D, rows), bf16), low_t=((D, rows), bf16),
        act=((rows, FF), bf16), slope=((rows, FF), bf16), state=((blocks, 144, PAIR), bf16),
    )
    out_shape = [jax.ShapeDtypeStruct(s, d) for s, d in shapes.values()]
    hbm = pl.BlockSpec(memory_space=pl.ANY)
    scratch = [
        pltpu.VMEM((D, 3 * D), bf16), pltpu.VMEM((D, D), bf16),
        pltpu.VMEM((D, FF), bf16), pltpu.VMEM((FF, D), bf16),
        pltpu.VMEM((thin, 4, D), f32), pltpu.VMEM((thin, FF), f32), pltpu.VMEM((thick, D), f32),
        pltpu.VMEM((rows, D), bf16), pltpu.VMEM((4, D), f32),
        pltpu.VMEM((PIECE, 2 * PAIR), f32), pltpu.VMEM((PIECE, PIECE // 2), bf16),
        pltpu.VMEM((rows, D), bf16), pltpu.VMEM((rows, D), bf16), pltpu.VMEM((rows, D), bf16),
        pltpu.VMEM((rows, D), f32), pltpu.VMEM((rows, D), f32), pltpu.VMEM((rows, D), bf16),
        pltpu.VMEM((rows, D), f32), pltpu.VMEM((rows, 128), f32), pltpu.VMEM((rows, D), bf16),
        pltpu.VMEM((rows, FF), bf16), pltpu.VMEM((rows, 256), bf16),
        pltpu.VMEM((rows, 256), bf16), pltpu.VMEM((rows, 256), f32),
        pltpu.VMEM((rows, 256), f32),
        pltpu.VMEM((D, rows), bf16), pltpu.VMEM((D, rows), bf16), pltpu.VMEM((D, rows), bf16),
        pltpu.VMEM((blocks, 144, PAIR), bf16), pltpu.VMEM((blocks, 144, PAIR), bf16),
        pltpu.VMEM((blocks, 144, PAIR), bf16), pltpu.VMEM((blocks, 144, PAIR), bf16),
        pltpu.SemaphoreType.DMA((8,)), pltpu.SemaphoreType.DMA((21,)),
        pltpu.SemaphoreType.DMA((2,)),
        pltpu.SemaphoreType.DMA((7, 28)), pltpu.SemaphoreType.DMA((7, 28)),
        pltpu.SemaphoreType.DMA((3,)), pltpu.SemaphoreType.DMA((3,)),
    ]
    return dict(
        zip(
            shapes,
            pl.pallas_call(
                forward_kernel,
                out_shape=out_shape,
                in_specs=[hbm] * 6,
                out_specs=[hbm] * len(out_shape),
                scratch_shapes=scratch,
                compiler_params=pltpu.CompilerParams(
                    collective_id=0, has_side_effects=True, vmem_limit_bytes=VMEM_BYTES
                ),
                name="gather_forward",
            )(
                tokens, attn_master, up_master, down_master, norm_params,
                trig,
            ),
        )
    )


def second_norm_kernel(
    act, wdn, xhat, cot, norm, out_o, gb_o, gb_t_o, gr2_o, sums_o, sum_s
):
    rows = act.shape[0]
    for column in range(0, D, 256):
        cols = slice(column, column + 256)
        sum_s[:, cols] = dot(act[...], wdn[:, cols])

    @pl.when(pl.program_id(0) == 0)
    def _():
        sums_o[...] = jnp.zeros_like(sums_o)

    def body(t, carry):
        span = ds(t * 256, 256, 256)
        first = xhat[span, :] * norm[0:1, :] + norm[1:2, :]
        unit, rstd = normed(first + sum_s[span, :])
        out_o[span, :] = (unit * norm[2:3, :] + norm[3:4, :]).astype(bf16)
        grad = cot[span, :].astype(f32)
        sums_o[0:1, :] += jnp.sum(grad * unit, axis=0, keepdims=True)
        sums_o[1:2, :] += jnp.sum(grad, axis=0, keepdims=True)
        grad = norm_back(grad * norm[2:3, :], unit, rstd)
        gr2_o[span, :] = grad
        low = grad.astype(bf16)
        gb_o[span, :] = low
        gb_t_o[:, span] = low.T
        return carry

    lax.fori_loop(0, rows // 256, body, 0)


def second_norm(s, cotangent, norm_params):
    rows = cotangent.shape[0]
    tile = rows // 2
    by_rows = lambda width: pl.BlockSpec((tile, width), lambda t: (t, 0))
    whole = lambda height, width: pl.BlockSpec((height, width), lambda t: (0, 0))
    outs = pl.pallas_call(
        second_norm_kernel,
        grid=(rows // tile,),
        in_specs=[by_rows(FF), whole(FF, D), by_rows(D), by_rows(D), whole(4, D)],
        out_specs=[
            by_rows(D), by_rows(D), pl.BlockSpec((D, tile), lambda t: (0, t)), by_rows(D),
            whole(8, D),
        ],
        out_shape=[
            jax.ShapeDtypeStruct((rows, D), bf16), jax.ShapeDtypeStruct((rows, D), bf16),
            jax.ShapeDtypeStruct((D, rows), bf16), jax.ShapeDtypeStruct((rows, D), f32),
            jax.ShapeDtypeStruct((8, D), f32),
        ],
        scratch_shapes=[pltpu.VMEM((tile, D), f32)],
        compiler_params=pltpu.CompilerParams(vmem_limit_bytes=VMEM_BYTES),
        name="second_norm",
    )(s["act"], s["wdn"], s["xhat"], cotangent, norm_params)
    return dict(zip(("out", "gb", "gb_t", "gr2", "sums"), outs))


def input_kernel(gp, w, part, out):
    for column in range(0, D, 256):
        cols = slice(column, column + 256)
        out[:, cols] = part[:, cols] + dot_nt(gp[...], w[cols, :])


def input_call(gp, w, part):
    rows = part.shape[0]
    tile = rows // 2
    by_rows = lambda width: pl.BlockSpec((tile, width), lambda t: (t, 0))
    return pl.pallas_call(
        input_kernel,
        grid=(rows // tile,),
        in_specs=[by_rows(3 * D), pl.BlockSpec((D, 3 * D), lambda t: (0, 0)), by_rows(D)],
        out_specs=by_rows(D),
        out_shape=jax.ShapeDtypeStruct((rows, D), f32),
        compiler_params=pltpu.CompilerParams(vmem_limit_bytes=VMEM_BYTES),
        name="input_gradient",
    )(gp, w, part)


def turning_table(seq_count):
    length = seq_count * PIECE
    angle = math.pi / 2 * np.arange(length, dtype=np.float64) / length
    trig = np.repeat(np.stack([np.cos(angle), np.sin(angle)], axis=1), PAIR, axis=1)
    return jnp.asarray(trig, f32)


class Share:
    def __init__(self, grad, first, units, column, width, by_units, early, bufs, out):
        self.grad, self.first, self.units = grad, first, units
        self.column, self.width, self.by_units, self.early = column, width, by_units, early
        self.count = units // 2 if by_units else units
        self.half = width if by_units else width // 2
        self.twin, self.from_x, self.from_y, self.via_x, self.via_y, self.planes, self.final = bufs
        self.out = out

    def side(self, x):
        if self.by_units:
            return x * self.count, slice(0, self.width)
        return 0, ds(x * self.half, self.half, 128)

    def part(self, x):
        first, lanes = self.side(x)
        return pl.ds(first, self.count), lanes


def add_into(target, at, other, there, more=None, where=None):
    total = target[at].astype(f32) + other[there].astype(f32)
    if more is not None:
        total = total + more[where].astype(f32)
    target[at] = total.astype(bf16)


class Reduce:
    def __init__(self, place, engine, send, recv, store_sem, squares):
        self.place, self.engine, self.send, self.recv = place, engine, send, recv
        self.store_sem, self.squares = store_sem, squares
        self.sent, self.stored, self.count = [], [], 0

    def copy(self, k, index, src, dst, device):
        return pltpu.make_async_remote_copy(
            src_ref=src, dst_ref=dst, send_sem=self.send.at[k, index],
            recv_sem=self.recv.at[k, index], device_id=device, device_id_type=MESH,
        )

    def push(self, k, index, src, dst, device, link):
        copy = self.copy(k, index, src, dst, device)
        copy.start()
        self.sent.append((k, index, copy))
        self.engine.sent(("part", k, index), link, 2 * math.prod(dst.shape))

    def settle(self, parts):
        for k, index, copy in list(self.sent):
            if k in parts and index == 0:
                copy.wait_send()
                self.sent.remove((k, index, copy))

    def pull(self, k, index, dst):
        self.copy(k, index, dst, dst, self.place.across_c()).wait_recv()

    def launch(self, share):
        k = self.count
        self.count += 1
        src = share.grad.at[
            share.first : share.first + share.units, :, :, 1 - self.place.c, :,
            share.column : share.column + share.width,
        ]
        self.push(k, 0, src, share.twin, self.place.across_c(), "c")
        for needs, act, mark, cost in [
            ((0,), self.fold_core, "core", 0.8),
            ((1, 2), self.fold_corner, None, 0.3),
            ((3, 4, 5, 6), self.fold_square, None, 0.4),
            ((7, 8, 9), self.fold_planes, "sum", 0.3),
            ((10,), self.share_x, None, 0.05),
            ((11,), self.share_c, "whole", 0.05),
        ]:
            keys = [("part", k, at) for at in needs]
            self.engine.add(keys, functools.partial(act, k, share), (mark, k), cost)

    def fold_core(self, k, s):
        p = self.place
        self.pull(k, 0, s.twin)

        def body(i, carry):
            u, z = i // PLANES, lax.rem(i, PLANES)
            for y in range(2):
                own = s.grad[s.first + u, z, y, p.c, :, s.column : s.column + s.width]
                total = s.twin[u, z, y].astype(f32) + own.astype(f32)
                s.twin[u, z, y] = total.astype(bf16)
            return carry

        lax.fori_loop(0, PLANES * s.units, body, 0)
        e, oy, t = s.early, 1 - p.y, s.twin
        (mine, near), (theirs, far) = s.part(p.x), s.part(1 - p.x)
        self.push(k, 1, t.at[theirs, 0:e, oy, :, far], s.via_x, p.across_x(), "x")
        self.push(k, 2, t.at[theirs, e:PLANES, oy, :, far], s.via_y, p.across_y(), "y")
        self.push(
            k, 3, t.at[theirs, 0:e, p.y, :, far], s.from_x.at[:, 0:e], p.across_x(), "x"
        )
        self.push(
            k, 4, t.at[mine, e:PLANES, oy, :, near], s.from_y.at[:, e:PLANES], p.across_y(), "y"
        )

    def fold_corner(self, k, s):
        p, e, t, oy = self.place, s.early, s.twin, 1 - self.place.y
        (mine, near), (theirs, far) = s.part(p.x), s.part(1 - p.x)
        self.pull(k, 1, s.via_x)

        def from_x(u, carry):
            for z in range(e):
                add_into(t, (s.side(p.x)[0] + u, z, oy, slice(None), near), s.via_x, (u, z))
            return carry

        lax.fori_loop(0, s.count, from_x, 0)
        self.push(k, 5, t.at[mine, 0:e, oy, :, near], s.from_y.at[:, 0:e], p.across_y(), "y")
        self.pull(k, 2, s.via_y)

        def from_y(u, carry):
            for z in range(e, PLANES):
                at = (s.side(1 - p.x)[0] + u, z, p.y, slice(None), far)
                add_into(t, at, s.via_y, (u, z - e))
            return carry

        lax.fori_loop(0, s.count, from_y, 0)
        self.push(
            k, 6, t.at[theirs, e:PLANES, p.y, :, far], s.from_x.at[:, e:PLANES], p.across_x(), "x"
        )

    def fold_square(self, k, s):
        p, e, t = self.place, s.early, s.twin
        mine, near = s.part(p.x)
        self.pull(k, 3, s.from_x.at[:, 0:e])
        self.pull(k, 4, s.from_y.at[:, e:PLANES])
        self.pull(k, 5, s.from_y.at[:, 0:e])
        self.pull(k, 6, s.from_x.at[:, e:PLANES])

        def body(i, carry):
            u, z = i // PLANES, lax.rem(i, PLANES)
            at = (s.side(p.x)[0] + u, z, p.y, slice(None), near)
            add_into(t, at, s.from_x, (u, z), s.from_y, (u, z))
            return carry

        lax.fori_loop(0, PLANES * s.count, body, 0)
        for step in (1, 3, 2):
            z = p.plane(step)
            self.push(
                k, 6 + step, t.at[mine, z, p.y, :, near], s.planes.at[:, step - 1],
                p.device(z=z), "z",
            )

    def fold_planes(self, k, s):
        p = self.place
        mine, near = s.part(p.x)
        for step in (1, 3, 2):
            self.pull(k, 6 + step, s.planes.at[:, step - 1])

        def body(u, carry):
            at = s.side(p.x)[0] + u
            total = s.twin[at, p.z, p.y, :, near].astype(f32)
            for step in range(3):
                total = total + s.planes[u, step].astype(f32)
            total = total.astype(bf16)
            s.final[at, p.c, :, near] = total
            wide = total.astype(f32)
            for lane in range(0, s.half, 128):
                part = wide[:, lane : lane + 128]
                self.squares[...] += jnp.sum((part * part).reshape(-1, 8, 128), axis=0)
            return carry

        lax.fori_loop(0, s.count, body, 0)
        piece = s.final.at[mine, p.c, :, near]
        self.push(k, 10, piece, piece, p.across_x(), "x")

    def share_x(self, k, s):
        p = self.place
        theirs, far = s.part(1 - p.x)
        self.pull(k, 10, s.final.at[theirs, p.c, :, far])
        half = s.final.at[:, p.c]
        self.push(k, 11, half, half, p.across_c(), "c")

    def share_c(self, k, s):
        self.pull(k, 11, s.final.at[:, 1 - self.place.c])
        copy = pltpu.make_async_copy(s.final, s.out, self.store_sem.at[k])
        copy.start()
        self.stored.append(copy)

    def drain(self):
        for _, _, copy in self.sent:
            copy.wait_send()
        for copy in self.stored:
            copy.wait()


class Total:
    def __init__(self, place, engine, name, value, near, planes, send, recv):
        self.place, self.engine, self.name = place, engine, name
        self.value, self.near, self.planes = value, near, planes
        self.send, self.recv, self.sent = send, recv, []
        y, x, c = 1 - place.y, 1 - place.x, 1 - place.c
        peers = [place.across_c(), place.across_x(), place.across_y()] + place.corners()
        flips = [(0, 0, 1), (0, 1, 0), (1, 0, 0), (0, 1, 1), (1, 0, 1), (1, 1, 0), (1, 1, 1)]
        self.slots = [
            ((y if flip[0] else place.y) * 2 + (x if flip[1] else place.x)) * 2
            + (c if flip[2] else place.c)
            for flip in flips
        ]
        own = near.at[place.in_plane()]
        near[place.in_plane()] = value[...]
        for at, peer in enumerate(peers):
            self.push(at, own, peer, "cxyxyxy"[at])
        engine.add([(name, at) for at in range(7)], self.across)

    def copy(self, index, ref, device):
        return pltpu.make_async_remote_copy(
            src_ref=ref, dst_ref=ref, send_sem=self.send.at[index],
            recv_sem=self.recv.at[index], device_id=device, device_id_type=MESH,
        )

    def push(self, index, ref, device, link):
        copy = self.copy(index, ref, device)
        copy.start()
        self.sent.append(copy)
        self.engine.sent((self.name, index), link, 4 * math.prod(ref.shape))

    def across(self):
        p = self.place
        for at, slot in enumerate(self.slots):
            self.copy(at, self.near.at[slot], p.across_c()).wait_recv()
        total = self.near[0]
        for at in range(1, 8):
            total = total + self.near[at]
        self.planes[p.z] = total
        for step in (1, 3, 2):
            self.push(6 + step, self.planes.at[p.z], p.device(z=p.plane(step)), "z")
        self.engine.add([(self.name, at) for at in (7, 8, 9)], self.end, self.name)

    def end(self):
        for step in (1, 3, 2):
            own = self.planes.at[self.place.plane(-step)]
            self.copy(6 + step, own, self.place.across_c()).wait_recv()
        self.value[...] = (self.planes[0] + self.planes[1]) + (self.planes[2] + self.planes[3])

    def drain(self):
        for copy in self.sent:
            copy.wait_send()


class StateSum:
    def __init__(self, place, engine, send, recv, own, twin, chip, prior, late):
        self.x, self.c, self.engine = place.x, place.c, engine
        self.own, self.twin, self.chip, self.prior = own, twin, chip, prior
        self.giver, self.taker = (1, 0) if late else (0, 1)
        half = own.shape[0] // 2
        self.size = math.prod(own.shape)
        mine, other = ds(place.c * half, half, 1), ds((1 - place.c) * half, half, 1)

        def copy(index, src, dst, device):
            return pltpu.make_async_remote_copy(
                src_ref=src, dst_ref=dst, send_sem=send.at[index], recv_sem=recv.at[index],
                device_id=device, device_id_type=MESH,
            )

        self.swap = copy(0, own, twin, place.across_c())
        self.over = copy(1, chip.at[mine], prior.at[mine], place.across_x())
        self.pass_on = copy(2, prior.at[mine], prior.at[mine], place.across_c())
        self.taken = copy(2, prior.at[other], prior.at[other], place.across_c())
        self.swap.start()
        engine.sent("swap", "c", 2 * self.size)
        engine.add(["swap"], self.join, None, 0.5)
        engine.add(["over"], self.forward)
        engine.add(["pass"], self.end, "state")

    def join(self):
        self.swap.wait_recv()
        self.chip[...] = (self.own[...].astype(f32) + self.twin[...].astype(f32)).astype(bf16)

        @pl.when(self.x == self.giver)
        def _():
            self.over.start()

        self.engine.sent("over", "x", self.size)

    def forward(self):
        @pl.when(self.x == self.taker)
        def _():
            self.over.wait_recv()
            self.pass_on.start()

        self.engine.sent("pass", "c", self.size)

    def end(self):
        @pl.when(self.x == self.taker)
        def _():
            self.taken.wait_recv()

        @pl.when(self.x == self.giver)
        def _():
            self.over.wait_send()

    def drain(self):
        self.swap.wait_send()

        @pl.when(self.x == self.taker)
        def _():
            self.pass_on.wait_send()

    def total(self, b):
        far = jnp.where(self.x == self.taker, self.prior[b].astype(f32), 0.0)
        return far + jnp.where(self.c == self.taker, self.twin[b].astype(f32), 0.0)


def lane_in_head(shape):
    return lax.broadcasted_iota(jnp.int32, shape, 1) & (HEAD - 1)


def backward_kernel(
    wo_h, wup_h, q_h, k_h, v_h, att_h, rden_h, xhat_h, rstd_h, x_t_h, att_t_h,
    low_t_h, act_h, slope_h, gb_h, gb_t_h, gr2_h, state_h, sums_h, wdn_h, norm_h, trig_h,
    gp_o, one_o, attn_o, up_o, down_o, norm_o, square_o,
    wup, acts, slope, gr2, gb, left, wide, rstd, ga_s, gd_s, gu_s,
    norm_s, trig_s, tri_s, state_s, st_own, st_twin, st_chip, st_prior,
    norm_v, norm_w, norm_z, sq_v, sq_w, sq_z,
    *rest,
):
    bufs = rest[: 7 * SHARES]
    load_sem, store_sem, r_send, r_recv, s_send, s_recv = rest[7 * SHARES : 7 * SHARES + 6]
    t_send, t_recv, u_send, u_recv = rest[7 * SHARES + 6 :]
    place = Place()
    rows_all = gr2.shape[0]
    blocks = state_s.shape[0]
    tile = 256
    count = [0]

    def load(src, dst):
        copy = pltpu.make_async_copy(src, dst, load_sem.at[count[0]])
        count[0] += 1
        copy.start()
        return copy

    def wait(copies):
        for copy in copies:
            copy.wait()

    first_in = [load(gb_t_h, wup.at[:, 0:rows_all])]
    act_in = [load(act_h.at[:, D * z : D * z + D], acts.at[:, D * z : D * z + D]) for z in range(4)]
    next_in = [load(gb_h, gb), load(wdn_h, ga_s), load(slope_h, slope), load(low_t_h, left)]
    mid_in = [
        load(gr2_h, gr2), load(xhat_h, wide), load(rstd_h, rstd), load(norm_h, norm_s),
        load(sums_h, norm_v),
    ]
    late_in = [
        load(state_h, state_s),
        load(trig_h.at[ds((place.x * 2 + place.c) * PIECE, PIECE, PIECE), :], trig_s),
    ]
    sq_v[...] = jnp.zeros_like(sq_v)
    fill_triangles(tri_s)
    engine = Engine(0.75)
    reduce = Reduce(place, engine, r_send, r_recv, store_sem, sq_v)
    shares = []
    for at, (kind, first, units, column, width, by_units, early) in enumerate(share_plan()):
        grad, out = {"down": (gd_s, down_o), "up": (gu_s, up_o), "attn": (ga_s, attn_o)}[kind]
        cut = out.at[first : first + units, :, :, column : column + width]
        mine = bufs[7 * at : 7 * at + 7]
        shares.append(Share(grad, first, units, column, width, by_units, early, mine, cut))
    shares = iter(shares)
    greet(place, corners=True)
    wait(first_in)

    for t in range(3):
        for z in range(PLANES):
            if t == 0:
                act_in[z].wait()
            starts = [D * z + 384 * y + 128 * t for y in range(2)]
            pair = [acts[:, start : start + 128] for start in starts]
            part = dot(wup[:, 0:rows_all], jnp.concatenate(pair, axis=1)).astype(bf16)
            for y in range(2):
                own = part[:, 128 * y : 128 * y + 128].reshape(8, 2, 48, 128)
                gd_s[:, z, y, :, :, 128 * t : 128 * t + 128] = own
            engine.tick(0.6)
        reduce.launch(next(shares))

    mid_in.append(load(wup_h, wup))
    for at, src in enumerate((q_h, k_h, v_h, att_h)):
        late_in.append(load(src, acts.at[:, D * at : D * at + D]))
    wait(next_in)
    for at in range(12):
        cols = slice(256 * at, 256 * at + 256)
        down_rows = ga_s[at // 3].reshape(D, D)[256 * (at % 3) : 256 * (at % 3) + 256]
        for part in range(0, rows_all, PIECE):
            span = slice(part, part + PIECE)
            grad = dot_nt(gb[span, :], down_rows) * slope[span, cols].astype(f32)
            slope[span, cols] = grad.astype(bf16)
        up = dot(left[...], slope[:, cols]).astype(bf16)
        gu_s[0, :, :, :, :, cols] = up.reshape(PLANES, 2, 2, 48, tile)
        engine.tick(1.4)
        if at % 4 == 3:
            reduce.launch(next(shares))
    att_t_in = load(att_t_h, left)
    wait(mid_in)
    gain_one = norm_s[0:1, :]
    norm_v[2:4, :] = norm_v[0:2, :]
    norm_v[0:2, :] = jnp.zeros((2, D), f32)

    def first_back(t, carry):
        cols = ds(t * tile, tile, tile)
        for part in range(0, rows_all, PIECE):
            span = slice(part, part + PIECE)
            gr2[span, cols] += dot_nt(slope[span, :], wup[cols, :])
        return carry

    def norm_part(t, carry):
        rows = ds(t * 128, 128, 128)
        unit, grad = wide[rows, :], gr2[rows, :]
        norm_v[0:1, :] += jnp.sum(grad * unit, axis=0, keepdims=True)
        norm_v[1:2, :] += jnp.sum(grad, axis=0, keepdims=True)
        grad = norm_back(grad * gain_one, unit, rstd[rows, 0:1])
        gr2[rows, :] = grad
        gb[rows, :] = grad.astype(bf16)
        return carry

    for part in range(3):
        lax.fori_loop(part, part + 1, first_back, 0)
        engine.tick(2.2)
    wo_in = load(wo_h, wup.at[:, 3 * D : 4 * D])
    for part in range(0, rows_all // 128, 4):
        lax.fori_loop(part, part + 4, norm_part, 0)
        engine.tick(0.8)
    norms = Total(place, engine, "norms", norm_v, norm_w, norm_z, t_send, t_recv)
    rden_in = load(rden_h, wide)
    att_t_in.wait()

    def outer(unit, column, grad):
        part = dot(left[...], grad).astype(bf16)
        part = part.reshape(PLANES, 2, 2, 48, 256)
        ga_s[unit, :, :, :, :, column : column + 256] = part
        engine.tick(0.6)

    for t in range(3):
        outer(3, 256 * t, gb[:, 256 * t : 256 * t + 256])
    reduce.launch(next(shares))
    x_t_in = load(x_t_h, left)
    wait(late_in)
    rden_in.wait()
    wo_in.wait()
    square = (2 * PAIR, PAIR)
    row_half = (lax.broadcasted_iota(jnp.int32, square, 0) & (PAIR - 1)) < HEAD
    by_head = (row_half == first_half(square)).astype(f32).astype(bf16)

    def split(i, carry):
        g, t = i // 3, lax.rem(i, 3)
        rows = ds(g * PIECE, PIECE, PIECE)
        grad = dot_nt(gb[rows, :], wup[ds(t * tile, tile, tile), 3 * D : 4 * D])
        for pair in range(2):
            base = t * tile + pair * PAIR
            cols, num_cols = ds(base, PAIR, PAIR), ds(3 * D + base, PAIR, PAIR)
            mine = grad[:, pair * PAIR : pair * PAIR + PAIR]
            recip = wide[rows, cols]
            along = mine * acts[rows, num_cols].astype(f32)
            high = along.astype(bf16)
            rest = (along - high.astype(f32)).astype(bf16)
            gden = -dot(jnp.concatenate([high, rest], axis=1), by_head) * recip
            high = gden.astype(bf16).astype(f32)
            lane = lane_in_head(gden.shape)
            both = jnp.where(lane == 0, high, jnp.where(lane == 1, gden - high, 0.0))
            acts[rows, num_cols] = both.astype(bf16)
            slope[rows, num_cols] = (mine * recip).astype(bf16)
        return carry

    for part in range(0, blocks // 2, 2):
        lax.fori_loop(part, part + 2, split, 0)
        engine.tick(1.6)

    def column_of(b, group):
        return ds(group * D + lax.rem(b, 6) * PAIR, PAIR, PAIR)

    def local(b, carry):
        rows, cols = block_of(b)
        queries = turned(acts[rows, cols], trig_s[...])
        state = dot_tn(queries, slope[rows, column_of(b, 3)])
        cross = dot_tn(acts[rows, column_of(b, 3)], queries)
        shape = (PAIR, 2 * PAIR)
        kept = jnp.where(top_half(shape) == pair_mask(shape), cross, 0.0)
        totals = jnp.broadcast_to(jnp.sum(kept, axis=0, keepdims=True), (16, 2 * PAIR))
        st_own[b] = squeeze_state(state, totals).astype(bf16)
        return carry

    for part in range(0, blocks, 4):
        lax.fori_loop(part, part + 4, local, 0)
        engine.tick(1.5)
    state = StateSum(place, engine, s_send, s_recv, st_own, st_twin, st_chip, st_prior, True)

    def soft_slope(feature):
        return 1.0 - jnp.exp(-feature.astype(f32))

    def take(b):
        rows, cols = block_of(b)
        num, den = slope[rows, column_of(b, 3)], acts[rows, column_of(b, 3)]
        q, k, v = (acts[rows, column_of(b, group)] for group in range(3))
        return jnp.concatenate([num, den], axis=1), num, q, k, v

    def query_grad(i, carry):
        marks = [2 * i, 2 * i + 1]
        taken = [take(b) + (state_s[b],) for b in marks]
        outs = []
        for own, _, q, k, v, packed in taken:
            grad = causal_product(own, with_ones(v), turned(k, trig_s[...]), tri_s)
            grad = (grad + dot_nt(own, spread_state(packed))) * trig_s[...]
            outs.append(((grad[:, :PAIR] + grad[:, PAIR:]) * soft_slope(q)).astype(bf16))
        for b, out in zip(marks, outs):
            slope[block_of(b)] = out
        return carry

    for part in range(blocks // 2):
        lax.fori_loop(part, part + 1, query_grad, 0)
        engine.tick(2.6)
    x_t_in.wait()
    for t in range(3):
        outer(0, 256 * t, slope[:, 256 * t : 256 * t + 256])
    reduce.launch(next(shares))
    engine.until("state")

    def key_grad(b, carry):
        own, num, q, k, v = take(b)
        queries, keys = turned(q, trig_s[...]), turned(k, trig_s[...])
        spread = spread_state(state.total(b).astype(bf16))
        grad = causal_transposed(own, with_ones(v), queries, tri_s)
        one = (lane_in_head(v.shape) == 0).astype(f32).astype(bf16)
        grad = (grad + dot_nt(jnp.concatenate([v, one], axis=1), spread)) * trig_s[...]
        grad = (grad[:, :PAIR] + grad[:, PAIR:]) * soft_slope(k)
        grad_v = causal_transposed(queries, keys, num, tri_s) + dot(keys, spread[:, :PAIR])
        rows, _ = block_of(b)
        slope[rows, column_of(b, 1)] = grad.astype(bf16)
        slope[rows, column_of(b, 2)] = grad_v.astype(bf16)
        return carry

    def group_of(t):
        def body(i, carry):
            return key_grad((i // 2) * 6 + t * 2 + lax.rem(i, 2), carry)

        return body

    for t in range(3):
        for part in range(blocks // 3):
            lax.fori_loop(part, part + 1, group_of(t), 0)
            engine.tick(2.3)
        for j in (1, 2):
            outer(j, 256 * t, slope[:, D * j + 256 * t : D * j + 256 * t + 256])
        reduce.launch(next(shares))
    stores = [
        pltpu.make_async_copy(slope.at[:, 0 : 3 * D], gp_o, load_sem.at[count[0]]),
        pltpu.make_async_copy(norm_v, norm_o, load_sem.at[count[0] + 1]),
        pltpu.make_async_copy(gr2, one_o, load_sem.at[count[0] + 2]),
    ]
    engine.until("norms")
    for copy in stores:
        copy.start()
    engine.until(*[("sum", k) for k in range(SHARES)])
    squares = Total(place, engine, "squares", sq_v, sq_w, sq_z, u_send, u_recv)
    engine.until("squares")
    stores.append(pltpu.make_async_copy(sq_v, square_o, load_sem.at[count[0] + 3]))
    stores[3].start()
    engine.rest()
    wait(stores)
    reduce.drain()
    norms.drain()
    squares.drain()
    state.drain()


def share_plan():
    plan = [("down", 0, 8, 128 * t, 128) for t in range(3)]
    plan += [("up", 0, 1, FF // 3 * t, FF // 3) for t in range(3)]
    plan += [("attn", 3, 1, 0, D), ("attn", 0, 1, 0, D)]
    plan += [("attn", 1, 2, 256 * t, 256) for t in range(3)]
    return [part + (part[0] == "down", 1 if at % 2 else 2) for at, part in enumerate(plan)]


SHARES = 11


def backward_call(s, norm_params, seq_count):
    rows = s["q"].shape[0]
    blocks = rows // PIECE * 6
    trig = turning_table(seq_count)
    names = (
        "wo", "wup", "q", "k", "v", "att", "rden", "xhat", "rstd", "x_t", "att_t",
        "low_t", "act", "slope", "gb", "gb_t", "gr2", "state", "sums",
    )
    wdn = s["wdn"].reshape(4, PLANES, 2, 2, 48, D)
    shapes = [
        ((rows, 3 * D), bf16), ((rows, D), f32),
        ((4, 2, 48, D), bf16), ((1, 2, 48, FF), bf16), ((8, 2, 48, FF // 8), bf16),
        ((8, D), f32), ((8, 128), f32),
    ]
    vmem = [
        ((D, FF), bf16), ((rows, FF), bf16), ((rows, FF), bf16), ((rows, D), f32),
        ((rows, D), bf16), ((D, rows), bf16), ((rows, D), f32), ((rows, 128), f32),
        ((4, PLANES, 2, 2, 48, D), bf16), ((8, PLANES, 2, 2, 48, FF // 8), bf16),
        ((1, PLANES, 2, 2, 48, FF), bf16),
        ((4, D), f32), ((PIECE, 2 * PAIR), f32), ((PIECE, PIECE // 2), bf16),
        ((blocks, 144, PAIR), bf16), ((blocks, 144, PAIR), bf16), ((blocks, 144, PAIR), bf16),
        ((blocks, 144, PAIR), bf16), ((blocks, 144, PAIR), bf16),
        ((8, D), f32), ((8, 8, D), f32), ((PLANES, 8, D), f32),
        ((8, 128), f32), ((8, 8, 128), f32), ((PLANES, 8, 128), f32),
    ]
    for _, _, units, _, width, by_units, early in share_plan():
        count, part = (units // 2, width) if by_units else (units, width // 2)
        vmem += [
            ((units, PLANES, 2, 48, width), bf16), ((count, PLANES, 48, part), bf16),
            ((count, PLANES, 48, part), bf16), ((count, early, 48, part), bf16),
            ((count, PLANES - early, 48, part), bf16), ((count, 3, 48, part), bf16),
            ((units, 2, 48, width), bf16),
        ]
    dma = pltpu.SemaphoreType.DMA
    sems = [(36,), (SHARES,), (SHARES, 12), (SHARES, 12), (3,), (3,), (10,), (10,), (10,), (10,)]
    hbm = pl.BlockSpec(memory_space=pl.ANY)
    return pl.pallas_call(
        backward_kernel,
        out_shape=[jax.ShapeDtypeStruct(*shape) for shape in shapes],
        in_specs=[hbm] * 22,
        out_specs=[hbm] * len(shapes),
        scratch_shapes=[pltpu.VMEM(*shape) for shape in vmem] + [dma(shape) for shape in sems],
        compiler_params=pltpu.CompilerParams(
            collective_id=1, has_side_effects=True, vmem_limit_bytes=VMEM_BYTES
        ),
        name="backward_reduce",
    )(*[s[name] for name in names], wdn, norm_params, trig)


def adam_step(weight, grad, first, second, rate, outs):
    first_new = beta_one * first + (1.0 - beta_one) * grad
    second_new = beta_two * second + (1.0 - beta_two) * grad * grad
    first_hat = first_new * (1.0 / (1.0 - beta_one**STEP))
    second_hat = second_new * (1.0 / (1.0 - beta_two**STEP))
    step = first_hat / (jnp.sqrt(second_hat) + epsilon) + weight_decay * weight
    grad_o, new_o, first_o, second_o = outs
    grad_o[...] = grad
    new_o[...] = weight - rate * step
    first_o[...] = first_new
    second_o[...] = second_new


def update_kernel(
    out_rate,
    attn_r, up_r, down_r, norm_r, square_r,
    attn_w, up_w, down_w, norm_w, attn_m, up_m, down_m, norm_m, attn_v, up_v, down_v, norm_v,
    attn_g, up_g, down_g, norm_g, grad_norm_o,
    attn_n, up_n, down_n, norm_n, attn_f, up_f, down_f, norm_f, attn_s, up_s, down_s, norm_s,
    grad_s, turned_s,
):
    norm_raw = norm_r[0:4, :]
    @pl.when(pl.program_id(0) == 0)
    def _():
        turned_s[...] = down_r[...].T.astype(f32)

    grad_norm = jnp.sqrt(
        jnp.sum(square_r[...], keepdims=True) + jnp.sum(norm_raw * norm_raw, keepdims=True)
    )
    clip = clip_limit / jnp.maximum(grad_norm, clip_limit)
    grad_norm_o[...] = grad_norm
    down_rate = learn_rate * math.sqrt(D / FF)
    grad = up_r[...].astype(f32) * clip
    adam_step(up_w[...], grad, up_m[...], up_v[...], learn_rate, (up_g, up_n, up_f, up_s))
    rows = down_w.shape[0]
    grad = turned_s[ds(pl.program_id(0) * rows, rows, rows), :] * clip
    outs = (down_g, down_n, down_f, down_s)
    adam_step(down_w[...], grad, down_m[...], down_v[...], down_rate, outs)
    for j in range(4):
        grad_s[:, j, :] = attn_r[j].astype(f32)
    shape = grad_s.shape
    rate = jnp.where(
        lax.broadcasted_iota(jnp.int32, shape, 1) == 3, learn_rate * out_rate, learn_rate
    )
    grad = grad_s[...] * clip.reshape(1, 1, 1)
    adam_step(attn_w[...], grad, attn_m[...], attn_v[...], rate, (attn_g, attn_n, attn_f, attn_s))
    outs = (norm_g, norm_n, norm_f, norm_s)
    adam_step(norm_w[...], norm_raw * clip, norm_m[...], norm_v[...], gain_rate, outs)


def update_call(raw, norm_raw, square, weights, firsts, seconds, length):
    steps = 6
    thin, thick = weights[0].shape[0], weights[2].shape[0]
    a, u, d = thin // steps, thin // steps, thick // steps
    attn = pl.BlockSpec((a, 4, D), lambda t: (t, 0, 0))
    up = pl.BlockSpec((u, FF), lambda t: (t, 0))
    down = pl.BlockSpec((d, D), lambda t: (t, 0))
    whole = lambda rows, cols: pl.BlockSpec((rows, cols), lambda t: (0, 0))
    norm = whole(4, D)
    kinds = [attn, up, down, norm]
    shapes = [jax.ShapeDtypeStruct(w.shape, f32) for w in weights]
    one = jax.ShapeDtypeStruct((1, 1), f32)
    return pl.pallas_call(
        functools.partial(update_kernel, math.sqrt(length // 8)),
        grid=(steps,),
        in_specs=[pl.BlockSpec((4, a, D), lambda t: (0, t, 0)), up, whole(D, thick)]
        + [whole(8, D), whole(8, 128)]
        + kinds * 3,
        out_specs=kinds + [whole(1, 1)] + kinds * 3,
        out_shape=shapes + [one] + shapes * 3,
        scratch_shapes=[
            pltpu.VMEM((a, 4, D), f32), pltpu.VMEM((thick, D), f32),
        ],
        compiler_params=pltpu.CompilerParams(vmem_limit_bytes=VMEM_BYTES),
        name="adamw_update",
    )(*raw, norm_raw, square, *weights, *firsts, *seconds)


def prefix(part, axis, combine, identity):
    place = lax.axis_index(axis)
    gathered = jax.tree.map(lambda a: lax.all_gather(a, axis), part)
    state = jax.tree.map(lambda a, e: jnp.zeros_like(a) + jnp.asarray(e, a.dtype), part, identity)

    def prefix_one(step, state):
        return combine(
            state, jax.tree.map(lambda a: lax.dynamic_index_in_dim(a, step, 0, False), gathered)
        )

    return lax.fori_loop(0, place, prefix_one, state)


def carried_in(shard, axis, join, neutral):
    count = lax.axis_size(axis)
    place = lax.axis_index(axis)
    ahead = count - 1 - place
    gathered = jax.tree.map(
        lambda a, kind: lax.all_gather(a.astype(kind), axis),
        shard,
        jax.tree.map(lambda a: jnp.bfloat16 if a.dtype == jnp.float32 else a.dtype, shard),
    )
    state = jax.tree.map(lambda a, e: jnp.zeros_like(a) + jnp.asarray(e, a.dtype), shard, neutral)

    def carried_one(step, state):
        source = count - 1 - step
        return join(
            state,
            jax.tree.map(
                lambda a, own: lax.dynamic_index_in_dim(a, source, 0, False).astype(own.dtype),
                gathered,
                shard,
            ),
        )

    return lax.fori_loop(0, ahead, carried_one, state)


def add_states(earlier, later):
    return jax.tree.map(jnp.add, earlier, later)


def layer_norm(values, gain_row, bias_row):
    centered = values - jnp.mean(values, axis=-1, keepdims=True)
    spread = jnp.mean(centered * centered, axis=-1, keepdims=True)
    return centered * lax.rsqrt(spread + norm_eps) * gain_row + bias_row


def piece_scores(query_cos, query_sin, key_cos, key_sin, causal):
    scores = jnp.einsum("ihe,jhe->hij", query_cos, key_cos, preferred_element_type=jnp.float32)
    scores = scores + jnp.einsum(
        "ihe,jhe->hij", query_sin, key_sin, preferred_element_type=jnp.float32
    )
    return jnp.where(causal[None], scores, 0.0)


def adamw(weight, gradient, first_moment, second, step_rate):
    first_new = beta_one * first_moment + (1.0 - beta_one) * gradient
    second_new = beta_two * second + (1.0 - beta_two) * gradient * gradient
    first_hat = first_new / (1.0 - beta_one**STEP)
    second_hat = second_new / (1.0 - beta_two**STEP)
    weight_new = weight - step_rate * (
        first_hat / (jnp.sqrt(second_hat) + epsilon) + weight_decay * weight
    )
    return (weight_new, first_new, second_new)


def plain_shards(
    layer_input,
    cotangent,
    attn_master,
    up_master,
    down_master,
    norm_params,
    attn_first,
    up_first,
    down_first,
    norm_first,
    attn_second,
    up_second,
    down_second,
    norm_second,
):
    groups, piece_rows, model_width = layer_input.shape
    head_count = model_width // HEAD
    length = piece_rows * lax.axis_size("seq")
    rows_all = groups * piece_rows
    attn_full, up_full, down_full = (
        lax.all_gather(attn_master.astype(jnp.bfloat16), "dp", axis=0, tiled=True),
        lax.all_gather(up_master.astype(jnp.bfloat16), "dp", axis=0, tiled=True),
        lax.all_gather(down_master.astype(jnp.bfloat16), "dp", axis=0, tiled=True),
    )
    project_in = attn_full[:, :3, :].reshape(model_width, 3 * model_width)
    out_weight = attn_full[:, 3, :]
    tokens = layer_input.reshape(rows_all, model_width)
    projected = jnp.dot(tokens, project_in, preferred_element_type=jnp.float32)
    query_pre = projected[:, :model_width]
    key_pre = projected[:, model_width : 2 * model_width]
    value_pre = projected[:, 2 * model_width :]
    position = (lax.axis_index("seq") * piece_rows + jnp.arange(piece_rows)).astype(jnp.float32)
    phase_angle = math.pi / 2 * position / length
    cosine_weight = jnp.tile(jnp.cos(phase_angle), groups)[:, None]
    sine_weight = jnp.tile(jnp.sin(phase_angle), groups)[:, None]
    query_feat = jax.nn.softplus(query_pre)
    key_feat = jax.nn.softplus(key_pre)
    shape_four = (groups, piece_rows, head_count, HEAD)
    query_cos = (query_feat * cosine_weight).astype(jnp.bfloat16).reshape(shape_four)
    query_sin = (query_feat * sine_weight).astype(jnp.bfloat16).reshape(shape_four)
    key_cos = (key_feat * cosine_weight).astype(jnp.bfloat16).reshape(shape_four)
    key_sin = (key_feat * sine_weight).astype(jnp.bfloat16).reshape(shape_four)
    values = value_pre.astype(jnp.bfloat16).reshape(shape_four)
    local_state = (
        jnp.stack(
            [
                jnp.einsum("gjhe,gjhf->ghef", key_cos, values, preferred_element_type=jnp.float32),
                jnp.einsum("gjhe,gjhf->ghef", key_sin, values, preferred_element_type=jnp.float32),
            ],
            axis=1,
        ),
        jnp.stack(
            [
                jnp.sum(key_cos, axis=1, dtype=jnp.float32),
                jnp.sum(key_sin, axis=1, dtype=jnp.float32),
            ],
            axis=1,
        ),
    )
    identity = jax.tree.map(jnp.zeros_like, local_state)
    prior_state, prior_total = prefix(
        (local_state[0], local_state[1]), "seq", add_states, (identity[0], identity[1])
    )
    causal = jnp.arange(piece_rows)[:, None] >= jnp.arange(piece_rows)[None, :]
    attended_list = []
    denominator_list = []
    for group_index in range(groups):
        scores = piece_scores(
            query_cos[group_index],
            query_sin[group_index],
            key_cos[group_index],
            key_sin[group_index],
            causal,
        )
        qcos_wide = query_cos[group_index].astype(jnp.float32)
        qsin_wide = query_sin[group_index].astype(jnp.float32)
        numerator = jnp.einsum(
            "hij,jhe->ihe",
            scores.astype(jnp.bfloat16),
            values[group_index],
            preferred_element_type=jnp.float32,
        )
        numerator = numerator + jnp.einsum(
            "ihe,hef->ihf", qcos_wide, prior_state[group_index, 0], precision=highest
        )
        numerator = numerator + jnp.einsum(
            "ihe,hef->ihf", qsin_wide, prior_state[group_index, 1], precision=highest
        )
        denominator = jnp.sum(scores, axis=-1).T
        denominator = denominator + jnp.einsum(
            "ihe,he->ih", qcos_wide, prior_total[group_index, 0], precision=highest
        )
        denominator = denominator + jnp.einsum(
            "ihe,he->ih", qsin_wide, prior_total[group_index, 1], precision=highest
        )
        attended_list.append(numerator / denominator[:, :, None])
        denominator_list.append(denominator)
    attended = jnp.stack(attended_list)
    attended_low = attended.reshape(rows_all, model_width).astype(jnp.bfloat16)
    branch_one = jnp.dot(attended_low, out_weight, preferred_element_type=jnp.float32)
    residual_one = tokens.astype(jnp.float32) + branch_one
    first_norm, norm_one_back = jax.vjp(layer_norm, residual_one, norm_params[0], norm_params[1])
    first_low = first_norm.astype(jnp.bfloat16)
    hidden = jnp.dot(first_low, up_full, preferred_element_type=jnp.float32)
    activated, gelu_back = jax.vjp(jax.nn.gelu, hidden)
    activated_low = activated.astype(jnp.bfloat16)
    branch_two = jnp.dot(activated_low, down_full, preferred_element_type=jnp.float32)
    result, norm_two_back = jax.vjp(
        layer_norm, first_norm + branch_two, norm_params[2], norm_params[3]
    )
    layer_output = result.astype(jnp.bfloat16).reshape(groups, piece_rows, model_width)
    grad_residual_two, grad_gain_two, grad_bias_two = norm_two_back(
        cotangent.reshape(rows_all, model_width).astype(jnp.float32)
    )
    grad_branch_two = grad_residual_two.astype(jnp.bfloat16)
    grad_down = jnp.einsum(
        "nf,nd->fd", activated_low, grad_branch_two, preferred_element_type=jnp.float32
    )
    grad_activated = jnp.einsum(
        "nd,fd->nf", grad_branch_two, down_full, preferred_element_type=jnp.float32
    )
    grad_hidden = gelu_back(grad_activated)[0].astype(jnp.bfloat16)
    grad_up = jnp.einsum("nd,nf->df", first_low, grad_hidden, preferred_element_type=jnp.float32)
    grad_first = grad_residual_two + jnp.einsum(
        "nf,df->nd", grad_hidden, up_full, preferred_element_type=jnp.float32
    )
    grad_residual_one, grad_gain_one, grad_bias_one = norm_one_back(grad_first)
    grad_branch_one = grad_residual_one.astype(jnp.bfloat16)
    grad_out_weight = jnp.einsum(
        "nd,ne->de", attended_low, grad_branch_one, preferred_element_type=jnp.float32
    )
    grad_attended = jnp.einsum(
        "ne,de->nd", grad_branch_one, out_weight, preferred_element_type=jnp.float32
    ).reshape(shape_four)
    grad_qcos_list = []
    grad_qsin_list = []
    grad_kcos_list = []
    grad_ksin_list = []
    grad_values_list = []
    prior_grad_state = []
    prior_grad_total = []
    for group_index in range(groups):
        denominator = denominator_list[group_index]
        grad_numerator = (grad_attended[group_index] / denominator[:, :, None]).astype(jnp.bfloat16)
        grad_denominator = (
            -jnp.sum(grad_attended[group_index] * attended[group_index], axis=-1) / denominator
        )
        scores = piece_scores(
            query_cos[group_index],
            query_sin[group_index],
            key_cos[group_index],
            key_sin[group_index],
            causal,
        )
        grad_scores = (
            jnp.einsum(
                "ihe,jhe->hij",
                grad_numerator,
                values[group_index],
                preferred_element_type=jnp.float32,
            )
            + grad_denominator.T[:, :, None]
        )
        grad_scores = jnp.where(causal[None], grad_scores, 0.0).astype(jnp.bfloat16)
        grad_numerator_wide = grad_numerator.astype(jnp.float32)
        grad_qcos = jnp.einsum(
            "hij,jhe->ihe", grad_scores, key_cos[group_index], preferred_element_type=jnp.float32
        )
        grad_qcos = grad_qcos + jnp.einsum(
            "ihf,hef->ihe", grad_numerator_wide, prior_state[group_index, 0], precision=highest
        )
        grad_qcos = grad_qcos + grad_denominator[:, :, None] * prior_total[group_index, 0][None]
        grad_qsin = jnp.einsum(
            "hij,jhe->ihe", grad_scores, key_sin[group_index], preferred_element_type=jnp.float32
        )
        grad_qsin = grad_qsin + jnp.einsum(
            "ihf,hef->ihe", grad_numerator_wide, prior_state[group_index, 1], precision=highest
        )
        grad_qsin = grad_qsin + grad_denominator[:, :, None] * prior_total[group_index, 1][None]
        grad_qcos_list.append(grad_qcos)
        grad_qsin_list.append(grad_qsin)
        grad_kcos_list.append(
            jnp.einsum(
                "hij,ihe->jhe",
                grad_scores,
                query_cos[group_index],
                preferred_element_type=jnp.float32,
            )
        )
        grad_ksin_list.append(
            jnp.einsum(
                "hij,ihe->jhe",
                grad_scores,
                query_sin[group_index],
                preferred_element_type=jnp.float32,
            )
        )
        grad_values_list.append(
            jnp.einsum(
                "hij,ihe->jhe",
                scores.astype(jnp.bfloat16),
                grad_numerator,
                preferred_element_type=jnp.float32,
            )
        )
        prior_grad_state.append(
            jnp.stack(
                [
                    jnp.einsum(
                        "ihe,ihf->hef",
                        query_cos[group_index],
                        grad_numerator,
                        preferred_element_type=jnp.float32,
                    ),
                    jnp.einsum(
                        "ihe,ihf->hef",
                        query_sin[group_index],
                        grad_numerator,
                        preferred_element_type=jnp.float32,
                    ),
                ]
            )
        )
        prior_grad_total.append(
            jnp.stack(
                [
                    jnp.einsum(
                        "ihe,ih->he",
                        query_cos[group_index].astype(jnp.float32),
                        grad_denominator,
                        precision=highest,
                    ),
                    jnp.einsum(
                        "ihe,ih->he",
                        query_sin[group_index].astype(jnp.float32),
                        grad_denominator,
                        precision=highest,
                    ),
                ]
            )
        )
    later_state, later_total = carried_in(
        (jnp.stack(prior_grad_state), jnp.stack(prior_grad_total)),
        "seq",
        add_states,
        (identity[0], identity[1]),
    )
    values_wide = values.astype(jnp.float32)
    kcos_wide = key_cos.astype(jnp.float32)
    ksin_wide = key_sin.astype(jnp.float32)
    grad_kcos = (
        jnp.stack(grad_kcos_list)
        + jnp.einsum("gjhf,ghef->gjhe", values_wide, later_state[:, 0], precision=highest)
        + later_total[:, 0][:, None]
    )
    grad_ksin = (
        jnp.stack(grad_ksin_list)
        + jnp.einsum("gjhf,ghef->gjhe", values_wide, later_state[:, 1], precision=highest)
        + later_total[:, 1][:, None]
    )
    grad_values = jnp.stack(grad_values_list)
    grad_values = grad_values + jnp.einsum(
        "gjhe,ghef->gjhf", kcos_wide, later_state[:, 0], precision=highest
    )
    grad_values = grad_values + jnp.einsum(
        "gjhe,ghef->gjhf", ksin_wide, later_state[:, 1], precision=highest
    )
    grad_query = (
        jnp.stack(grad_qcos_list).reshape(rows_all, model_width) * cosine_weight
        + jnp.stack(grad_qsin_list).reshape(rows_all, model_width) * sine_weight
    )
    grad_keys = (
        grad_kcos.reshape(rows_all, model_width) * cosine_weight
        + grad_ksin.reshape(rows_all, model_width) * sine_weight
    )
    grad_projected = jnp.concatenate(
        [
            (grad_query * jax.nn.sigmoid(query_pre)).astype(jnp.bfloat16),
            (grad_keys * jax.nn.sigmoid(key_pre)).astype(jnp.bfloat16),
            grad_values.reshape(rows_all, model_width).astype(jnp.bfloat16),
        ],
        axis=1,
    )
    input_grad = grad_residual_one + jnp.einsum(
        "nk,dk->nd", grad_projected, project_in, preferred_element_type=jnp.float32
    )
    input_grad = input_grad.reshape(groups, piece_rows, model_width)
    grad_in = jnp.einsum("nd,nk->dk", tokens, grad_projected, preferred_element_type=jnp.float32)
    grad_attn = jnp.concatenate(
        [grad_in.reshape(model_width, 3, model_width), grad_out_weight[:, None, :]], axis=1
    )
    norm_grad_local = jnp.stack([grad_gain_one, grad_bias_one, grad_gain_two, grad_bias_two])
    norm_grad_raw = lax.psum(norm_grad_local, ("dp", "seq"))
    row_blocks = (
        lax.psum_scatter(
            grad_attn.astype(jnp.bfloat16), "dp", scatter_dimension=0, tiled=True
        ).astype(jnp.float32),
        lax.psum_scatter(
            grad_up.astype(jnp.bfloat16), "dp", scatter_dimension=0, tiled=True
        ).astype(jnp.float32),
        lax.psum_scatter(
            grad_down.astype(jnp.bfloat16), "dp", scatter_dimension=0, tiled=True
        ).astype(jnp.float32),
    )
    shard_attn, shard_up, shard_down = (
        lax.psum(row_blocks[0].astype(jnp.bfloat16), "seq").astype(jnp.float32),
        lax.psum(row_blocks[1].astype(jnp.bfloat16), "seq").astype(jnp.float32),
        lax.psum(row_blocks[2].astype(jnp.bfloat16), "seq").astype(jnp.float32),
    )
    local_square = (
        jnp.sum(shard_attn * shard_attn)
        + jnp.sum(shard_up * shard_up)
        + jnp.sum(shard_down * shard_down)
    )
    square = lax.psum(local_square, "dp") + jnp.sum(norm_grad_raw * norm_grad_raw)
    grad_norm = jnp.sqrt(square)
    clip_scale = clip_limit / jnp.maximum(grad_norm, clip_limit)
    attn_grad = shard_attn * clip_scale
    up_grad = shard_up * clip_scale
    down_grad = shard_down * clip_scale
    norm_grad = norm_grad_raw * clip_scale
    attn_rate = (
        learn_rate * jnp.array([1.0, 1.0, 1.0, math.sqrt(length // 8)], jnp.float32)[None, :, None]
    )
    attn_new, attn_first_new, attn_second_new = adamw(
        attn_master, attn_grad, attn_first, attn_second, attn_rate
    )
    up_new, up_first_new, up_second_new = adamw(up_master, up_grad, up_first, up_second, learn_rate)
    down_new, down_first_new, down_second_new = adamw(
        down_master, down_grad, down_first, down_second, learn_rate * math.sqrt(D / FF)
    )
    norm_new, norm_first_new, norm_second_new = adamw(
        norm_params, norm_grad, norm_first, norm_second, gain_rate
    )
    return (
        layer_output,
        input_grad,
        attn_grad,
        up_grad,
        down_grad,
        norm_grad,
        grad_norm,
        attn_new,
        up_new,
        down_new,
        norm_new,
        attn_first_new,
        up_first_new,
        down_first_new,
        norm_first_new,
        attn_second_new,
        up_second_new,
        down_second_new,
        norm_second_new,
    )


def fused_shards(
    layer_input, cotangent, attn_master, up_master, down_master, norm_params,
    attn_first, up_first, down_first, norm_first,
    attn_second, up_second, down_second, norm_second,
):
    groups, piece_rows, model_width = layer_input.shape
    seq_count = lax.axis_size("seq")
    rows = groups * piece_rows
    weights = (attn_master, up_master, down_master, norm_params)
    saved = forward_call(
        layer_input.reshape(rows, model_width), *weights, seq_count,
    )
    saved |= second_norm(saved, cotangent.reshape(rows, model_width), norm_params)
    gp, one, attn, up, down, norm_raw, square = backward_call(saved, norm_params, seq_count)
    input_grad = input_call(gp, saved["wqkv"], one)
    raw = (attn.reshape(4, -1, D), up.reshape(-1, FF), down.reshape(D, -1))
    outs = update_call(
        raw, norm_raw, square, weights,
        (attn_first, up_first, down_first, norm_first),
        (attn_second, up_second, down_second, norm_second), piece_rows * seq_count,
    )
    return (
        saved["out"].reshape(layer_input.shape), input_grad.reshape(layer_input.shape),
        *outs[:4], outs[4].reshape(()), *outs[5:],
    )


def shards(*args):
    groups, piece_rows, model_width = args[0].shape
    planes = lax.axis_size("dp") // 2
    if piece_rows == PIECE and planes == PLANES and lax.axis_size("seq") == 4:
        return fused_shards(*args)
    return plain_shards(*args)


def solution(mesh):
    in_specs = (
        P("dp", "seq", None),
        P("dp", "seq", None),
        P("dp", None, None),
        P("dp", None),
        P("dp", None),
        P(),
        P("dp", None, None),
        P("dp", None),
        P("dp", None),
        P(),
        P("dp", None, None),
        P("dp", None),
        P("dp", None),
        P(),
    )
    out_specs = (
        P("dp", "seq", None),
        P("dp", "seq", None),
        P("dp", None, None),
        P("dp", None),
        P("dp", None),
        P(),
        P(),
        P("dp", None, None),
        P("dp", None),
        P("dp", None),
        P(),
        P("dp", None, None),
        P("dp", None),
        P("dp", None),
        P(),
        P("dp", None, None),
        P("dp", None),
        P("dp", None),
        P(),
    )
    return jax.shard_map(shards, mesh=mesh, in_specs=in_specs, out_specs=out_specs, check_vma=False)
```

```python
import functools
import math

import jax
import jax.numpy as jnp
import numpy as np
from jax import lax
from jax.experimental import pallas as pl
from jax.experimental.pallas import tpu as pltpu
from jax.sharding import PartitionSpec as P

D = 768
HEAD = 64
FF = 3072
STEP = 5


highest = lax.Precision.HIGHEST
beta_one = 0.5
beta_two = 0.5
learn_rate = 0.02
gain_rate = 0.2
epsilon = 1e-08
weight_decay = 0.01
norm_eps = 1e-05
clip_limit = 1.0


MESH = pl.DeviceIdType.MESH
f32, bf16 = jnp.float32, jnp.bfloat16
PIECE = 512
PAIR = 2 * HEAD
PLANES = 4
VMEM_BYTES = 63 * 1024 * 1024


def dot(left, right):
    return jnp.dot(left, right, preferred_element_type=f32)


def dot_nt(left, right):
    return lax.dot_general(left, right, (((1,), (1,)), ((), ())), preferred_element_type=f32)


def dot_tn(left, right):
    return lax.dot_general(left, right, (((0,), (0,)), ((), ())), preferred_element_type=f32)


def first_half(shape):
    return lax.broadcasted_iota(jnp.int32, shape, 1) < HEAD


def top_half(shape):
    return lax.broadcasted_iota(jnp.int32, shape, 0) < HEAD


def own_head(value, head):
    mask = first_half(value.shape)
    zero = jnp.zeros_like(value)
    return jnp.where(mask, value, zero) if head == 0 else jnp.where(mask, zero, value)


def two_heads(first, second):
    return jnp.where(first_half(first.shape), first, second)


def pair_mask(shape):
    return (lax.broadcasted_iota(jnp.int32, shape, 1) & (PAIR - 1)) < HEAD


def stack_heads(value):
    mask, zero = pair_mask(value.shape), jnp.zeros_like(value)
    return jnp.concatenate([jnp.where(mask, value, zero), jnp.where(mask, zero, value)], axis=0)


def join_heads(stacked):
    first, second = stacked[: stacked.shape[0] // 2], stacked[stacked.shape[0] // 2 :]
    return jnp.where(pair_mask(first.shape), first, second)


def side_by_side(wide):
    half = wide.shape[1] // 2
    return jnp.concatenate([wide[:, :half], wide[:, half:]], axis=0)


def fill_triangles(tri_s):
    half = tri_s.shape[1]
    row = lax.broadcasted_iota(jnp.int32, (half, half), 0)
    col = lax.broadcasted_iota(jnp.int32, (half, half), 1)
    tri_s[0:half] = (row >= col).astype(f32).astype(bf16)
    tri_s[half:] = (row <= col).astype(f32).astype(bf16)


def causal_product(own, other, right, tri_s):
    half = PIECE // 2
    tri = jnp.concatenate([tri_s[0:half], tri_s[0:half]], axis=0)
    tops, lows = stack_heads(own[0:half]), stack_heads(own[half:])
    first = dot_nt(jnp.concatenate([tops, lows], axis=0), other[0:half]).astype(bf16)
    near = dot_nt(lows, other[half:]).astype(bf16) * tri
    first = jnp.concatenate([first[:PIECE] * tri, first[PIECE:]], axis=0)
    out = dot(first, right[0:half])
    low = out[PIECE:] + dot(near, right[half:])
    return jnp.concatenate([join_heads(out[:PIECE]), join_heads(low)], axis=0)


def causal_transposed(own, other, right, tri_s):
    half = PIECE // 2
    tri = jnp.concatenate([tri_s[half:], tri_s[half:]], axis=1)
    top = dot_nt(other[0:half], stack_heads(own[0:half])).astype(bf16) * tri
    low = dot_nt(other, stack_heads(own[half:])).astype(bf16)
    low = jnp.concatenate([low[0:half], low[half:] * tri], axis=0)
    out = dot(side_by_side(low), right[half:])
    more = dot(side_by_side(top), right[0:half])
    first = jnp.concatenate([out[0:half] + more[0:half], out[half:PIECE]], axis=0)
    second = jnp.concatenate([out[PIECE : PIECE + half] + more[half:], out[PIECE + half :]], axis=0)
    return jnp.where(pair_mask(first.shape), first, second)


def with_ones(value):
    return jnp.concatenate([value, jnp.ones_like(value)], axis=1)


def turned(value, trig):
    wide = value.astype(f32)
    cos, sin = trig[:, :PAIR], trig[:, PAIR:]
    return jnp.concatenate([(wide * cos).astype(bf16), (wide * sin).astype(bf16)], axis=1)


def squeeze_state(state, totals):
    cos = two_heads(state[0:HEAD], state[HEAD : 2 * HEAD])
    sin = two_heads(state[2 * HEAD : 3 * HEAD], state[3 * HEAD :])
    row = lax.broadcasted_iota(jnp.int32, (16, PAIR), 0)
    sums = jnp.where(row == 0, totals[:, :PAIR], totals[:, PAIR:])
    return jnp.concatenate([cos, sin, sums], axis=0)


def spread_state(packed):
    cos, sin = packed[0:HEAD], packed[HEAD:PAIR]
    state = jnp.concatenate(
        [own_head(cos, 0), own_head(cos, 1), own_head(sin, 0), own_head(sin, 1)], axis=0
    )
    row = lax.broadcasted_iota(jnp.int32, (16, PAIR), 0)
    sums = packed[PAIR:]
    ones = jnp.ones((16, PAIR), bf16)
    blocks = []
    for kind in range(2):
        column = dot_tn(jnp.where(row == kind, sums, jnp.zeros_like(sums)), ones).astype(bf16)
        blocks += [own_head(column[0:HEAD], 0), own_head(column[HEAD:], 1)]
    return jnp.concatenate([state, jnp.concatenate(blocks, axis=0)], axis=1)


def normed(value):
    centered = value - jnp.mean(value, axis=-1, keepdims=True)
    rstd = lax.rsqrt(jnp.mean(centered * centered, axis=-1, keepdims=True) + norm_eps)
    return centered * rstd, rstd


def norm_back(grad, unit, rstd):
    mean = jnp.mean(grad, axis=-1, keepdims=True)
    along = jnp.mean(grad * unit, axis=-1, keepdims=True)
    return rstd * (grad - mean - unit * along)


class Place:
    def __init__(self):
        dp, seq = lax.axis_index("dp"), lax.axis_index("seq")
        self.z, self.y, self.x, self.c = dp // 2, dp % 2, seq // 2, seq % 2
        self.shard = dp

    def device(self, z=None, y=None, x=None, c=None):
        z = self.z if z is None else z
        y = self.y if y is None else y
        x = self.x if x is None else x
        c = self.c if c is None else c
        return {"dp": z * 2 + y, "seq": x * 2 + c}

    def plane(self, shift):
        return lax.rem(self.z + shift + PLANES, PLANES)

    def across_y(self):
        return self.device(y=1 - self.y)

    def across_x(self):
        return self.device(x=1 - self.x)

    def across_c(self):
        return self.device(c=1 - self.c)

    def neighbours(self):
        planes = [self.device(z=self.plane(step)) for step in range(1, PLANES)]
        return planes + [self.across_y(), self.across_x(), self.across_c()]

    def corners(self):
        y, x, c = 1 - self.y, 1 - self.x, 1 - self.c
        return [
            self.device(x=x, c=c), self.device(y=y, c=c),
            self.device(y=y, x=x), self.device(y=y, x=x, c=c),
        ]

    def in_plane(self):
        return (self.y * 2 + self.x) * 2 + self.c


def greet(place, corners=False):
    barrier = pltpu.get_barrier_semaphore()
    peers = place.neighbours() + (place.corners() if corners else [])
    for peer in peers:
        pl.semaphore_signal(barrier, inc=1, device_id=peer, device_id_type=MESH)
    pl.semaphore_wait(barrier, len(peers))


class Engine:
    RATES = {"x": 30e3, "y": 30e3, "z": 23e3, "c": 200e3}

    def __init__(self, pace=1.0):
        self.now, self.free, self.pace = 0.0, dict.fromkeys(self.RATES, 0.0), pace
        self.eta, self.tasks, self.done = {}, [], set()

    def sent(self, key, link, size):
        self.now += 0.04
        start = max(self.now, self.free[link])
        self.free[link] = start + size / (self.pace * self.RATES[link])
        self.eta[key] = self.free[link] + 1.5

    def add(self, needs, act, mark=None, cost=0.05):
        self.tasks.append((needs, act, mark, cost))

    def due(self, task):
        return max((self.eta.get(key, math.inf) for key in task[0]), default=0.0)

    def run(self, task):
        self.tasks.remove(task)
        self.now = max(self.now, self.due(task)) + task[3]
        task[1]()
        if task[2] is not None:
            self.done.add(task[2])

    def tick(self, cost):
        self.now += cost
        while self.tasks:
            task = min(self.tasks, key=self.due)
            if self.due(task) > self.now:
                return
            self.run(task)

    def until(self, *marks):
        while not self.done.issuperset(marks):
            self.run(min(self.tasks, key=self.due))

    def rest(self):
        while self.tasks:
            self.run(min(self.tasks, key=self.due))


class Gather:
    def __init__(self, place, engine, chunks, send, recv, ready):
        self.place, self.engine, self.chunks = place, engine, chunks
        self.send, self.recv, self.sent, self.ready = send, recv, [], ready
        for k in range(len(chunks)):
            self.plan(k)

    def piece(self, k, z, y, x, c):
        ref, stride, base, height, column, width = self.chunks[k]
        if stride is None:
            return ref.at[
                z * 2 + y, base, ds(c * height, height, 16),
                pl.ds(pl.multiple_of(column + x * width, 128), width),
            ]
        row = (z * 2 + y) * stride + base + c * height
        return ref.at[
            pl.ds(pl.multiple_of(row, 16), height),
            pl.ds(pl.multiple_of(column + x * width, 128), width),
        ]

    def copy(self, k, index, ref, device):
        return pltpu.make_async_remote_copy(
            src_ref=ref,
            dst_ref=ref,
            send_sem=self.send.at[k, index],
            recv_sem=self.recv.at[k, index],
            device_id=device,
            device_id_type=MESH,
        )

    def push(self, k, index, ref, device, link):
        copy = self.copy(k, index, ref, device)
        copy.start()
        self.sent.append(copy)
        self.engine.sent((k, index), link, 2 * self.chunks[k][3] * self.chunks[k][5])

    def pull(self, k, index, ref):
        self.copy(k, index, ref, self.place.across_c()).wait_recv()

    def twin(self, k, index, ref):
        self.push(k, 14 + index, ref, self.place.across_c(), "c")

    def begin(self, k):
        p = self.place
        self.ready(k)
        own = self.piece(k, p.z, p.y, p.x, p.c)
        for step in (1, 3, 2):
            self.push(k, step - 1, own, p.device(z=p.plane(step)), "z")
        self.push(k, 3, own, p.across_y(), "y")
        other = self.piece(k, p.z, p.y, 1 - p.x, p.c)
        self.push(k, 10, other, p.across_y(), "y")
        self.push(k, 7, other, p.device(z=p.plane(1)), "z")

    def from_plane(self, k, step):
        p = self.place
        ref = self.piece(k, p.plane(-step), p.y, p.x, p.c)
        self.pull(k, step - 1, ref)
        self.push(k, 3 + step, ref, p.across_y(), "y")
        if step != 1:
            self.push(k, 6 + step, ref, p.across_x(), "x")
        self.twin(k, step - 1, ref)

    def by_y(self, k):
        return (1, 3) if k == 6 else ()

    def from_y(self, k, step):
        p = self.place
        ref = self.piece(k, p.plane(-step), 1 - p.y, p.x, p.c)
        self.pull(k, 3 + step, ref)
        if step and step not in self.by_y(k):
            self.push(k, 10 + step, ref, p.across_x(), "x")
        self.twin(k, 3 + step, ref)

    def from_x(self, k, step):
        p = self.place
        ref = self.piece(k, p.plane(-step), p.y, 1 - p.x, p.c)
        self.pull(k, 6 + step, ref)
        if step in self.by_y(k):
            self.push(k, 10 + step, ref, p.across_y(), "y")
        self.twin(k, 6 + step, ref)

    def corner(self, k, step):
        p = self.place
        ref = self.piece(k, p.plane(-step), 1 - p.y, 1 - p.x, p.c)
        self.pull(k, 10 + step, ref)
        self.twin(k, 10 + step, ref)

    def finish(self, k):
        p = self.place
        far = 1 - p.c
        for step in range(PLANES):
            z = p.plane(-step)
            if step:
                self.pull(k, 14 + step - 1, self.piece(k, z, p.y, p.x, far))
                self.pull(k, 20 + step, self.piece(k, z, p.y, 1 - p.x, far))
            self.pull(k, 17 + step, self.piece(k, z, 1 - p.y, p.x, far))
            self.pull(k, 24 + step, self.piece(k, z, 1 - p.y, 1 - p.x, far))

    def plan(self, k):
        before = [(k - 2, at) for at in range(3)] if k > 1 else []
        add = self.engine.add
        add(before, functools.partial(self.begin, k))
        for step in (1, 3, 2):
            add([(k, step - 1)], functools.partial(self.from_plane, k, step))
            add([(k, 6 + step)], functools.partial(self.from_x, k, step))
        for step in (0, 1, 3, 2):
            add([(k, 3 + step)], functools.partial(self.from_y, k, step))
            add([(k, 10 + step)], functools.partial(self.corner, k, step))
        add([(k, 14 + at) for at in range(14)], functools.partial(self.finish, k), k, 0.3)

    def drain(self):
        for copy in self.sent:
            copy.wait_send()


def ds(start, size, unit):
    return pl.ds(pl.multiple_of(start, unit), size)


def turn_over(source, target):
    for at in range(0, source.shape[0], 256):
        target[:, at : at + 256] = source[at : at + 256, :].T


def block_of(b):
    return ds((b // 6) * PIECE, PIECE, PIECE), ds(lax.rem(b, 6) * PAIR, PAIR, PAIR)


def forward_kernel(
    x_h, attn_h, up_h, down_h, norm_h, trig_h,
    wqkv_o, wo_o, wup_o, wdn_o, q_o, k_o, v_o, att_o, rden_o, xhat_o, rstd_o, xt_o, att_t_o,
    low_t_o, act_o, slope_o, state_o,
    wqkv, wo, wup, wdn, attn_st, up_st, down_st, x_s, norm_s, trig_s, tri_s,
    q_s, k_s, v_s, num_s, den_s, att_s, xhat_s, rstd_s, low_s, act_s, slope_a, slope_b, hid_a, hid_b,
    x_t_s, att_t_s, low_t_s, st_own, st_twin, st_chip, st_prior,
    load_sem, store_sem, tile_sem, g_send, g_recv, st_send, st_recv,
):
    place = Place()
    shard, x, c = place.shard, place.x, place.c
    groups = x_s.shape[0] // PIECE
    blocks = groups * 6
    loads = []
    for at, (src, dst) in enumerate(
        [
            (attn_h, attn_st), (up_h, up_st), (down_h, down_st), (x_h, x_s), (norm_h, norm_s),
            (trig_h.at[ds((x * 2 + c) * PIECE, PIECE, PIECE), :], trig_s),
        ]
    ):
        copy = pltpu.make_async_copy(src, dst, load_sem.at[at])
        copy.start()
        loads.append(copy)
    stores = []

    def store(src, dst):
        copy = pltpu.make_async_copy(src, dst, store_sem.at[len(stores)])
        copy.start()
        stores.append(copy)

    thin, thick = attn_st.shape[0], down_st.shape[0]
    chunks = [
        (wqkv, thin, 0, thin // 2, D, D),
        (wqkv, thin, 0, thin // 2, 0, D // 2),
        (wo, thin, 0, thin // 2, 0, D // 2),
        (wup, thin, 0, thin // 2, 0, FF // 4),
        (wup, thin, 0, thin // 2, FF // 2, FF // 4),
        (wdn, None, 0, thick // 4, 0, D // 2),
        (wdn, None, 1, thick // 4, 0, D // 2),
    ]
    def ready(k):
        narrow = ds(shard * thin, thin, 32)
        if k == 0:
            loads[0].wait()
            for j in range(3):
                wqkv[narrow, j * D : (j + 1) * D] = attn_st[:, j, :].astype(bf16)
        elif k == 2:
            wo[narrow, :] = attn_st[:, 3, :].astype(bf16)
        elif k == 3:
            loads[1].wait()
            wup[narrow, :] = up_st[...].astype(bf16)
        elif k == 5:
            loads[2].wait()
            wdn[shard] = down_st[...].astype(bf16).reshape(2, thick // 2, D)

    engine = Engine()
    gather = Gather(place, engine, chunks, g_send, g_recv, ready)
    greet(place)
    engine.tick(0.0)
    fill_triangles(tri_s)
    for copy in loads[3:]:
        copy.wait()
    turn_over(x_s, x_t_s)
    store(x_t_s, xt_o)
    engine.tick(3.0)
    engine.until(0)

    hidden = (hid_a, hid_b)

    def chain(products, finish, cost):
        hidden[0][...] = products[0]()
        for t in range(len(products)):
            if t + 1 < len(products):
                hidden[(t + 1) % 2][...] = products[t + 1]()
            finish(t, hidden[t % 2])
            engine.tick(cost)

    def project(parts):
        tiles = [(target, column, t, soft) for target, column, soft in parts for t in range(3)]

        def product(target, column, t, soft):
            return dot(x_s[...], wqkv[:, column + 256 * t : column + 256 * t + 256])

        def finish(at, pre):
            target, _, t, soft = tiles[at]
            pre = pre[...]
            if soft:
                pre = jnp.maximum(pre, 0.0) + jnp.log1p(jnp.exp(-jnp.abs(pre)))
            target[:, 256 * t : 256 * t + 256] = pre.astype(bf16)

        chain([functools.partial(product, *tile) for tile in tiles], finish, 0.7)

    project([(k_s, D, True), (v_s, 2 * D, False)])

    def local(b, carry):
        rows, cols = ds((b // 6) * PIECE, PIECE, PIECE), ds(lax.rem(b, 6) * PAIR, PAIR, PAIR)
        keys = turned(k_s[rows, cols], trig_s[...])
        state = dot_tn(keys, v_s[rows, cols])
        totals = dot(jnp.ones((16, PIECE), bf16), keys)
        st_own[b] = squeeze_state(state, totals).astype(bf16)
        return carry

    for part in range(0, blocks, 4):
        lax.fori_loop(part, part + 4, local, 0)
        engine.tick(1.4)
    state = StateSum(place, engine, st_send, st_recv, st_own, st_twin, st_chip, st_prior, False)
    engine.tick(0.0)
    engine.until(1)
    project([(q_s, 0, True)])
    store(wqkv, wqkv_o)
    store(q_s, q_o)
    store(k_s, k_o)
    store(v_s, v_o)

    def intra(i, carry):
        spots = [block_of(2 * i), block_of(2 * i + 1)]
        taken = [(q_s[at], k_s[at], v_s[at]) for at in spots]
        outs = [
            causal_product(
                turned(q, trig_s[...]), turned(k, trig_s[...]), with_ones(v), tri_s
            )
            for q, k, v in taken
        ]
        for at, out in zip(spots, outs):
            num_s[at] = out[:, :PAIR]
            den_s[at] = out[:, PAIR:]
        return carry

    for part in range(blocks // 2):
        lax.fori_loop(part, part + 1, intra, 0)
        engine.tick(1.6)
    engine.until("state")

    def inter(i, carry):
        spots = [block_of(2 * i), block_of(2 * i + 1)]
        states = [state.total(2 * i + at).astype(bf16) for at in range(2)]
        taken = [(q_s[at], num_s[at], den_s[at]) for at in spots]
        outs = []
        for (q, num, den), packed in zip(taken, states):
            more = dot(turned(q, trig_s[...]), spread_state(packed))
            recip = 1.0 / (den + more[:, PAIR:])
            outs.append((((num + more[:, :PAIR]) * recip).astype(bf16), recip))
        for at, (attended, recip) in zip(spots, outs):
            att_s[at] = attended
            den_s[at] = recip
        for at, packed in enumerate(states):
            st_chip[2 * i + at] = packed
        return carry

    for part in range(0, blocks // 2, 2):
        lax.fori_loop(part, part + 2, inter, 0)
        engine.tick(1.6)
    store(att_s, att_o)
    store(den_s, rden_o)
    turn_over(att_s, att_t_s)
    store(att_t_s, att_t_o)
    store(st_chip, state_o)
    engine.tick(1.0)
    engine.until(2)
    store(wo, wo_o)

    gain_one, bias_one = norm_s[0:1, :], norm_s[1:2, :]
    tile = 256

    def join(t, carry):
        cols = ds(t * tile, tile, tile)
        xhat_s[:, cols] = x_s[:, cols].astype(f32) + dot(att_s[...], wo[:, cols])
        return carry

    def join_norm(t, carry):
        rows = ds(t * tile, tile, tile)
        unit, rstd = normed(xhat_s[rows, :])
        xhat_s[rows, :] = unit
        rstd_s[rows, :] = jnp.broadcast_to(rstd, (tile, 128))
        low_s[rows, :] = (unit * gain_one + bias_one).astype(bf16)
        return carry

    for t in range(D // tile):
        lax.fori_loop(t, t + 1, join, 0)
        engine.tick(0.7)
    for part in range(x_s.shape[0] // tile):
        lax.fori_loop(part, part + 1, join_norm, 0)
        engine.tick(0.4)
    store(xhat_s, xhat_o)
    store(rstd_s, rstd_o)
    turn_over(low_s, low_t_s)
    store(low_t_s, low_t_o)
    engine.tick(1.0)
    engine.until(3)

    slopes, scale = (slope_a, slope_b), math.sqrt(2.0 / math.pi)

    def slope_copy(t):
        return pltpu.make_async_copy(
            slopes[t % 2], slope_o.at[:, 256 * t : 256 * t + 256], tile_sem.at[t % 2]
        )

    def expand(t, value):
        if t >= 2:
            slope_copy(t - 2).wait()
        value = value[...]
        squared = value * value
        curve = jnp.tanh(value * (scale + (scale * 0.044715) * squared))
        half = 0.5 + 0.5 * curve
        active = value * half
        slope = half + active * (1.0 - curve) * (scale + (3.0 * scale * 0.044715) * squared)
        act_s[:, 256 * t : 256 * t + 256] = active.astype(bf16)
        if t % 3 == 2:
            span = slice(256 * t - 512, 256 * t + 256)
            store(act_s.at[:, span], act_o.at[:, span])
        slopes[t % 2][...] = slope.astype(bf16)
        slope_copy(t).start()

    def raised(t):
        if t == 6:
            engine.until(4)
            store(wup, wup_o)
        return dot(low_s[...], wup[:, 256 * t : 256 * t + 256])

    chain([functools.partial(raised, t) for t in range(FF // 256)], expand, 1.1)
    engine.until(5)
    store(wdn.at[:, 0], wdn_o.at[:, 0])
    engine.until(6)
    store(wdn.at[:, 1], wdn_o.at[:, 1])
    for copy in stores + [slope_copy(10), slope_copy(11)]:
        copy.wait()
    gather.drain()
    state.drain()


def forward_call(tokens, attn_master, up_master, down_master, norm_params, seq_count):
    rows = tokens.shape[0]
    blocks = rows // PIECE * 6
    thin, thick = attn_master.shape[0], down_master.shape[0]
    trig = turning_table(seq_count)
    shapes = dict(
        wqkv=((D, 3 * D), bf16), wo=((D, D), bf16), wup=((D, FF), bf16), wdn=((FF // thick, 2, thick // 2, D), bf16),
        q=((rows, D), bf16), k=((rows, D), bf16), v=((rows, D), bf16), att=((rows, D), bf16),
        rden=((rows, D), f32), xhat=((rows, D), f32), rstd=((rows, 128), f32),
        x_t=((D, rows), bf16), att_t=((D, rows), bf16), low_t=((D, rows), bf16),
        act=((rows, FF), bf16), slope=((rows, FF), bf16), state=((blocks, 144, PAIR), bf16),
    )
    out_shape = [jax.ShapeDtypeStruct(s, d) for s, d in shapes.values()]
    hbm = pl.BlockSpec(memory_space=pl.ANY)
    scratch = [
        pltpu.VMEM((D, 3 * D), bf16), pltpu.VMEM((D, D), bf16),
        pltpu.VMEM((D, FF), bf16), pltpu.VMEM((FF // thick, 2, thick // 2, D), bf16),
        pltpu.VMEM((thin, 4, D), f32), pltpu.VMEM((thin, FF), f32), pltpu.VMEM((thick, D), f32),
        pltpu.VMEM((rows, D), bf16), pltpu.VMEM((4, D), f32),
        pltpu.VMEM((PIECE, 2 * PAIR), f32), pltpu.VMEM((PIECE, PIECE // 2), bf16),
        pltpu.VMEM((rows, D), bf16), pltpu.VMEM((rows, D), bf16), pltpu.VMEM((rows, D), bf16),
        pltpu.VMEM((rows, D), f32), pltpu.VMEM((rows, D), f32), pltpu.VMEM((rows, D), bf16),
        pltpu.VMEM((rows, D), f32), pltpu.VMEM((rows, 128), f32), pltpu.VMEM((rows, D), bf16),
        pltpu.VMEM((rows, FF), bf16), pltpu.VMEM((rows, 256), bf16),
        pltpu.VMEM((rows, 256), bf16), pltpu.VMEM((rows, 256), f32),
        pltpu.VMEM((rows, 256), f32),
        pltpu.VMEM((D, rows), bf16), pltpu.VMEM((D, rows), bf16), pltpu.VMEM((D, rows), bf16),
        pltpu.VMEM((blocks, 144, PAIR), bf16), pltpu.VMEM((blocks, 144, PAIR), bf16),
        pltpu.VMEM((blocks, 144, PAIR), bf16), pltpu.VMEM((blocks, 144, PAIR), bf16),
        pltpu.SemaphoreType.DMA((8,)), pltpu.SemaphoreType.DMA((24,)),
        pltpu.SemaphoreType.DMA((2,)),
        pltpu.SemaphoreType.DMA((7, 28)), pltpu.SemaphoreType.DMA((7, 28)),
        pltpu.SemaphoreType.DMA((3,)), pltpu.SemaphoreType.DMA((3,)),
    ]
    return dict(
        zip(
            shapes,
            pl.pallas_call(
                forward_kernel,
                out_shape=out_shape,
                in_specs=[hbm] * 6,
                out_specs=[hbm] * len(out_shape),
                scratch_shapes=scratch,
                compiler_params=pltpu.CompilerParams(
                    collective_id=0, has_side_effects=True, vmem_limit_bytes=VMEM_BYTES
                ),
                name="gather_forward",
            )(
                tokens, attn_master, up_master, down_master, norm_params,
                trig,
            ),
        )
    )


def second_norm_kernel(
    act, wdn, xhat, cot, norm, out_o, gb_o, gb_t_o, gr2_o, sums_o, sum_s
):
    rows = act.shape[0]
    for column in range(0, D, 256):
        cols = slice(column, column + 256)
        sum_s[:, cols] = dot(act[...], wdn[:, cols])

    @pl.when(pl.program_id(0) == 0)
    def _():
        sums_o[...] = jnp.zeros_like(sums_o)

    def body(t, carry):
        span = ds(t * 256, 256, 256)
        first = xhat[span, :] * norm[0:1, :] + norm[1:2, :]
        unit, rstd = normed(first + sum_s[span, :])
        out_o[span, :] = (unit * norm[2:3, :] + norm[3:4, :]).astype(bf16)
        grad = cot[span, :].astype(f32)
        sums_o[0:1, :] += jnp.sum(grad * unit, axis=0, keepdims=True)
        sums_o[1:2, :] += jnp.sum(grad, axis=0, keepdims=True)
        grad = norm_back(grad * norm[2:3, :], unit, rstd)
        gr2_o[span, :] = grad
        low = grad.astype(bf16)
        gb_o[span, :] = low
        gb_t_o[:, span] = low.T
        return carry

    lax.fori_loop(0, rows // 256, body, 0)


def second_norm(s, cotangent, norm_params):
    rows = cotangent.shape[0]
    tile = rows // 2
    by_rows = lambda width: pl.BlockSpec((tile, width), lambda t: (t, 0))
    whole = lambda height, width: pl.BlockSpec((height, width), lambda t: (0, 0))
    outs = pl.pallas_call(
        second_norm_kernel,
        grid=(rows // tile,),
        in_specs=[by_rows(FF), whole(FF, D), by_rows(D), by_rows(D), whole(4, D)],
        out_specs=[
            by_rows(D), by_rows(D), pl.BlockSpec((D, tile), lambda t: (0, t)), by_rows(D),
            whole(8, D),
        ],
        out_shape=[
            jax.ShapeDtypeStruct((rows, D), bf16), jax.ShapeDtypeStruct((rows, D), bf16),
            jax.ShapeDtypeStruct((D, rows), bf16), jax.ShapeDtypeStruct((rows, D), f32),
            jax.ShapeDtypeStruct((8, D), f32),
        ],
        scratch_shapes=[pltpu.VMEM((tile, D), f32)],
        compiler_params=pltpu.CompilerParams(vmem_limit_bytes=VMEM_BYTES),
        name="second_norm",
    )(s["act"], s["wdn"].reshape(FF, D), s["xhat"], cotangent, norm_params)
    return dict(zip(("out", "gb", "gb_t", "gr2", "sums"), outs))


def turning_table(seq_count):
    length = seq_count * PIECE
    angle = math.pi / 2 * np.arange(length, dtype=np.float64) / length
    trig = np.repeat(np.stack([np.cos(angle), np.sin(angle)], axis=1), PAIR, axis=1)
    return jnp.asarray(trig, f32)


class Share:
    def __init__(self, grad, first, units, column, width, by_units, early, bufs, out):
        self.grad, self.first, self.units = grad, first, units
        self.column, self.width, self.by_units, self.early = column, width, by_units, early
        self.count = units // 2 if by_units else units
        self.half = width if by_units else width // 2
        self.twin, self.from_x, self.from_y, self.via_x, self.via_y, self.planes, self.final = bufs
        self.out = out

    def side(self, x):
        if self.by_units:
            return x * self.count, slice(0, self.width)
        return 0, ds(x * self.half, self.half, 128)

    def part(self, x):
        first, lanes = self.side(x)
        return pl.ds(first, self.count), lanes


class Reduce:
    def __init__(self, place, engine, send, recv, store_sem, squares):
        self.place, self.engine, self.send, self.recv = place, engine, send, recv
        self.store_sem, self.squares = store_sem, squares
        self.sent, self.stored, self.count = [], [], 0

    def copy(self, k, index, src, dst, device):
        return pltpu.make_async_remote_copy(
            src_ref=src, dst_ref=dst, send_sem=self.send.at[k, index],
            recv_sem=self.recv.at[k, index], device_id=device, device_id_type=MESH,
        )

    def push(self, k, index, src, dst, device, link):
        copy = self.copy(k, index, src, dst, device)
        copy.start()
        self.sent.append((k, index, copy))
        self.engine.sent(("part", k, index), link, 2 * math.prod(dst.shape))

    def settle(self, parts):
        for k, index, copy in list(self.sent):
            if k in parts and index == 0:
                copy.wait_send()
                self.sent.remove((k, index, copy))

    def pull(self, k, index, dst):
        self.copy(k, index, dst, dst, self.place.across_c()).wait_recv()

    def launch(self, share):
        k = self.count
        self.count += 1
        src = share.grad.at[
            share.first : share.first + share.units, :, :, 1 - self.place.c, :,
            share.column : share.column + share.width,
        ]
        self.push(k, 0, src, share.twin, self.place.across_c(), "c")
        for needs, act, mark, cost in [
            ((0,), self.fold_core, "core", 0.8),
            ((1, 2), self.fold_corner, None, 0.3),
            ((3, 4, 5, 6), self.fold_square, None, 0.4),
            ((7, 8, 9), self.fold_planes, "sum", 0.3),
            ((10,), self.share_x, None, 0.05),
            ((11,), self.share_c, "whole", 0.05),
        ]:
            keys = [("part", k, at) for at in needs]
            self.engine.add(keys, functools.partial(act, k, share), (mark, k), cost)

    def fold_core(self, k, s):
        p = self.place
        self.pull(k, 0, s.twin)
        own = s.grad[s.first : s.first + s.units, :, :, p.c, :, s.column : s.column + s.width]
        s.twin[...] = (s.twin[...].astype(f32) + own.astype(f32)).astype(bf16)
        e, oy, t = s.early, 1 - p.y, s.twin
        (mine, near), (theirs, far) = s.part(p.x), s.part(1 - p.x)
        self.push(k, 1, t.at[theirs, 0:e, oy, :, far], s.via_x, p.across_x(), "x")
        self.push(k, 2, t.at[theirs, e:PLANES, oy, :, far], s.via_y, p.across_y(), "y")
        self.push(
            k, 3, t.at[theirs, 0:e, p.y, :, far], s.from_x.at[:, 0:e], p.across_x(), "x"
        )
        self.push(
            k, 4, t.at[mine, e:PLANES, oy, :, near], s.from_y.at[:, e:PLANES], p.across_y(), "y"
        )

    def fold_corner(self, k, s):
        p, e, t, oy = self.place, s.early, s.twin, 1 - self.place.y
        (mine, near), (theirs, far) = s.part(p.x), s.part(1 - p.x)
        self.pull(k, 1, s.via_x)
        at = (mine, slice(0, e), oy, slice(None), near)
        t[at] = (t[at].astype(f32) + s.via_x[...].astype(f32)).astype(bf16)
        self.push(k, 5, t.at[mine, 0:e, oy, :, near], s.from_y.at[:, 0:e], p.across_y(), "y")
        self.pull(k, 2, s.via_y)
        at = (theirs, slice(e, PLANES), p.y, slice(None), far)
        t[at] = (t[at].astype(f32) + s.via_y[...].astype(f32)).astype(bf16)
        self.push(
            k, 6, t.at[theirs, e:PLANES, p.y, :, far], s.from_x.at[:, e:PLANES], p.across_x(), "x"
        )

    def fold_square(self, k, s):
        p, e, t = self.place, s.early, s.twin
        mine, near = s.part(p.x)
        self.pull(k, 3, s.from_x.at[:, 0:e])
        self.pull(k, 4, s.from_y.at[:, e:PLANES])
        self.pull(k, 5, s.from_y.at[:, 0:e])
        self.pull(k, 6, s.from_x.at[:, e:PLANES])
        at = (mine, slice(None), p.y, slice(None), near)
        total = t[at].astype(f32) + s.from_x[...].astype(f32) + s.from_y[...].astype(f32)
        t[at] = total.astype(bf16)
        for step in (1, 3, 2):
            z = p.plane(step)
            self.push(
                k, 6 + step, t.at[mine, z, p.y, :, near], s.planes.at[:, step - 1],
                p.device(z=z), "z",
            )

    def fold_planes(self, k, s):
        p = self.place
        mine, near = s.part(p.x)
        for step in (1, 3, 2):
            self.pull(k, 6 + step, s.planes.at[:, step - 1])
        total = s.twin[mine, p.z, p.y, :, near].astype(f32)
        for step in range(3):
            total = total + s.planes[:, step].astype(f32)
        total = total.astype(bf16)
        s.final[mine, p.c, :, near] = total
        wide = total.astype(f32).reshape(s.count * 48, s.half)
        for lane in range(0, s.half, 128):
            part = wide[:, lane : lane + 128]
            self.squares[...] += jnp.sum((part * part).reshape(-1, 8, 128), axis=0)
        piece = s.final.at[mine, p.c, :, near]
        self.push(k, 10, piece, piece, p.across_x(), "x")

    def share_x(self, k, s):
        p = self.place
        theirs, far = s.part(1 - p.x)
        self.pull(k, 10, s.final.at[theirs, p.c, :, far])
        half = s.final.at[:, p.c]
        self.push(k, 11, half, half, p.across_c(), "c")

    def share_c(self, k, s):
        self.pull(k, 11, s.final.at[:, 1 - self.place.c])
        copy = pltpu.make_async_copy(s.final, s.out, self.store_sem.at[k])
        copy.start()
        self.stored.append(copy)

    def drain(self):
        for _, _, copy in self.sent:
            copy.wait_send()
        for copy in self.stored:
            copy.wait()


class Total:
    def __init__(self, place, engine, name, value, near, planes, send, recv):
        self.place, self.engine, self.name = place, engine, name
        self.value, self.near, self.planes = value, near, planes
        self.send, self.recv, self.sent = send, recv, []
        y, x, c = 1 - place.y, 1 - place.x, 1 - place.c
        peers = [place.across_c(), place.across_x(), place.across_y()] + place.corners()
        flips = [(0, 0, 1), (0, 1, 0), (1, 0, 0), (0, 1, 1), (1, 0, 1), (1, 1, 0), (1, 1, 1)]
        self.slots = [
            ((y if flip[0] else place.y) * 2 + (x if flip[1] else place.x)) * 2
            + (c if flip[2] else place.c)
            for flip in flips
        ]
        own = near.at[place.in_plane()]
        near[place.in_plane()] = value[...]
        for at, peer in enumerate(peers):
            self.push(at, own, peer, "cxyxyxy"[at])
        engine.add([(name, at) for at in range(7)], self.across)

    def copy(self, index, ref, device):
        return pltpu.make_async_remote_copy(
            src_ref=ref, dst_ref=ref, send_sem=self.send.at[index],
            recv_sem=self.recv.at[index], device_id=device, device_id_type=MESH,
        )

    def push(self, index, ref, device, link):
        copy = self.copy(index, ref, device)
        copy.start()
        self.sent.append(copy)
        self.engine.sent((self.name, index), link, 4 * math.prod(ref.shape))

    def across(self):
        p = self.place
        for at, slot in enumerate(self.slots):
            self.copy(at, self.near.at[slot], p.across_c()).wait_recv()
        total = self.near[0]
        for at in range(1, 8):
            total = total + self.near[at]
        self.planes[p.z] = total
        for step in (1, 3, 2):
            self.push(6 + step, self.planes.at[p.z], p.device(z=p.plane(step)), "z")
        self.engine.add([(self.name, at) for at in (7, 8, 9)], self.end, self.name)

    def end(self):
        for step in (1, 3, 2):
            own = self.planes.at[self.place.plane(-step)]
            self.copy(6 + step, own, self.place.across_c()).wait_recv()
        self.value[...] = (self.planes[0] + self.planes[1]) + (self.planes[2] + self.planes[3])

    def drain(self):
        for copy in self.sent:
            copy.wait_send()


class StateSum:
    def __init__(self, place, engine, send, recv, own, twin, chip, prior, late):
        self.x, self.c, self.engine = place.x, place.c, engine
        self.own, self.twin, self.chip, self.prior = own, twin, chip, prior
        self.giver, self.taker = (1, 0) if late else (0, 1)
        half = own.shape[0] // 2
        self.size = math.prod(own.shape)
        mine, other = ds(place.c * half, half, 1), ds((1 - place.c) * half, half, 1)

        def copy(index, src, dst, device):
            return pltpu.make_async_remote_copy(
                src_ref=src, dst_ref=dst, send_sem=send.at[index], recv_sem=recv.at[index],
                device_id=device, device_id_type=MESH,
            )

        self.swap = copy(0, own, twin, place.across_c())
        self.over = copy(1, chip.at[mine], prior.at[mine], place.across_x())
        self.pass_on = copy(2, prior.at[mine], prior.at[mine], place.across_c())
        self.taken = copy(2, prior.at[other], prior.at[other], place.across_c())
        self.swap.start()
        engine.sent("swap", "c", 2 * self.size)
        engine.add(["swap"], self.join, None, 0.5)
        engine.add(["over"], self.forward)
        engine.add(["pass"], self.end, "state")

    def join(self):
        self.swap.wait_recv()
        self.chip[...] = (self.own[...].astype(f32) + self.twin[...].astype(f32)).astype(bf16)

        @pl.when(self.x == self.giver)
        def _():
            self.over.start()

        self.engine.sent("over", "x", self.size)

    def forward(self):
        @pl.when(self.x == self.taker)
        def _():
            self.over.wait_recv()
            self.pass_on.start()

        self.engine.sent("pass", "c", self.size)

    def end(self):
        @pl.when(self.x == self.taker)
        def _():
            self.taken.wait_recv()

        @pl.when(self.x == self.giver)
        def _():
            self.over.wait_send()

    def drain(self):
        self.swap.wait_send()

        @pl.when(self.x == self.taker)
        def _():
            self.pass_on.wait_send()

    def total(self, b):
        far = jnp.where(self.x == self.taker, self.prior[b].astype(f32), 0.0)
        return far + jnp.where(self.c == self.taker, self.twin[b].astype(f32), 0.0)


def lane_in_head(shape):
    return lax.broadcasted_iota(jnp.int32, shape, 1) & (HEAD - 1)


def backward_kernel(
    wqkv_h, wo_h, wup_h, q_h, k_h, v_h, att_h, rden_h, xhat_h, rstd_h, x_t_h, att_t_h,
    low_t_h, act_h, slope_h, gb_h, gb_t_h, gr2_h, state_h, sums_h, wdn_h, norm_h, trig_h,
    input_o, attn_o, up_o, down_o, norm_o, square_o,
    wup, acts, slope, gr2, gb, left, wide, rstd, ga_s, gd_s, gu_s,
    norm_s, trig_s, tri_s, state_s, st_own, st_twin, st_chip, st_prior,
    norm_v, norm_w, norm_z, sq_v, sq_w, sq_z,
    *rest,
):
    bufs = rest[: 7 * SHARES]
    load_sem, store_sem, r_send, r_recv, s_send, s_recv = rest[7 * SHARES : 7 * SHARES + 6]
    t_send, t_recv, u_send, u_recv = rest[7 * SHARES + 6 :]
    place = Place()
    rows_all = gr2.shape[0]
    blocks = state_s.shape[0]
    tile = 256
    count = [0]

    def load(src, dst):
        copy = pltpu.make_async_copy(src, dst, load_sem.at[count[0]])
        count[0] += 1
        copy.start()
        return copy

    def wait(copies):
        for copy in copies:
            copy.wait()

    first_in = [load(gb_t_h, wup.at[:, 0:rows_all])]
    act_in = [load(act_h.at[:, D * z : D * z + D], acts.at[:, D * z : D * z + D]) for z in range(4)]
    sq_v[...] = jnp.zeros_like(sq_v)
    fill_triangles(tri_s)
    engine = Engine(0.75)
    reduce = Reduce(place, engine, r_send, r_recv, store_sem, sq_v)
    shares = []
    for at, (kind, first, units, column, width, by_units, early) in enumerate(share_plan()):
        grad, out = {"down": (gd_s, down_o), "up": (gu_s, up_o), "attn": (ga_s, attn_o)}[kind]
        cut = out.at[first : first + units, :, :, column : column + width]
        mine = bufs[7 * at : 7 * at + 7]
        shares.append(Share(grad, first, units, column, width, by_units, early, mine, cut))
    shares = iter(shares)
    greet(place, corners=True)
    wait(first_in)

    for t in range(3):
        for z in range(PLANES):
            if t == 0:
                act_in[z].wait()
            if t == 0 and z == PLANES - 1:
                next_in = [
                    load(gb_h, gb), load(wdn_h, ga_s), load(slope_h, slope), load(low_t_h, left),
                ]
            starts = [D * z + 384 * y + 128 * t for y in range(2)]
            pair = [acts[:, start : start + 128] for start in starts]
            part = dot(wup[:, 0:rows_all], jnp.concatenate(pair, axis=1)).astype(bf16)
            for y in range(2):
                own = part[:, 128 * y : 128 * y + 128].reshape(8, 2, 48, 128)
                gd_s[:, z, y, :, :, 128 * t : 128 * t + 128] = own
            engine.tick(0.6)
        reduce.launch(next(shares))

    mid_in = [
        load(wup_h, wup), load(gr2_h, gr2), load(xhat_h, wide), load(rstd_h, rstd),
        load(norm_h, norm_s), load(sums_h, norm_v),
    ]
    late_in = [
        load(state_h, state_s),
        load(trig_h.at[ds((place.x * 2 + place.c) * PIECE, PIECE, PIECE), :], trig_s),
    ]
    for at, src in enumerate((q_h, k_h, v_h, att_h)):
        late_in.append(load(src, acts.at[:, D * at : D * at + D]))
    wait(next_in)
    for at in range(12):
        cols = slice(256 * at, 256 * at + 256)
        down_rows = ga_s[at // 3].reshape(D, D)[256 * (at % 3) : 256 * (at % 3) + 256]
        for part in range(0, rows_all, PIECE):
            span = slice(part, part + PIECE)
            grad = dot_nt(gb[span, :], down_rows) * slope[span, cols].astype(f32)
            slope[span, cols] = grad.astype(bf16)
        up = dot(left[...], slope[:, cols]).astype(bf16)
        gu_s[0, :, :, :, :, cols] = up.reshape(PLANES, 2, 2, 48, tile)
        engine.tick(1.4)
        if at % 4 == 3:
            reduce.launch(next(shares))
    att_t_in = load(att_t_h, left)
    wait(mid_in)
    gain_one = norm_s[0:1, :]
    norm_v[2:4, :] = norm_v[0:2, :]
    norm_v[0:2, :] = jnp.zeros((2, D), f32)

    def first_back(t, carry):
        cols = ds(t * tile, tile, tile)
        for part in range(0, rows_all, PIECE):
            span = slice(part, part + PIECE)
            gr2[span, cols] += dot_nt(slope[span, :], wup[cols, :])
        return carry

    def norm_part(t, carry):
        rows = ds(t * 128, 128, 128)
        unit, grad = wide[rows, :], gr2[rows, :]
        norm_v[0:1, :] += jnp.sum(grad * unit, axis=0, keepdims=True)
        norm_v[1:2, :] += jnp.sum(grad, axis=0, keepdims=True)
        grad = norm_back(grad * gain_one, unit, rstd[rows, 0:1])
        gr2[rows, :] = grad
        gb[rows, :] = grad.astype(bf16)
        return carry

    for part in range(3):
        lax.fori_loop(part, part + 1, first_back, 0)
        engine.tick(2.2)
    wo_in = load(wo_h, wup.at[:, 3 * D : 4 * D])
    wqkv_in = load(wqkv_h, wup.at[:, 0 : 3 * D])
    for part in range(0, rows_all // 128, 4):
        lax.fori_loop(part, part + 4, norm_part, 0)
        engine.tick(0.8)
    norms = Total(place, engine, "norms", norm_v, norm_w, norm_z, t_send, t_recv)
    rden_in = load(rden_h, wide)
    att_t_in.wait()

    def outer(unit, column, grad):
        part = dot(left[...], grad).astype(bf16)
        part = part.reshape(PLANES, 2, 2, 48, 256)
        ga_s[unit, :, :, :, :, column : column + 256] = part
        engine.tick(0.6)

    for t in range(3):
        outer(3, 256 * t, gb[:, 256 * t : 256 * t + 256])
    reduce.launch(next(shares))
    x_t_in = load(x_t_h, left)
    wait(late_in)
    rden_in.wait()
    wo_in.wait()
    square = (2 * PAIR, PAIR)
    row_half = (lax.broadcasted_iota(jnp.int32, square, 0) & (PAIR - 1)) < HEAD
    by_head = (row_half == first_half(square)).astype(f32).astype(bf16)

    def split(i, carry):
        g, t = i // 3, lax.rem(i, 3)
        rows = ds(g * PIECE, PIECE, PIECE)
        grad = dot_nt(gb[rows, :], wup[ds(t * tile, tile, tile), 3 * D : 4 * D])
        for pair in range(2):
            base = t * tile + pair * PAIR
            cols, num_cols = ds(base, PAIR, PAIR), ds(3 * D + base, PAIR, PAIR)
            mine = grad[:, pair * PAIR : pair * PAIR + PAIR]
            recip = wide[rows, cols]
            along = mine * acts[rows, num_cols].astype(f32)
            high = along.astype(bf16)
            rest = (along - high.astype(f32)).astype(bf16)
            gden = -dot(jnp.concatenate([high, rest], axis=1), by_head) * recip
            high = gden.astype(bf16).astype(f32)
            lane = lane_in_head(gden.shape)
            both = jnp.where(lane == 0, high, jnp.where(lane == 1, gden - high, 0.0))
            acts[rows, num_cols] = both.astype(bf16)
            slope[rows, num_cols] = (mine * recip).astype(bf16)
        return carry

    for part in range(0, blocks // 2, 2):
        lax.fori_loop(part, part + 2, split, 0)
        engine.tick(1.6)

    def column_of(b, group):
        return ds(group * D + lax.rem(b, 6) * PAIR, PAIR, PAIR)

    def local(b, carry):
        rows, cols = block_of(b)
        queries = turned(acts[rows, cols], trig_s[...])
        state = dot_tn(queries, slope[rows, column_of(b, 3)])
        cross = dot_tn(acts[rows, column_of(b, 3)], queries)
        shape = (PAIR, 2 * PAIR)
        kept = jnp.where(top_half(shape) == pair_mask(shape), cross, 0.0)
        totals = jnp.broadcast_to(jnp.sum(kept, axis=0, keepdims=True), (16, 2 * PAIR))
        st_own[b] = squeeze_state(state, totals).astype(bf16)
        return carry

    for part in range(0, blocks, 4):
        lax.fori_loop(part, part + 4, local, 0)
        engine.tick(1.5)
    state = StateSum(place, engine, s_send, s_recv, st_own, st_twin, st_chip, st_prior, True)

    def soft_slope(feature):
        return 1.0 - jnp.exp(-feature.astype(f32))

    def take(b):
        rows, cols = block_of(b)
        num, den = slope[rows, column_of(b, 3)], acts[rows, column_of(b, 3)]
        q, k, v = (acts[rows, column_of(b, group)] for group in range(3))
        return jnp.concatenate([num, den], axis=1), num, q, k, v

    def query_grad(i, carry):
        marks = [2 * i, 2 * i + 1]
        taken = [take(b) + (state_s[b],) for b in marks]
        outs = []
        for own, _, q, k, v, packed in taken:
            grad = causal_product(own, with_ones(v), turned(k, trig_s[...]), tri_s)
            grad = (grad + dot_nt(own, spread_state(packed))) * trig_s[...]
            outs.append(((grad[:, :PAIR] + grad[:, PAIR:]) * soft_slope(q)).astype(bf16))
        for b, out in zip(marks, outs):
            slope[block_of(b)] = out
        return carry

    for part in range(blocks // 2):
        lax.fori_loop(part, part + 1, query_grad, 0)
        engine.tick(2.6)
    x_t_in.wait()
    for t in range(3):
        outer(0, 256 * t, slope[:, 256 * t : 256 * t + 256])
    reduce.launch(next(shares))
    engine.until("state")

    def key_pair(t):
        def body(g, carry):
            marks = [g * 6 + 2 * t, g * 6 + 2 * t + 1]
            taken = [take(b) + (state.total(b).astype(bf16),) for b in marks]
            outs = []
            for own, num, q, k, v, packed in taken:
                queries, keys = turned(q, trig_s[...]), turned(k, trig_s[...])
                spread = spread_state(packed)
                grad = causal_transposed(own, with_ones(v), queries, tri_s)
                one = (lane_in_head(v.shape) == 0).astype(f32).astype(bf16)
                grad = (grad + dot_nt(jnp.concatenate([v, one], axis=1), spread)) * trig_s[...]
                grad = (grad[:, :PAIR] + grad[:, PAIR:]) * soft_slope(k)
                grad_v = causal_transposed(queries, keys, num, tri_s)
                grad_v = grad_v + dot(keys, spread[:, :PAIR])
                outs.append((grad.astype(bf16), grad_v.astype(bf16)))
            for b, (grad, grad_v) in zip(marks, outs):
                rows, _ = block_of(b)
                slope[rows, column_of(b, 1)] = grad
                slope[rows, column_of(b, 2)] = grad_v
            return carry

        return body

    for t in range(3):
        for part in range(blocks // 6):
            lax.fori_loop(part, part + 1, key_pair(t), 0)
            engine.tick(4.4)
        for j in (1, 2):
            outer(j, 256 * t, slope[:, D * j + 256 * t : D * j + 256 * t + 256])
        reduce.launch(next(shares))
    wqkv_in.wait()

    def input_grad(t, carry):
        cols = ds(t * tile, tile, tile)
        for part in range(0, rows_all, PIECE):
            span = slice(part, part + PIECE)
            gr2[span, cols] += dot_nt(slope[span, 0 : 3 * D], wup[cols, 0 : 3 * D])
        return carry

    for part in range(3):
        lax.fori_loop(part, part + 1, input_grad, 0)
        engine.tick(1.8)
    stores = [
        pltpu.make_async_copy(gr2, input_o, load_sem.at[count[0]]),
        pltpu.make_async_copy(norm_v, norm_o, load_sem.at[count[0] + 1]),
    ]
    engine.until("norms")
    for copy in stores:
        copy.start()
    engine.until(*[("sum", k) for k in range(SHARES)])
    squares = Total(place, engine, "squares", sq_v, sq_w, sq_z, u_send, u_recv)
    engine.until("squares")
    stores.append(pltpu.make_async_copy(sq_v, square_o, load_sem.at[count[0] + 2]))
    stores[2].start()
    engine.rest()
    wait(stores)
    reduce.drain()
    norms.drain()
    squares.drain()
    state.drain()


def share_plan():
    plan = [("down", 0, 8, 128 * t, 128) for t in range(3)]
    plan += [("up", 0, 1, FF // 3 * t, FF // 3) for t in range(3)]
    plan += [("attn", 3, 1, 0, D), ("attn", 0, 1, 0, D)]
    plan += [("attn", 1, 2, 256 * t, 256) for t in range(3)]
    return [part + (part[0] == "down", 1 if at % 2 else 2) for at, part in enumerate(plan)]


SHARES = 11


def backward_call(s, norm_params, seq_count):
    rows = s["q"].shape[0]
    blocks = rows // PIECE * 6
    trig = turning_table(seq_count)
    names = (
        "wqkv", "wo", "wup", "q", "k", "v", "att", "rden", "xhat", "rstd", "x_t", "att_t",
        "low_t", "act", "slope", "gb", "gb_t", "gr2", "state", "sums",
    )
    wdn = s["wdn"].reshape(4, PLANES, 2, 2, 48, D)
    shapes = [
        ((rows, D), f32),
        ((4, 2, 48, D), bf16), ((1, 2, 48, FF), bf16), ((8, 2, 48, FF // 8), bf16),
        ((8, D), f32), ((8, 128), f32),
    ]
    vmem = [
        ((D, FF), bf16), ((rows, FF), bf16), ((rows, FF), bf16), ((rows, D), f32),
        ((rows, D), bf16), ((D, rows), bf16), ((rows, D), f32), ((rows, 128), f32),
        ((4, PLANES, 2, 2, 48, D), bf16), ((8, PLANES, 2, 2, 48, FF // 8), bf16),
        ((1, PLANES, 2, 2, 48, FF), bf16),
        ((4, D), f32), ((PIECE, 2 * PAIR), f32), ((PIECE, PIECE // 2), bf16),
        ((blocks, 144, PAIR), bf16), ((blocks, 144, PAIR), bf16), ((blocks, 144, PAIR), bf16),
        ((blocks, 144, PAIR), bf16), ((blocks, 144, PAIR), bf16),
        ((8, D), f32), ((8, 8, D), f32), ((PLANES, 8, D), f32),
        ((8, 128), f32), ((8, 8, 128), f32), ((PLANES, 8, 128), f32),
    ]
    for _, _, units, _, width, by_units, early in share_plan():
        count, part = (units // 2, width) if by_units else (units, width // 2)
        vmem += [
            ((units, PLANES, 2, 48, width), bf16), ((count, PLANES, 48, part), bf16),
            ((count, PLANES, 48, part), bf16), ((count, early, 48, part), bf16),
            ((count, PLANES - early, 48, part), bf16), ((count, 3, 48, part), bf16),
            ((units, 2, 48, width), bf16),
        ]
    dma = pltpu.SemaphoreType.DMA
    sems = [(36,), (SHARES,), (SHARES, 12), (SHARES, 12), (3,), (3,), (10,), (10,), (10,), (10,)]
    hbm = pl.BlockSpec(memory_space=pl.ANY)
    return pl.pallas_call(
        backward_kernel,
        out_shape=[jax.ShapeDtypeStruct(*shape) for shape in shapes],
        in_specs=[hbm] * 23,
        out_specs=[hbm] * len(shapes),
        scratch_shapes=[pltpu.VMEM(*shape) for shape in vmem] + [dma(shape) for shape in sems],
        compiler_params=pltpu.CompilerParams(
            collective_id=1, has_side_effects=True, vmem_limit_bytes=VMEM_BYTES
        ),
        name="backward_reduce",
    )(*[s[name] for name in names], wdn, norm_params, trig)


def adam_step(weight, grad, first, second, rate, outs):
    first_new = beta_one * first + (1.0 - beta_one) * grad
    second_new = beta_two * second + (1.0 - beta_two) * grad * grad
    first_hat = first_new * (1.0 / (1.0 - beta_one**STEP))
    second_hat = second_new * (1.0 / (1.0 - beta_two**STEP))
    step = first_hat / (jnp.sqrt(second_hat) + epsilon) + weight_decay * weight
    grad_o, new_o, first_o, second_o = outs
    grad_o[...] = grad
    new_o[...] = weight - rate * step
    first_o[...] = first_new
    second_o[...] = second_new


def update_kernel(
    out_rate, steps,
    input_h, attn_r, up_r, down_r, norm_r, square_r,
    attn_w, up_w, down_w, norm_w, attn_m, up_m, down_m, norm_m, attn_v, up_v, down_v, norm_v,
    input_o, attn_g, up_g, down_g, norm_g, grad_norm_o,
    attn_n, up_n, down_n, norm_n, attn_f, up_f, down_f, norm_f, attn_s, up_s, down_s, norm_s,
    grad_s, turned_s, input_s, copy_sem,
):
    norm_raw = norm_r[0:4, :]
    inward = pltpu.make_async_copy(input_h, input_s, copy_sem.at[0])
    outward = pltpu.make_async_copy(input_s, input_o, copy_sem.at[1])

    @pl.when(pl.program_id(0) == 0)
    def _():
        inward.start()
        turned_s[...] = down_r[...].T.astype(f32)

    grad_norm = jnp.sqrt(
        jnp.sum(square_r[...], keepdims=True) + jnp.sum(norm_raw * norm_raw, keepdims=True)
    )
    clip = clip_limit / jnp.maximum(grad_norm, clip_limit)
    grad_norm_o[...] = grad_norm
    down_rate = learn_rate * math.sqrt(D / FF)
    grad = up_r[...].astype(f32) * clip
    adam_step(up_w[...], grad, up_m[...], up_v[...], learn_rate, (up_g, up_n, up_f, up_s))
    rows = down_w.shape[0]
    grad = turned_s[ds(pl.program_id(0) * rows, rows, rows), :] * clip
    outs = (down_g, down_n, down_f, down_s)
    adam_step(down_w[...], grad, down_m[...], down_v[...], down_rate, outs)
    for j in range(4):
        grad_s[:, j, :] = attn_r[j].astype(f32)
    shape = grad_s.shape
    rate = jnp.where(
        lax.broadcasted_iota(jnp.int32, shape, 1) == 3, learn_rate * out_rate, learn_rate
    )
    grad = grad_s[...] * clip.reshape(1, 1, 1)
    adam_step(attn_w[...], grad, attn_m[...], attn_v[...], rate, (attn_g, attn_n, attn_f, attn_s))
    outs = (norm_g, norm_n, norm_f, norm_s)
    adam_step(norm_w[...], norm_raw * clip, norm_m[...], norm_v[...], gain_rate, outs)

    @pl.when(pl.program_id(0) == 1)
    def _():
        inward.wait()
        outward.start()

    @pl.when(pl.program_id(0) == steps - 1)
    def _():
        outward.wait()


def update_call(input_grad, raw, norm_raw, square, weights, firsts, seconds, length):
    steps = 6
    thin, thick = weights[0].shape[0], weights[2].shape[0]
    a, u, d = thin // steps, thin // steps, thick // steps
    attn = pl.BlockSpec((a, 4, D), lambda t: (t, 0, 0))
    up = pl.BlockSpec((u, FF), lambda t: (t, 0))
    down = pl.BlockSpec((d, D), lambda t: (t, 0))
    whole = lambda rows, cols: pl.BlockSpec((rows, cols), lambda t: (0, 0))
    norm = whole(4, D)
    kinds = [attn, up, down, norm]
    shapes = [jax.ShapeDtypeStruct(w.shape, f32) for w in weights]
    one = jax.ShapeDtypeStruct((1, 1), f32)
    hbm = pl.BlockSpec(memory_space=pl.ANY)
    return pl.pallas_call(
        functools.partial(update_kernel, math.sqrt(length // 8), steps),
        grid=(steps,),
        in_specs=[hbm, pl.BlockSpec((4, a, D), lambda t: (0, t, 0)), up, whole(D, thick)]
        + [whole(8, D), whole(8, 128)]
        + kinds * 3,
        out_specs=[hbm] + kinds + [whole(1, 1)] + kinds * 3,
        out_shape=[jax.ShapeDtypeStruct(input_grad.shape, f32)] + shapes + [one] + shapes * 3,
        scratch_shapes=[
            pltpu.VMEM((a, 4, D), f32), pltpu.VMEM((thick, D), f32),
            pltpu.VMEM(input_grad.shape, f32), pltpu.SemaphoreType.DMA((2,)),
        ],
        compiler_params=pltpu.CompilerParams(vmem_limit_bytes=VMEM_BYTES),
        name="adamw_update",
    )(input_grad, *raw, norm_raw, square, *weights, *firsts, *seconds)


def prefix(part, axis, combine, identity):
    place = lax.axis_index(axis)
    gathered = jax.tree.map(lambda a: lax.all_gather(a, axis), part)
    state = jax.tree.map(lambda a, e: jnp.zeros_like(a) + jnp.asarray(e, a.dtype), part, identity)

    def prefix_one(step, state):
        return combine(
            state, jax.tree.map(lambda a: lax.dynamic_index_in_dim(a, step, 0, False), gathered)
        )

    return lax.fori_loop(0, place, prefix_one, state)


def carried_in(shard, axis, join, neutral):
    count = lax.axis_size(axis)
    place = lax.axis_index(axis)
    ahead = count - 1 - place
    gathered = jax.tree.map(
        lambda a, kind: lax.all_gather(a.astype(kind), axis),
        shard,
        jax.tree.map(lambda a: jnp.bfloat16 if a.dtype == jnp.float32 else a.dtype, shard),
    )
    state = jax.tree.map(lambda a, e: jnp.zeros_like(a) + jnp.asarray(e, a.dtype), shard, neutral)

    def carried_one(step, state):
        source = count - 1 - step
        return join(
            state,
            jax.tree.map(
                lambda a, own: lax.dynamic_index_in_dim(a, source, 0, False).astype(own.dtype),
                gathered,
                shard,
            ),
        )

    return lax.fori_loop(0, ahead, carried_one, state)


def add_states(earlier, later):
    return jax.tree.map(jnp.add, earlier, later)


def layer_norm(values, gain_row, bias_row):
    centered = values - jnp.mean(values, axis=-1, keepdims=True)
    spread = jnp.mean(centered * centered, axis=-1, keepdims=True)
    return centered * lax.rsqrt(spread + norm_eps) * gain_row + bias_row


def piece_scores(query_cos, query_sin, key_cos, key_sin, causal):
    scores = jnp.einsum("ihe,jhe->hij", query_cos, key_cos, preferred_element_type=jnp.float32)
    scores = scores + jnp.einsum(
        "ihe,jhe->hij", query_sin, key_sin, preferred_element_type=jnp.float32
    )
    return jnp.where(causal[None], scores, 0.0)


def adamw(weight, gradient, first_moment, second, step_rate):
    first_new = beta_one * first_moment + (1.0 - beta_one) * gradient
    second_new = beta_two * second + (1.0 - beta_two) * gradient * gradient
    first_hat = first_new / (1.0 - beta_one**STEP)
    second_hat = second_new / (1.0 - beta_two**STEP)
    weight_new = weight - step_rate * (
        first_hat / (jnp.sqrt(second_hat) + epsilon) + weight_decay * weight
    )
    return (weight_new, first_new, second_new)


def plain_shards(
    layer_input,
    cotangent,
    attn_master,
    up_master,
    down_master,
    norm_params,
    attn_first,
    up_first,
    down_first,
    norm_first,
    attn_second,
    up_second,
    down_second,
    norm_second,
):
    groups, piece_rows, model_width = layer_input.shape
    head_count = model_width // HEAD
    length = piece_rows * lax.axis_size("seq")
    rows_all = groups * piece_rows
    attn_full, up_full, down_full = (
        lax.all_gather(attn_master.astype(jnp.bfloat16), "dp", axis=0, tiled=True),
        lax.all_gather(up_master.astype(jnp.bfloat16), "dp", axis=0, tiled=True),
        lax.all_gather(down_master.astype(jnp.bfloat16), "dp", axis=0, tiled=True),
    )
    project_in = attn_full[:, :3, :].reshape(model_width, 3 * model_width)
    out_weight = attn_full[:, 3, :]
    tokens = layer_input.reshape(rows_all, model_width)
    projected = jnp.dot(tokens, project_in, preferred_element_type=jnp.float32)
    query_pre = projected[:, :model_width]
    key_pre = projected[:, model_width : 2 * model_width]
    value_pre = projected[:, 2 * model_width :]
    position = (lax.axis_index("seq") * piece_rows + jnp.arange(piece_rows)).astype(jnp.float32)
    phase_angle = math.pi / 2 * position / length
    cosine_weight = jnp.tile(jnp.cos(phase_angle), groups)[:, None]
    sine_weight = jnp.tile(jnp.sin(phase_angle), groups)[:, None]
    query_feat = jax.nn.softplus(query_pre)
    key_feat = jax.nn.softplus(key_pre)
    shape_four = (groups, piece_rows, head_count, HEAD)
    query_cos = (query_feat * cosine_weight).astype(jnp.bfloat16).reshape(shape_four)
    query_sin = (query_feat * sine_weight).astype(jnp.bfloat16).reshape(shape_four)
    key_cos = (key_feat * cosine_weight).astype(jnp.bfloat16).reshape(shape_four)
    key_sin = (key_feat * sine_weight).astype(jnp.bfloat16).reshape(shape_four)
    values = value_pre.astype(jnp.bfloat16).reshape(shape_four)
    local_state = (
        jnp.stack(
            [
                jnp.einsum("gjhe,gjhf->ghef", key_cos, values, preferred_element_type=jnp.float32),
                jnp.einsum("gjhe,gjhf->ghef", key_sin, values, preferred_element_type=jnp.float32),
            ],
            axis=1,
        ),
        jnp.stack(
            [
                jnp.sum(key_cos, axis=1, dtype=jnp.float32),
                jnp.sum(key_sin, axis=1, dtype=jnp.float32),
            ],
            axis=1,
        ),
    )
    identity = jax.tree.map(jnp.zeros_like, local_state)
    prior_state, prior_total = prefix(
        (local_state[0], local_state[1]), "seq", add_states, (identity[0], identity[1])
    )
    causal = jnp.arange(piece_rows)[:, None] >= jnp.arange(piece_rows)[None, :]
    attended_list = []
    denominator_list = []
    for group_index in range(groups):
        scores = piece_scores(
            query_cos[group_index],
            query_sin[group_index],
            key_cos[group_index],
            key_sin[group_index],
            causal,
        )
        qcos_wide = query_cos[group_index].astype(jnp.float32)
        qsin_wide = query_sin[group_index].astype(jnp.float32)
        numerator = jnp.einsum(
            "hij,jhe->ihe",
            scores.astype(jnp.bfloat16),
            values[group_index],
            preferred_element_type=jnp.float32,
        )
        numerator = numerator + jnp.einsum(
            "ihe,hef->ihf", qcos_wide, prior_state[group_index, 0], precision=highest
        )
        numerator = numerator + jnp.einsum(
            "ihe,hef->ihf", qsin_wide, prior_state[group_index, 1], precision=highest
        )
        denominator = jnp.sum(scores, axis=-1).T
        denominator = denominator + jnp.einsum(
            "ihe,he->ih", qcos_wide, prior_total[group_index, 0], precision=highest
        )
        denominator = denominator + jnp.einsum(
            "ihe,he->ih", qsin_wide, prior_total[group_index, 1], precision=highest
        )
        attended_list.append(numerator / denominator[:, :, None])
        denominator_list.append(denominator)
    attended = jnp.stack(attended_list)
    attended_low = attended.reshape(rows_all, model_width).astype(jnp.bfloat16)
    branch_one = jnp.dot(attended_low, out_weight, preferred_element_type=jnp.float32)
    residual_one = tokens.astype(jnp.float32) + branch_one
    first_norm, norm_one_back = jax.vjp(layer_norm, residual_one, norm_params[0], norm_params[1])
    first_low = first_norm.astype(jnp.bfloat16)
    hidden = jnp.dot(first_low, up_full, preferred_element_type=jnp.float32)
    activated, gelu_back = jax.vjp(jax.nn.gelu, hidden)
    activated_low = activated.astype(jnp.bfloat16)
    branch_two = jnp.dot(activated_low, down_full, preferred_element_type=jnp.float32)
    result, norm_two_back = jax.vjp(
        layer_norm, first_norm + branch_two, norm_params[2], norm_params[3]
    )
    layer_output = result.astype(jnp.bfloat16).reshape(groups, piece_rows, model_width)
    grad_residual_two, grad_gain_two, grad_bias_two = norm_two_back(
        cotangent.reshape(rows_all, model_width).astype(jnp.float32)
    )
    grad_branch_two = grad_residual_two.astype(jnp.bfloat16)
    grad_down = jnp.einsum(
        "nf,nd->fd", activated_low, grad_branch_two, preferred_element_type=jnp.float32
    )
    grad_activated = jnp.einsum(
        "nd,fd->nf", grad_branch_two, down_full, preferred_element_type=jnp.float32
    )
    grad_hidden = gelu_back(grad_activated)[0].astype(jnp.bfloat16)
    grad_up = jnp.einsum("nd,nf->df", first_low, grad_hidden, preferred_element_type=jnp.float32)
    grad_first = grad_residual_two + jnp.einsum(
        "nf,df->nd", grad_hidden, up_full, preferred_element_type=jnp.float32
    )
    grad_residual_one, grad_gain_one, grad_bias_one = norm_one_back(grad_first)
    grad_branch_one = grad_residual_one.astype(jnp.bfloat16)
    grad_out_weight = jnp.einsum(
        "nd,ne->de", attended_low, grad_branch_one, preferred_element_type=jnp.float32
    )
    grad_attended = jnp.einsum(
        "ne,de->nd", grad_branch_one, out_weight, preferred_element_type=jnp.float32
    ).reshape(shape_four)
    grad_qcos_list = []
    grad_qsin_list = []
    grad_kcos_list = []
    grad_ksin_list = []
    grad_values_list = []
    prior_grad_state = []
    prior_grad_total = []
    for group_index in range(groups):
        denominator = denominator_list[group_index]
        grad_numerator = (grad_attended[group_index] / denominator[:, :, None]).astype(jnp.bfloat16)
        grad_denominator = (
            -jnp.sum(grad_attended[group_index] * attended[group_index], axis=-1) / denominator
        )
        scores = piece_scores(
            query_cos[group_index],
            query_sin[group_index],
            key_cos[group_index],
            key_sin[group_index],
            causal,
        )
        grad_scores = (
            jnp.einsum(
                "ihe,jhe->hij",
                grad_numerator,
                values[group_index],
                preferred_element_type=jnp.float32,
            )
            + grad_denominator.T[:, :, None]
        )
        grad_scores = jnp.where(causal[None], grad_scores, 0.0).astype(jnp.bfloat16)
        grad_numerator_wide = grad_numerator.astype(jnp.float32)
        grad_qcos = jnp.einsum(
            "hij,jhe->ihe", grad_scores, key_cos[group_index], preferred_element_type=jnp.float32
        )
        grad_qcos = grad_qcos + jnp.einsum(
            "ihf,hef->ihe", grad_numerator_wide, prior_state[group_index, 0], precision=highest
        )
        grad_qcos = grad_qcos + grad_denominator[:, :, None] * prior_total[group_index, 0][None]
        grad_qsin = jnp.einsum(
            "hij,jhe->ihe", grad_scores, key_sin[group_index], preferred_element_type=jnp.float32
        )
        grad_qsin = grad_qsin + jnp.einsum(
            "ihf,hef->ihe", grad_numerator_wide, prior_state[group_index, 1], precision=highest
        )
        grad_qsin = grad_qsin + grad_denominator[:, :, None] * prior_total[group_index, 1][None]
        grad_qcos_list.append(grad_qcos)
        grad_qsin_list.append(grad_qsin)
        grad_kcos_list.append(
            jnp.einsum(
                "hij,ihe->jhe",
                grad_scores,
                query_cos[group_index],
                preferred_element_type=jnp.float32,
            )
        )
        grad_ksin_list.append(
            jnp.einsum(
                "hij,ihe->jhe",
                grad_scores,
                query_sin[group_index],
                preferred_element_type=jnp.float32,
            )
        )
        grad_values_list.append(
            jnp.einsum(
                "hij,ihe->jhe",
                scores.astype(jnp.bfloat16),
                grad_numerator,
                preferred_element_type=jnp.float32,
            )
        )
        prior_grad_state.append(
            jnp.stack(
                [
                    jnp.einsum(
                        "ihe,ihf->hef",
                        query_cos[group_index],
                        grad_numerator,
                        preferred_element_type=jnp.float32,
                    ),
                    jnp.einsum(
                        "ihe,ihf->hef",
                        query_sin[group_index],
                        grad_numerator,
                        preferred_element_type=jnp.float32,
                    ),
                ]
            )
        )
        prior_grad_total.append(
            jnp.stack(
                [
                    jnp.einsum(
                        "ihe,ih->he",
                        query_cos[group_index].astype(jnp.float32),
                        grad_denominator,
                        precision=highest,
                    ),
                    jnp.einsum(
                        "ihe,ih->he",
                        query_sin[group_index].astype(jnp.float32),
                        grad_denominator,
                        precision=highest,
                    ),
                ]
            )
        )
    later_state, later_total = carried_in(
        (jnp.stack(prior_grad_state), jnp.stack(prior_grad_total)),
        "seq",
        add_states,
        (identity[0], identity[1]),
    )
    values_wide = values.astype(jnp.float32)
    kcos_wide = key_cos.astype(jnp.float32)
    ksin_wide = key_sin.astype(jnp.float32)
    grad_kcos = (
        jnp.stack(grad_kcos_list)
        + jnp.einsum("gjhf,ghef->gjhe", values_wide, later_state[:, 0], precision=highest)
        + later_total[:, 0][:, None]
    )
    grad_ksin = (
        jnp.stack(grad_ksin_list)
        + jnp.einsum("gjhf,ghef->gjhe", values_wide, later_state[:, 1], precision=highest)
        + later_total[:, 1][:, None]
    )
    grad_values = jnp.stack(grad_values_list)
    grad_values = grad_values + jnp.einsum(
        "gjhe,ghef->gjhf", kcos_wide, later_state[:, 0], precision=highest
    )
    grad_values = grad_values + jnp.einsum(
        "gjhe,ghef->gjhf", ksin_wide, later_state[:, 1], precision=highest
    )
    grad_query = (
        jnp.stack(grad_qcos_list).reshape(rows_all, model_width) * cosine_weight
        + jnp.stack(grad_qsin_list).reshape(rows_all, model_width) * sine_weight
    )
    grad_keys = (
        grad_kcos.reshape(rows_all, model_width) * cosine_weight
        + grad_ksin.reshape(rows_all, model_width) * sine_weight
    )
    grad_projected = jnp.concatenate(
        [
            (grad_query * jax.nn.sigmoid(query_pre)).astype(jnp.bfloat16),
            (grad_keys * jax.nn.sigmoid(key_pre)).astype(jnp.bfloat16),
            grad_values.reshape(rows_all, model_width).astype(jnp.bfloat16),
        ],
        axis=1,
    )
    input_grad = grad_residual_one + jnp.einsum(
        "nk,dk->nd", grad_projected, project_in, preferred_element_type=jnp.float32
    )
    input_grad = input_grad.reshape(groups, piece_rows, model_width)
    grad_in = jnp.einsum("nd,nk->dk", tokens, grad_projected, preferred_element_type=jnp.float32)
    grad_attn = jnp.concatenate(
        [grad_in.reshape(model_width, 3, model_width), grad_out_weight[:, None, :]], axis=1
    )
    norm_grad_local = jnp.stack([grad_gain_one, grad_bias_one, grad_gain_two, grad_bias_two])
    norm_grad_raw = lax.psum(norm_grad_local, ("dp", "seq"))
    row_blocks = (
        lax.psum_scatter(
            grad_attn.astype(jnp.bfloat16), "dp", scatter_dimension=0, tiled=True
        ).astype(jnp.float32),
        lax.psum_scatter(
            grad_up.astype(jnp.bfloat16), "dp", scatter_dimension=0, tiled=True
        ).astype(jnp.float32),
        lax.psum_scatter(
            grad_down.astype(jnp.bfloat16), "dp", scatter_dimension=0, tiled=True
        ).astype(jnp.float32),
    )
    shard_attn, shard_up, shard_down = (
        lax.psum(row_blocks[0].astype(jnp.bfloat16), "seq").astype(jnp.float32),
        lax.psum(row_blocks[1].astype(jnp.bfloat16), "seq").astype(jnp.float32),
        lax.psum(row_blocks[2].astype(jnp.bfloat16), "seq").astype(jnp.float32),
    )
    local_square = (
        jnp.sum(shard_attn * shard_attn)
        + jnp.sum(shard_up * shard_up)
        + jnp.sum(shard_down * shard_down)
    )
    square = lax.psum(local_square, "dp") + jnp.sum(norm_grad_raw * norm_grad_raw)
    grad_norm = jnp.sqrt(square)
    clip_scale = clip_limit / jnp.maximum(grad_norm, clip_limit)
    attn_grad = shard_attn * clip_scale
    up_grad = shard_up * clip_scale
    down_grad = shard_down * clip_scale
    norm_grad = norm_grad_raw * clip_scale
    attn_rate = (
        learn_rate * jnp.array([1.0, 1.0, 1.0, math.sqrt(length // 8)], jnp.float32)[None, :, None]
    )
    attn_new, attn_first_new, attn_second_new = adamw(
        attn_master, attn_grad, attn_first, attn_second, attn_rate
    )
    up_new, up_first_new, up_second_new = adamw(up_master, up_grad, up_first, up_second, learn_rate)
    down_new, down_first_new, down_second_new = adamw(
        down_master, down_grad, down_first, down_second, learn_rate * math.sqrt(D / FF)
    )
    norm_new, norm_first_new, norm_second_new = adamw(
        norm_params, norm_grad, norm_first, norm_second, gain_rate
    )
    return (
        layer_output,
        input_grad,
        attn_grad,
        up_grad,
        down_grad,
        norm_grad,
        grad_norm,
        attn_new,
        up_new,
        down_new,
        norm_new,
        attn_first_new,
        up_first_new,
        down_first_new,
        norm_first_new,
        attn_second_new,
        up_second_new,
        down_second_new,
        norm_second_new,
    )


def fused_shards(
    layer_input, cotangent, attn_master, up_master, down_master, norm_params,
    attn_first, up_first, down_first, norm_first,
    attn_second, up_second, down_second, norm_second,
):
    groups, piece_rows, model_width = layer_input.shape
    seq_count = lax.axis_size("seq")
    rows = groups * piece_rows
    weights = (attn_master, up_master, down_master, norm_params)
    saved = forward_call(
        layer_input.reshape(rows, model_width), *weights, seq_count,
    )
    saved |= second_norm(saved, cotangent.reshape(rows, model_width), norm_params)
    input_grad, attn, up, down, norm_raw, square = backward_call(saved, norm_params, seq_count)
    raw = (attn.reshape(4, -1, D), up.reshape(-1, FF), down.reshape(D, -1))
    input_grad, *outs = update_call(
        input_grad, raw, norm_raw, square, weights,
        (attn_first, up_first, down_first, norm_first),
        (attn_second, up_second, down_second, norm_second), piece_rows * seq_count,
    )
    return (
        saved["out"].reshape(layer_input.shape), input_grad.reshape(layer_input.shape),
        *outs[:4], outs[4].reshape(()), *outs[5:],
    )


def shards(*args):
    groups, piece_rows, model_width = args[0].shape
    planes = lax.axis_size("dp") // 2
    if piece_rows == PIECE and planes == PLANES and lax.axis_size("seq") == 4:
        return fused_shards(*args)
    return plain_shards(*args)


def solution(mesh):
    in_specs = (
        P("dp", "seq", None),
        P("dp", "seq", None),
        P("dp", None, None),
        P("dp", None),
        P("dp", None),
        P(),
        P("dp", None, None),
        P("dp", None),
        P("dp", None),
        P(),
        P("dp", None, None),
        P("dp", None),
        P("dp", None),
        P(),
    )
    out_specs = (
        P("dp", "seq", None),
        P("dp", "seq", None),
        P("dp", None, None),
        P("dp", None),
        P("dp", None),
        P(),
        P(),
        P("dp", None, None),
        P("dp", None),
        P("dp", None),
        P(),
        P("dp", None, None),
        P("dp", None),
        P("dp", None),
        P(),
        P("dp", None, None),
        P("dp", None),
        P("dp", None),
        P(),
    )
    return jax.shard_map(shards, mesh=mesh, in_specs=in_specs, out_specs=out_specs, check_vma=False)
```

```python
import functools
import math

import jax
import jax.numpy as jnp
import numpy as np
from jax import lax
from jax.experimental import pallas as pl
from jax.experimental.pallas import tpu as pltpu
from jax.sharding import PartitionSpec as P

D = 768
HEAD = 64
FF = 3072
STEP = 5


highest = lax.Precision.HIGHEST
beta_one = 0.5
beta_two = 0.5
learn_rate = 0.02
gain_rate = 0.2
epsilon = 1e-08
weight_decay = 0.01
norm_eps = 1e-05
clip_limit = 1.0


MESH = pl.DeviceIdType.MESH
f32, bf16 = jnp.float32, jnp.bfloat16
PIECE = 512
PAIR = 2 * HEAD
PLANES = 4
VMEM_BYTES = 63 * 1024 * 1024


def dot(left, right):
    return jnp.dot(left, right, preferred_element_type=f32)


def dot_nt(left, right):
    return lax.dot_general(left, right, (((1,), (1,)), ((), ())), preferred_element_type=f32)


def dot_tn(left, right):
    return lax.dot_general(left, right, (((0,), (0,)), ((), ())), preferred_element_type=f32)


def first_half(shape):
    return lax.broadcasted_iota(jnp.int32, shape, 1) < HEAD


def top_half(shape):
    return lax.broadcasted_iota(jnp.int32, shape, 0) < HEAD


def own_head(value, head):
    mask = first_half(value.shape)
    zero = jnp.zeros_like(value)
    return jnp.where(mask, value, zero) if head == 0 else jnp.where(mask, zero, value)


def two_heads(first, second):
    return jnp.where(first_half(first.shape), first, second)


def pair_mask(shape):
    return (lax.broadcasted_iota(jnp.int32, shape, 1) & (PAIR - 1)) < HEAD


def stack_heads(value):
    mask, zero = pair_mask(value.shape), jnp.zeros_like(value)
    return jnp.concatenate([jnp.where(mask, value, zero), jnp.where(mask, zero, value)], axis=0)


def join_heads(stacked):
    first, second = stacked[: stacked.shape[0] // 2], stacked[stacked.shape[0] // 2 :]
    return jnp.where(pair_mask(first.shape), first, second)


def side_by_side(wide):
    half = wide.shape[1] // 2
    return jnp.concatenate([wide[:, :half], wide[:, half:]], axis=0)


def fill_triangles(tri_s):
    half = tri_s.shape[1]
    row = lax.broadcasted_iota(jnp.int32, (half, half), 0)
    col = lax.broadcasted_iota(jnp.int32, (half, half), 1)
    tri_s[0:half] = (row >= col).astype(f32).astype(bf16)
    tri_s[half:] = (row <= col).astype(f32).astype(bf16)


def causal_product(own, other, right, tri_s):
    half = PIECE // 2
    tri = jnp.concatenate([tri_s[0:half], tri_s[0:half]], axis=0)
    tops, lows = stack_heads(own[0:half]), stack_heads(own[half:])
    first = dot_nt(jnp.concatenate([tops, lows], axis=0), other[0:half]).astype(bf16)
    near = dot_nt(lows, other[half:]).astype(bf16) * tri
    first = jnp.concatenate([first[:PIECE] * tri, first[PIECE:]], axis=0)
    out = dot(first, right[0:half])
    low = out[PIECE:] + dot(near, right[half:])
    return jnp.concatenate([join_heads(out[:PIECE]), join_heads(low)], axis=0)


def causal_transposed(own, other, right, tri_s):
    half = PIECE // 2
    tri = jnp.concatenate([tri_s[half:], tri_s[half:]], axis=1)
    top = dot_nt(other[0:half], stack_heads(own[0:half])).astype(bf16) * tri
    low = dot_nt(other, stack_heads(own[half:])).astype(bf16)
    low = jnp.concatenate([low[0:half], low[half:] * tri], axis=0)
    out = dot(side_by_side(low), right[half:])
    more = dot(side_by_side(top), right[0:half])
    first = jnp.concatenate([out[0:half] + more[0:half], out[half:PIECE]], axis=0)
    second = jnp.concatenate([out[PIECE : PIECE + half] + more[half:], out[PIECE + half :]], axis=0)
    return jnp.where(pair_mask(first.shape), first, second)


def with_ones(value):
    return jnp.concatenate([value, jnp.ones_like(value)], axis=1)


def turned(value, trig):
    wide = value.astype(f32)
    cos, sin = trig[:, :PAIR], trig[:, PAIR:]
    return jnp.concatenate([(wide * cos).astype(bf16), (wide * sin).astype(bf16)], axis=1)


def squeeze_state(state, totals):
    cos = two_heads(state[0:HEAD], state[HEAD : 2 * HEAD])
    sin = two_heads(state[2 * HEAD : 3 * HEAD], state[3 * HEAD :])
    row = lax.broadcasted_iota(jnp.int32, (16, PAIR), 0)
    sums = jnp.where(row == 0, totals[:, :PAIR], totals[:, PAIR:])
    return jnp.concatenate([cos, sin, sums], axis=0)


def spread_state(packed):
    cos, sin = packed[0:HEAD], packed[HEAD:PAIR]
    state = jnp.concatenate(
        [own_head(cos, 0), own_head(cos, 1), own_head(sin, 0), own_head(sin, 1)], axis=0
    )
    row = lax.broadcasted_iota(jnp.int32, (16, PAIR), 0)
    sums = packed[PAIR:]
    ones = jnp.ones((16, PAIR), bf16)
    blocks = []
    for kind in range(2):
        column = dot_tn(jnp.where(row == kind, sums, jnp.zeros_like(sums)), ones).astype(bf16)
        blocks += [own_head(column[0:HEAD], 0), own_head(column[HEAD:], 1)]
    return jnp.concatenate([state, jnp.concatenate(blocks, axis=0)], axis=1)


def normed(value):
    centered = value - jnp.mean(value, axis=-1, keepdims=True)
    rstd = lax.rsqrt(jnp.mean(centered * centered, axis=-1, keepdims=True) + norm_eps)
    return centered * rstd, rstd


def norm_back(grad, unit, rstd):
    mean = jnp.mean(grad, axis=-1, keepdims=True)
    along = jnp.mean(grad * unit, axis=-1, keepdims=True)
    return rstd * (grad - mean - unit * along)


class Place:
    def __init__(self):
        dp, seq = lax.axis_index("dp"), lax.axis_index("seq")
        self.z, self.y, self.x, self.c = dp // 2, dp % 2, seq // 2, seq % 2
        self.shard = dp

    def device(self, z=None, y=None, x=None, c=None):
        z = self.z if z is None else z
        y = self.y if y is None else y
        x = self.x if x is None else x
        c = self.c if c is None else c
        return {"dp": z * 2 + y, "seq": x * 2 + c}

    def plane(self, shift):
        return lax.rem(self.z + shift + PLANES, PLANES)

    def across_y(self):
        return self.device(y=1 - self.y)

    def across_x(self):
        return self.device(x=1 - self.x)

    def across_c(self):
        return self.device(c=1 - self.c)

    def neighbours(self):
        planes = [self.device(z=self.plane(step)) for step in range(1, PLANES)]
        return planes + [self.across_y(), self.across_x(), self.across_c()]

    def corners(self):
        y, x, c = 1 - self.y, 1 - self.x, 1 - self.c
        return [
            self.device(x=x, c=c), self.device(y=y, c=c),
            self.device(y=y, x=x), self.device(y=y, x=x, c=c),
        ]

    def in_plane(self):
        return (self.y * 2 + self.x) * 2 + self.c


def greet(place, corners=False):
    barrier = pltpu.get_barrier_semaphore()
    peers = place.neighbours() + (place.corners() if corners else [])
    for peer in peers:
        pl.semaphore_signal(barrier, inc=1, device_id=peer, device_id_type=MESH)
    pl.semaphore_wait(barrier, len(peers))


class Engine:
    RATES = {"x": 30e3, "y": 30e3, "z": 23e3, "c": 200e3}

    def __init__(self, pace=1.0):
        self.now, self.free, self.pace = 0.0, dict.fromkeys(self.RATES, 0.0), pace
        self.eta, self.tasks, self.done = {}, [], set()

    def sent(self, key, link, size):
        self.now += 0.04
        start = max(self.now, self.free[link])
        self.free[link] = start + size / (self.pace * self.RATES[link])
        self.eta[key] = self.free[link] + 1.5

    def add(self, needs, act, mark=None, cost=0.05):
        self.tasks.append((needs, act, mark, cost))

    def due(self, task):
        return max((self.eta.get(key, math.inf) for key in task[0]), default=0.0)

    def run(self, task):
        self.tasks.remove(task)
        self.now = max(self.now, self.due(task)) + task[3]
        task[1]()
        if task[2] is not None:
            self.done.add(task[2])

    def tick(self, cost):
        self.now += cost
        while self.tasks:
            task = min(self.tasks, key=self.due)
            if self.due(task) > self.now:
                return
            self.run(task)

    def until(self, *marks):
        while not self.done.issuperset(marks):
            self.run(min(self.tasks, key=self.due))

    def rest(self):
        while self.tasks:
            self.run(min(self.tasks, key=self.due))


def two_parts(ref):
    rows = ref.shape[-2]
    cut = rows // 32 * 16 if rows % 32 == 0 else (rows // 32 + 1) * 16
    lead = (slice(None),) * (len(ref.shape) - 2)
    return [ref.at[lead + (slice(a, b), slice(None))] for a, b in ((0, cut), (cut, rows))]


class Gather:
    def __init__(self, place, engine, chunks, send, recv, ready):
        self.place, self.engine, self.chunks = place, engine, chunks
        self.send, self.recv, self.sent, self.ready = send, recv, [], ready
        for k in range(len(chunks)):
            self.plan(k)

    def piece(self, k, z, y, x, c):
        ref, stride, base, height, column, width = self.chunks[k]
        row = (z * 2 + y) * stride + base + c * height
        return ref.at[
            pl.ds(pl.multiple_of(row, 16), height),
            pl.ds(pl.multiple_of(column + x * width, 128), width),
        ]

    def copy(self, k, index, ref, device):
        return pltpu.make_async_remote_copy(
            src_ref=ref,
            dst_ref=ref,
            send_sem=self.send.at[k, index],
            recv_sem=self.recv.at[k, index],
            device_id=device,
            device_id_type=MESH,
        )

    def push(self, k, index, ref, device, link):
        for part in [ref] if link == "c" else two_parts(ref):
            self.copy(k, index, part, device).start()
        self.sent.append(self.copy(k, index, ref, device))
        self.engine.sent((k, index), link, 2 * self.chunks[k][3] * self.chunks[k][5])

    def pull(self, k, index, ref):
        self.copy(k, index, ref, self.place.across_c()).wait_recv()

    def twin(self, k, index, ref):
        self.push(k, 14 + index, ref, self.place.across_c(), "c")

    def begin(self, k):
        p = self.place
        self.ready(k)
        own = self.piece(k, p.z, p.y, p.x, p.c)
        for step in (1, 3, 2):
            self.push(k, step - 1, own, p.device(z=p.plane(step)), "z")
        self.push(k, 3, own, p.across_y(), "y")
        other = self.piece(k, p.z, p.y, 1 - p.x, p.c)
        self.push(k, 10, other, p.across_y(), "y")
        self.push(k, 7, other, p.device(z=p.plane(1)), "z")

    def from_plane(self, k, step):
        p = self.place
        ref = self.piece(k, p.plane(-step), p.y, p.x, p.c)
        self.pull(k, step - 1, ref)
        self.push(k, 3 + step, ref, p.across_y(), "y")
        if step != 1:
            self.push(k, 6 + step, ref, p.across_x(), "x")
        self.twin(k, step - 1, ref)

    def by_y(self, k):
        return (1, 3) if k == 6 else ()

    def from_y(self, k, step):
        p = self.place
        ref = self.piece(k, p.plane(-step), 1 - p.y, p.x, p.c)
        self.pull(k, 3 + step, ref)
        if step and step not in self.by_y(k):
            self.push(k, 10 + step, ref, p.across_x(), "x")
        self.twin(k, 3 + step, ref)

    def from_x(self, k, step):
        p = self.place
        ref = self.piece(k, p.plane(-step), p.y, 1 - p.x, p.c)
        self.pull(k, 6 + step, ref)
        if step in self.by_y(k):
            self.push(k, 10 + step, ref, p.across_y(), "y")
        self.twin(k, 6 + step, ref)

    def corner(self, k, step):
        p = self.place
        ref = self.piece(k, p.plane(-step), 1 - p.y, 1 - p.x, p.c)
        self.pull(k, 10 + step, ref)
        self.twin(k, 10 + step, ref)

    def finish(self, k):
        p = self.place
        far = 1 - p.c
        for step in range(PLANES):
            z = p.plane(-step)
            if step:
                self.pull(k, 14 + step - 1, self.piece(k, z, p.y, p.x, far))
                self.pull(k, 20 + step, self.piece(k, z, p.y, 1 - p.x, far))
            self.pull(k, 17 + step, self.piece(k, z, 1 - p.y, p.x, far))
            self.pull(k, 24 + step, self.piece(k, z, 1 - p.y, 1 - p.x, far))

    def plan(self, k):
        before = [(k - 2, at) for at in range(3)] if k > 1 else []
        add = self.engine.add
        add(before, functools.partial(self.begin, k))
        for step in (1, 3, 2):
            add([(k, step - 1)], functools.partial(self.from_plane, k, step))
            add([(k, 6 + step)], functools.partial(self.from_x, k, step))
        for step in (0, 1, 3, 2):
            add([(k, 3 + step)], functools.partial(self.from_y, k, step))
            add([(k, 10 + step)], functools.partial(self.corner, k, step))
        add([(k, 14 + at) for at in range(14)], functools.partial(self.finish, k), k, 0.3)

    def drain(self):
        for copy in self.sent:
            copy.wait_send()


def ds(start, size, unit):
    return pl.ds(pl.multiple_of(start, unit), size)


def turn_over(source, target):
    for at in range(0, source.shape[0], 256):
        target[:, at : at + 256] = source[at : at + 256, :].T


def block_of(b):
    return ds((b // 6) * PIECE, PIECE, PIECE), ds(lax.rem(b, 6) * PAIR, PAIR, PAIR)


def forward_kernel(
    x_h, cot_h, attn_h, up_h, down_h, norm_h, trig_h,
    wqkv_o, wo_o, wup_o, wdn_o, q_o, k_o, v_o, att_o, rden_o, xhat_o, rstd_o, xt_o, att_t_o,
    low_t_o, act_o, slope_o, gb_o, gb_t_o, gr2_o, out_o, state_o, sums_o,
    wqkv, wo, wup, wdn, attn_st, up_st, down_st, x_s, cot_s, norm_s, trig_s, tri_s,
    q_s, k_s, v_s, num_s, den_s, att_s, xhat_s, rstd_s, low_s, act_s, slope_a, slope_b, hid_a, hid_b, out_s,
    x_t_s, att_t_s, low_t_s, sums_s, st_own, st_twin, st_chip, st_prior,
    load_sem, store_sem, tile_sem, g_send, g_recv, st_send, st_recv,
):
    place = Place()
    shard, x, c = place.shard, place.x, place.c
    groups = x_s.shape[0] // PIECE
    blocks = groups * 6
    loads = []
    for at, (src, dst) in enumerate(
        [
            (attn_h, attn_st), (up_h, up_st), (down_h, down_st), (x_h, x_s), (norm_h, norm_s),
            (trig_h.at[ds((x * 2 + c) * PIECE, PIECE, PIECE), :], trig_s), (cot_h, cot_s),
        ]
    ):
        copy = pltpu.make_async_copy(src, dst, load_sem.at[at])
        copy.start()
        loads.append(copy)
    stores = []

    def store(src, dst):
        copy = pltpu.make_async_copy(src, dst, store_sem.at[len(stores)])
        copy.start()
        stores.append(copy)

    thin, thick = attn_st.shape[0], down_st.shape[0]
    chunks = [
        (wqkv, thin, 0, thin // 2, D, D),
        (wqkv, thin, 0, thin // 2, 0, D // 2),
        (wo, thin, 0, thin // 2, 0, D // 2),
        (wup, thin, 0, thin // 2, 0, FF // 4),
        (wup, thin, 0, thin // 2, FF // 2, FF // 4),
        (wdn, thick, 0, thick // 2, 0, D // 3),
        (wdn, thick, 0, thick // 2, 2 * D // 3, D // 6),
    ]
    def ready(k):
        narrow = ds(shard * thin, thin, 32)
        if k == 0:
            loads[0].wait()
            for j in range(3):
                wqkv[narrow, j * D : (j + 1) * D] = attn_st[:, j, :].astype(bf16)
        elif k == 2:
            wo[narrow, :] = attn_st[:, 3, :].astype(bf16)
        elif k == 3:
            loads[1].wait()
            wup[narrow, :] = up_st[...].astype(bf16)
        elif k == 5:
            loads[2].wait()
            wdn[ds(shard * thick, thick, 128), :] = down_st[...].astype(bf16)

    engine = Engine()
    gather = Gather(place, engine, chunks, g_send, g_recv, ready)
    greet(place)
    engine.tick(0.0)
    fill_triangles(tri_s)
    for copy in loads[3:6]:
        copy.wait()
    turn_over(x_s, x_t_s)
    store(x_t_s, xt_o)
    engine.tick(3.0)
    engine.until(0)

    hidden = (hid_a, hid_b)

    def chain(products, finish, cost):
        hidden[0][...] = products[0]()
        for t in range(len(products)):
            if t + 1 < len(products):
                hidden[(t + 1) % 2][...] = products[t + 1]()
            finish(t, hidden[t % 2])
            engine.tick(cost)

    def project(parts):
        tiles = [(target, column, t, soft) for target, column, soft in parts for t in range(3)]

        def product(target, column, t, soft):
            return dot(x_s[...], wqkv[:, column + 256 * t : column + 256 * t + 256])

        def finish(at, pre):
            target, _, t, soft = tiles[at]
            pre = pre[...]
            if soft:
                pre = jnp.maximum(pre, 0.0) + jnp.log1p(jnp.exp(-jnp.abs(pre)))
            target[:, 256 * t : 256 * t + 256] = pre.astype(bf16)

        chain([functools.partial(product, *tile) for tile in tiles], finish, 0.7)

    project([(k_s, D, True), (v_s, 2 * D, False)])

    def local(b, carry):
        rows, cols = ds((b // 6) * PIECE, PIECE, PIECE), ds(lax.rem(b, 6) * PAIR, PAIR, PAIR)
        keys = turned(k_s[rows, cols], trig_s[...])
        state = dot_tn(keys, v_s[rows, cols])
        totals = dot(jnp.ones((16, PIECE), bf16), keys)
        st_own[b] = squeeze_state(state, totals).astype(bf16)
        return carry

    for part in range(0, blocks, 4):
        lax.fori_loop(part, part + 4, local, 0)
        engine.tick(1.4)
    state = StateSum(place, engine, st_send, st_recv, st_own, st_twin, st_chip, st_prior, False)
    engine.tick(0.0)
    engine.until(1)
    project([(q_s, 0, True)])
    store(wqkv, wqkv_o)
    store(q_s, q_o)
    store(k_s, k_o)
    store(v_s, v_o)

    def intra(i, carry):
        spots = [block_of(2 * i), block_of(2 * i + 1)]
        taken = [(q_s[at], k_s[at], v_s[at]) for at in spots]
        outs = [
            causal_product(
                turned(q, trig_s[...]), turned(k, trig_s[...]), with_ones(v), tri_s
            )
            for q, k, v in taken
        ]
        for at, out in zip(spots, outs):
            num_s[at] = out[:, :PAIR]
            den_s[at] = out[:, PAIR:]
        return carry

    for part in range(blocks // 2):
        lax.fori_loop(part, part + 1, intra, 0)
        engine.tick(1.6)
    engine.until("state")

    def inter(i, carry):
        spots = [block_of(2 * i), block_of(2 * i + 1)]
        states = [state.total(2 * i + at).astype(bf16) for at in range(2)]
        taken = [(q_s[at], num_s[at], den_s[at]) for at in spots]
        outs = []
        for (q, num, den), packed in zip(taken, states):
            more = dot(turned(q, trig_s[...]), spread_state(packed))
            recip = 1.0 / (den + more[:, PAIR:])
            outs.append((((num + more[:, :PAIR]) * recip).astype(bf16), recip))
        for at, (attended, recip) in zip(spots, outs):
            att_s[at] = attended
            den_s[at] = recip
        for at, packed in enumerate(states):
            st_chip[2 * i + at] = packed
        return carry

    for part in range(0, blocks // 2, 2):
        lax.fori_loop(part, part + 2, inter, 0)
        engine.tick(1.6)
    store(att_s, att_o)
    store(den_s, rden_o)
    turn_over(att_s, att_t_s)
    store(att_t_s, att_t_o)
    store(st_chip, state_o)
    engine.tick(1.0)
    engine.until(2)
    store(wo, wo_o)

    gain_one, bias_one = norm_s[0:1, :], norm_s[1:2, :]
    tile = 256

    def join(t, carry):
        cols = ds(t * tile, tile, tile)
        xhat_s[:, cols] = x_s[:, cols].astype(f32) + dot(att_s[...], wo[:, cols])
        return carry

    def join_norm(t, carry):
        rows = ds(t * tile, tile, tile)
        unit, rstd = normed(xhat_s[rows, :])
        xhat_s[rows, :] = unit
        rstd_s[rows, :] = jnp.broadcast_to(rstd, (tile, 128))
        low_s[rows, :] = (unit * gain_one + bias_one).astype(bf16)
        return carry

    for t in range(D // tile):
        lax.fori_loop(t, t + 1, join, 0)
        engine.tick(0.7)
    for part in range(x_s.shape[0] // tile):
        lax.fori_loop(part, part + 1, join_norm, 0)
        engine.tick(0.4)
    store(xhat_s, xhat_o)
    store(rstd_s, rstd_o)
    turn_over(low_s, low_t_s)
    store(low_t_s, low_t_o)
    engine.tick(1.0)
    engine.until(3)

    slopes, scale = (slope_a, slope_b), math.sqrt(2.0 / math.pi)

    def slope_copy(t):
        return pltpu.make_async_copy(
            slopes[t % 2], slope_o.at[:, 256 * t : 256 * t + 256], tile_sem.at[t % 2]
        )

    def expand(t, value):
        if t >= 2:
            slope_copy(t - 2).wait()
        value = value[...]
        squared = value * value
        curve = jnp.tanh(value * (scale + (scale * 0.044715) * squared))
        half = 0.5 + 0.5 * curve
        active = value * half
        slope = half + active * (1.0 - curve) * (scale + (3.0 * scale * 0.044715) * squared)
        act_s[:, 256 * t : 256 * t + 256] = active.astype(bf16)
        if t % 3 == 2:
            span = slice(256 * t - 512, 256 * t + 256)
            store(act_s.at[:, span], act_o.at[:, span])
        slopes[t % 2][...] = slope.astype(bf16)
        slope_copy(t).start()

    def raised(t):
        if t == 6:
            engine.until(4)
            store(wup, wup_o)
        return dot(low_s[...], wup[:, 256 * t : 256 * t + 256])

    chain([functools.partial(raised, t) for t in range(FF // 256)], expand, 1.1)
    loads[6].wait()
    sums_s[...] = jnp.zeros_like(sums_s)
    gain_two, bias_two = norm_s[2:3, :], norm_s[3:4, :]

    def contract(t):
        cols = slice(tile * t, tile * t + tile)
        num_s[:, cols] = dot(act_s[...], wdn[:, cols])
        engine.tick(2.5)

    engine.until(5)
    store(wdn.at[:, 0 : 2 * tile], wdn_o.at[:, 0 : 2 * tile])
    contract(0)
    contract(1)
    engine.until(6)
    store(wdn.at[:, 2 * tile :], wdn_o.at[:, 2 * tile :])
    contract(2)

    def contract_norm(t, carry):
        rows = ds(t * tile, tile, tile)
        unit, rstd = normed(xhat_s[rows, :] * gain_one + bias_one + num_s[rows, :])
        out_s[rows, :] = (unit * gain_two + bias_two).astype(bf16)
        cot = cot_s[rows, :].astype(f32)
        sums_s[0:1, :] += jnp.sum(cot * unit, axis=0, keepdims=True)
        sums_s[1:2, :] += jnp.sum(cot, axis=0, keepdims=True)
        grad = norm_back(cot * gain_two, unit, rstd)
        num_s[rows, :] = grad
        low_s[rows, :] = grad.astype(bf16)
        return carry

    stores[0].wait()
    for t in range(x_s.shape[0] // tile):
        span = slice(tile * t, tile * t + tile)
        lax.fori_loop(t, t + 1, contract_norm, 0)
        x_t_s[:, span] = low_s[span, :].T
        store(num_s.at[span, :], gr2_o.at[span, :])
        store(low_s.at[span, :], gb_o.at[span, :])
        store(out_s.at[span, :], out_o.at[span, :])
    store(x_t_s, gb_t_o)
    store(sums_s, sums_o)
    for copy in stores[1:] + [slope_copy(10), slope_copy(11)]:
        copy.wait()
    gather.drain()
    state.drain()


def forward_call(tokens, cotangent, attn_master, up_master, down_master, norm_params, seq_count):
    rows = tokens.shape[0]
    blocks = rows // PIECE * 6
    thin, thick = attn_master.shape[0], down_master.shape[0]
    trig = turning_table(seq_count)
    shapes = dict(
        wqkv=((D, 3 * D), bf16), wo=((D, D), bf16), wup=((D, FF), bf16), wdn=((FF, D), bf16),
        q=((rows, D), bf16), k=((rows, D), bf16), v=((rows, D), bf16), att=((rows, D), bf16),
        rden=((rows, D), f32), xhat=((rows, D), f32), rstd=((rows, 128), f32),
        x_t=((D, rows), bf16), att_t=((D, rows), bf16), low_t=((D, rows), bf16),
        act=((rows, FF), bf16), slope=((rows, FF), bf16), gb=((rows, D), bf16),
        gb_t=((D, rows), bf16),
        gr2=((rows, D), f32), out=((rows, D), bf16), state=((blocks, 144, PAIR), bf16),
        sums=((8, D), f32),
    )
    out_shape = [jax.ShapeDtypeStruct(s, d) for s, d in shapes.values()]
    hbm = pl.BlockSpec(memory_space=pl.ANY)
    scratch = [
        pltpu.VMEM((D, 3 * D), bf16), pltpu.VMEM((D, D), bf16),
        pltpu.VMEM((D, FF), bf16), pltpu.VMEM((FF, D), bf16),
        pltpu.VMEM((thin, 4, D), f32), pltpu.VMEM((thin, FF), f32), pltpu.VMEM((thick, D), f32),
        pltpu.VMEM((rows, D), bf16), pltpu.VMEM((rows, D), bf16), pltpu.VMEM((4, D), f32),
        pltpu.VMEM((PIECE, 2 * PAIR), f32), pltpu.VMEM((PIECE, PIECE // 2), bf16),
        pltpu.VMEM((rows, D), bf16), pltpu.VMEM((rows, D), bf16), pltpu.VMEM((rows, D), bf16),
        pltpu.VMEM((rows, D), f32), pltpu.VMEM((rows, D), f32), pltpu.VMEM((rows, D), bf16),
        pltpu.VMEM((rows, D), f32), pltpu.VMEM((rows, 128), f32), pltpu.VMEM((rows, D), bf16),
        pltpu.VMEM((rows, FF), bf16), pltpu.VMEM((rows, 256), bf16),
        pltpu.VMEM((rows, 256), bf16), pltpu.VMEM((rows, 256), f32),
        pltpu.VMEM((rows, 256), f32), pltpu.VMEM((rows, D), bf16),
        pltpu.VMEM((D, rows), bf16), pltpu.VMEM((D, rows), bf16), pltpu.VMEM((D, rows), bf16),
        pltpu.VMEM((8, D), f32),
        pltpu.VMEM((blocks, 144, PAIR), bf16), pltpu.VMEM((blocks, 144, PAIR), bf16),
        pltpu.VMEM((blocks, 144, PAIR), bf16), pltpu.VMEM((blocks, 144, PAIR), bf16),
        pltpu.SemaphoreType.DMA((8,)), pltpu.SemaphoreType.DMA((40,)),
        pltpu.SemaphoreType.DMA((2,)),
        pltpu.SemaphoreType.DMA((7, 28)), pltpu.SemaphoreType.DMA((7, 28)),
        pltpu.SemaphoreType.DMA((3,)), pltpu.SemaphoreType.DMA((3,)),
    ]
    return dict(
        zip(
            shapes,
            pl.pallas_call(
                forward_kernel,
                out_shape=out_shape,
                in_specs=[hbm] * 7,
                out_specs=[hbm] * len(out_shape),
                scratch_shapes=scratch,
                compiler_params=pltpu.CompilerParams(
                    collective_id=0, has_side_effects=True, vmem_limit_bytes=VMEM_BYTES
                ),
                name="gather_forward",
            )(
                tokens, cotangent, attn_master, up_master, down_master, norm_params,
                trig,
            ),
        )
    )


def turning_table(seq_count):
    length = seq_count * PIECE
    angle = math.pi / 2 * np.arange(length, dtype=np.float64) / length
    trig = np.repeat(np.stack([np.cos(angle), np.sin(angle)], axis=1), PAIR, axis=1)
    return jnp.asarray(trig, f32)


class Share:
    def __init__(self, grad, first, units, column, width, by_units, early, z_first, bufs, out):
        self.grad, self.first, self.units = grad, first, units
        self.column, self.width, self.by_units, self.early = column, width, by_units, early
        self.count = units // 2 if by_units else units
        self.half = width if by_units else width // 2
        self.twin, self.from_x, self.from_y, self.via_x, self.via_y, self.planes, self.final = bufs
        self.out, self.z_first = out, z_first

    def side(self, x):
        if self.by_units:
            return x * self.count, slice(0, self.width)
        return 0, ds(x * self.half, self.half, 128)

    def part(self, x):
        first, lanes = self.side(x)
        return pl.ds(first, self.count), lanes


class Reduce:
    def __init__(self, place, engine, send, recv, store_sem, squares):
        self.place, self.engine, self.send, self.recv = place, engine, send, recv
        self.store_sem, self.squares = store_sem, squares
        self.sent, self.stored, self.count = [], [], 0

    def copy(self, k, index, src, dst, device):
        return pltpu.make_async_remote_copy(
            src_ref=src, dst_ref=dst, send_sem=self.send.at[k, index],
            recv_sem=self.recv.at[k, index], device_id=device, device_id_type=MESH,
        )

    def push(self, k, index, src, dst, device, link):
        parts = [(src, dst)] if link == "c" else zip(two_parts(src), two_parts(dst))
        for one, other in parts:
            self.copy(k, index, one, other, device).start()
        self.sent.append((k, index, self.copy(k, index, src, dst, device)))
        self.engine.sent(("part", k, index), link, 2 * math.prod(dst.shape))

    def settle(self, parts):
        for k, index, copy in list(self.sent):
            if k in parts and index == 0:
                copy.wait_send()
                self.sent.remove((k, index, copy))

    def pull(self, k, index, dst):
        self.copy(k, index, dst, dst, self.place.across_c()).wait_recv()

    def launch(self, share):
        k = self.count
        self.count += 1
        src = share.grad.at[
            share.first : share.first + share.units, :, :, 1 - self.place.c, :,
            share.column : share.column + share.width,
        ]
        self.push(k, 0, src, share.twin, self.place.across_c(), "c")
        middle = [
            ((1, 2), self.fold_corner, None, 0.3),
            ((3, 4, 5, 6), self.fold_square, None, 0.4),
            ((7, 8, 9), self.fold_planes, "sum", 0.3),
        ]
        if share.z_first:
            middle = [
                ((1, 2, 3), self.first_planes, None, 0.3),
                ((4,), self.then_y, None, 0.1),
                ((5,), self.then_x, "sum", 0.1),
            ]
        for needs, act, mark, cost in [
            ((0,), self.fold_core, "core", 0.5),
            *middle,
            ((10,), self.share_x, None, 0.05),
            ((11,), self.share_c, "whole", 0.05),
        ]:
            keys = [("part", k, at) for at in needs]
            self.engine.add(keys, functools.partial(act, k, share), (mark, k), cost)

    def fold_core(self, k, s):
        p = self.place
        self.pull(k, 0, s.twin)
        own = s.grad[s.first : s.first + s.units, :, :, p.c, :, s.column : s.column + s.width]
        s.twin[...] = (s.twin[...].astype(f32) + own.astype(f32)).astype(bf16)
        e, oy, t = s.early, 1 - p.y, s.twin
        if s.z_first:
            for step in (1, 3, 2):
                z = p.plane(step)
                self.push(k, step, t.at[:, z], s.planes.at[:, step - 1], p.device(z=z), "z")
            return
        (mine, near), (theirs, far) = s.part(p.x), s.part(1 - p.x)
        self.push(k, 1, t.at[theirs, 0:e, oy, :, far], s.via_x, p.across_x(), "x")
        self.push(k, 2, t.at[theirs, e:PLANES, oy, :, far], s.via_y, p.across_y(), "y")
        self.push(
            k, 3, t.at[theirs, 0:e, p.y, :, far], s.from_x.at[:, 0:e], p.across_x(), "x"
        )
        self.push(
            k, 4, t.at[mine, e:PLANES, oy, :, near], s.from_y.at[:, e:PLANES], p.across_y(), "y"
        )

    def fold_corner(self, k, s):
        p, e, t, oy = self.place, s.early, s.twin, 1 - self.place.y
        (mine, near), (theirs, far) = s.part(p.x), s.part(1 - p.x)
        self.pull(k, 1, s.via_x)
        at = (mine, slice(0, e), oy, slice(None), near)
        t[at] = (t[at].astype(f32) + s.via_x[...].astype(f32)).astype(bf16)
        self.push(k, 5, t.at[mine, 0:e, oy, :, near], s.from_y.at[:, 0:e], p.across_y(), "y")
        self.pull(k, 2, s.via_y)
        at = (theirs, slice(e, PLANES), p.y, slice(None), far)
        t[at] = (t[at].astype(f32) + s.via_y[...].astype(f32)).astype(bf16)
        self.push(
            k, 6, t.at[theirs, e:PLANES, p.y, :, far], s.from_x.at[:, e:PLANES], p.across_x(), "x"
        )

    def fold_square(self, k, s):
        p, e, t = self.place, s.early, s.twin
        mine, near = s.part(p.x)
        self.pull(k, 3, s.from_x.at[:, 0:e])
        self.pull(k, 4, s.from_y.at[:, e:PLANES])
        self.pull(k, 5, s.from_y.at[:, 0:e])
        self.pull(k, 6, s.from_x.at[:, e:PLANES])
        at = (mine, slice(None), p.y, slice(None), near)
        total = t[at].astype(f32) + s.from_x[...].astype(f32) + s.from_y[...].astype(f32)
        t[at] = total.astype(bf16)
        for step in (1, 3, 2):
            z = p.plane(step)
            self.push(
                k, 6 + step, t.at[mine, z, p.y, :, near], s.planes.at[:, step - 1],
                p.device(z=z), "z",
            )

    def fold_planes(self, k, s):
        p = self.place
        mine, near = s.part(p.x)
        for step in (1, 3, 2):
            self.pull(k, 6 + step, s.planes.at[:, step - 1])
        total = s.twin[mine, p.z, p.y, :, near].astype(f32)
        for step in range(3):
            total = total + s.planes[:, step].astype(f32)
        self.own_sum(k, s, total.astype(bf16))

    def first_planes(self, k, s):
        p, t = self.place, s.twin
        for step in (1, 3, 2):
            self.pull(k, step, s.planes.at[:, step - 1])
        total = t[:, p.z].astype(f32)
        for step in range(3):
            total = total + s.planes[:, step].astype(f32)
        t[:, p.z] = total.astype(bf16)
        self.push(k, 4, t.at[:, p.z, 1 - p.y], s.from_y, p.across_y(), "y")

    def then_y(self, k, s):
        p, t = self.place, s.twin
        theirs, far = s.part(1 - p.x)
        self.pull(k, 4, s.from_y)
        total = t[:, p.z, p.y].astype(f32) + s.from_y[...].astype(f32)
        t[:, p.z, p.y] = total.astype(bf16)
        self.push(k, 5, t.at[theirs, p.z, p.y, :, far], s.from_x, p.across_x(), "x")

    def then_x(self, k, s):
        p = self.place
        mine, near = s.part(p.x)
        self.pull(k, 5, s.from_x)
        total = s.twin[mine, p.z, p.y, :, near].astype(f32) + s.from_x[...].astype(f32)
        self.own_sum(k, s, total.astype(bf16))

    def own_sum(self, k, s, total):
        p = self.place
        mine, near = s.part(p.x)
        s.final[mine, p.c, :, near] = total
        wide = total.astype(f32).reshape(s.count * 48, s.half)
        for lane in range(0, s.half, 128):
            part = wide[:, lane : lane + 128]
            self.squares[...] += jnp.sum((part * part).reshape(-1, 8, 128), axis=0)
        piece = s.final.at[mine, p.c, :, near]
        self.push(k, 10, piece, piece, p.across_x(), "x")

    def share_x(self, k, s):
        p = self.place
        theirs, far = s.part(1 - p.x)
        self.pull(k, 10, s.final.at[theirs, p.c, :, far])
        half = s.final.at[:, p.c]
        self.push(k, 11, half, half, p.across_c(), "c")

    def share_c(self, k, s):
        self.pull(k, 11, s.final.at[:, 1 - self.place.c])
        copy = pltpu.make_async_copy(s.final, s.out, self.store_sem.at[k])
        copy.start()
        self.stored.append(copy)

    def drain(self):
        for _, _, copy in self.sent:
            copy.wait_send()
        for copy in self.stored:
            copy.wait()


class Total:
    def __init__(self, place, engine, name, value, near, planes, send, recv):
        self.place, self.engine, self.name = place, engine, name
        self.value, self.near, self.planes = value, near, planes
        self.send, self.recv, self.sent = send, recv, []
        y, x, c = 1 - place.y, 1 - place.x, 1 - place.c
        peers = [place.across_c(), place.across_x(), place.across_y()] + place.corners()
        flips = [(0, 0, 1), (0, 1, 0), (1, 0, 0), (0, 1, 1), (1, 0, 1), (1, 1, 0), (1, 1, 1)]
        self.slots = [
            ((y if flip[0] else place.y) * 2 + (x if flip[1] else place.x)) * 2
            + (c if flip[2] else place.c)
            for flip in flips
        ]
        own = near.at[place.in_plane()]
        near[place.in_plane()] = value[...]
        for at, peer in enumerate(peers):
            self.push(at, own, peer, "cxyxyxy"[at])
        engine.add([(name, at) for at in range(7)], self.across)

    def copy(self, index, ref, device):
        return pltpu.make_async_remote_copy(
            src_ref=ref, dst_ref=ref, send_sem=self.send.at[index],
            recv_sem=self.recv.at[index], device_id=device, device_id_type=MESH,
        )

    def push(self, index, ref, device, link):
        copy = self.copy(index, ref, device)
        copy.start()
        self.sent.append(copy)
        self.engine.sent((self.name, index), link, 4 * math.prod(ref.shape))

    def across(self):
        p = self.place
        for at, slot in enumerate(self.slots):
            self.copy(at, self.near.at[slot], p.across_c()).wait_recv()
        total = self.near[0]
        for at in range(1, 8):
            total = total + self.near[at]
        self.planes[p.z] = total
        for step in (1, 3, 2):
            self.push(6 + step, self.planes.at[p.z], p.device(z=p.plane(step)), "z")
        self.engine.add([(self.name, at) for at in (7, 8, 9)], self.end, self.name)

    def end(self):
        for step in (1, 3, 2):
            own = self.planes.at[self.place.plane(-step)]
            self.copy(6 + step, own, self.place.across_c()).wait_recv()
        self.value[...] = (self.planes[0] + self.planes[1]) + (self.planes[2] + self.planes[3])

    def drain(self):
        for copy in self.sent:
            copy.wait_send()


class StateSum:
    def __init__(self, place, engine, send, recv, own, twin, chip, prior, late):
        self.x, self.c, self.engine = place.x, place.c, engine
        self.own, self.twin, self.chip, self.prior = own, twin, chip, prior
        self.giver, self.taker = (1, 0) if late else (0, 1)
        half = own.shape[0] // 2
        self.size = math.prod(own.shape)
        mine, other = ds(place.c * half, half, 1), ds((1 - place.c) * half, half, 1)

        def copy(index, src, dst, device):
            return pltpu.make_async_remote_copy(
                src_ref=src, dst_ref=dst, send_sem=send.at[index], recv_sem=recv.at[index],
                device_id=device, device_id_type=MESH,
            )

        self.swap = copy(0, own, twin, place.across_c())
        self.over = copy(1, chip.at[mine], prior.at[mine], place.across_x())
        self.pass_on = copy(2, prior.at[mine], prior.at[mine], place.across_c())
        self.taken = copy(2, prior.at[other], prior.at[other], place.across_c())
        self.swap.start()
        engine.sent("swap", "c", 2 * self.size)
        engine.add(["swap"], self.join, None, 0.5)
        engine.add(["over"], self.forward)
        engine.add(["pass"], self.end, "state")

    def join(self):
        self.swap.wait_recv()
        self.chip[...] = (self.own[...].astype(f32) + self.twin[...].astype(f32)).astype(bf16)

        @pl.when(self.x == self.giver)
        def _():
            self.over.start()

        self.engine.sent("over", "x", self.size)

    def forward(self):
        @pl.when(self.x == self.taker)
        def _():
            self.over.wait_recv()
            self.pass_on.start()

        self.engine.sent("pass", "c", self.size)

    def end(self):
        @pl.when(self.x == self.taker)
        def _():
            self.taken.wait_recv()

        @pl.when(self.x == self.giver)
        def _():
            self.over.wait_send()

    def drain(self):
        self.swap.wait_send()

        @pl.when(self.x == self.taker)
        def _():
            self.pass_on.wait_send()

    def total(self, b):
        far = jnp.where(self.x == self.taker, self.prior[b].astype(f32), 0.0)
        return far + jnp.where(self.c == self.taker, self.twin[b].astype(f32), 0.0)


def lane_in_head(shape):
    return lax.broadcasted_iota(jnp.int32, shape, 1) & (HEAD - 1)


def backward_kernel(
    wqkv_h, wo_h, wup_h, q_h, k_h, v_h, att_h, rden_h, xhat_h, rstd_h, x_t_h, att_t_h,
    low_t_h, act_h, slope_h, gb_h, gb_t_h, gr2_h, state_h, sums_h, wdn_h, norm_h, trig_h,
    input_o, attn_o, up_o, down_o, norm_o, square_o,
    wup, acts, slope, gr2, gb, left, wide, rstd, ga_s, gd_s, gu_s,
    norm_s, trig_s, tri_s, state_s, st_own, st_twin, st_chip, st_prior,
    norm_v, norm_w, norm_z, sq_v, sq_w, sq_z,
    *rest,
):
    bufs = rest[: 7 * SHARES]
    load_sem, store_sem, r_send, r_recv, s_send, s_recv = rest[7 * SHARES : 7 * SHARES + 6]
    t_send, t_recv, u_send, u_recv = rest[7 * SHARES + 6 :]
    place = Place()
    rows_all = gr2.shape[0]
    blocks = state_s.shape[0]
    tile = 256
    count = [0]

    def load(src, dst):
        copy = pltpu.make_async_copy(src, dst, load_sem.at[count[0]])
        count[0] += 1
        copy.start()
        return copy

    def wait(copies):
        for copy in copies:
            copy.wait()

    first_in = [load(gb_t_h, wup.at[:, 0:rows_all])]
    act_in = [load(act_h.at[:, D * z : D * z + D], acts.at[:, D * z : D * z + D]) for z in range(4)]
    sq_v[...] = jnp.zeros_like(sq_v)
    fill_triangles(tri_s)
    engine = Engine(0.75)
    reduce = Reduce(place, engine, r_send, r_recv, store_sem, sq_v)
    shares = []
    for at, (kind, first, units, column, width, by_units, early, z_first) in enumerate(share_plan()):
        grad, out = {"down": (gd_s, down_o), "up": (gu_s, up_o), "attn": (ga_s, attn_o)}[kind]
        cut = out.at[first : first + units, :, :, column : column + width]
        mine = bufs[7 * at : 7 * at + 7]
        shares.append(
            Share(grad, first, units, column, width, by_units, early, z_first, mine, cut)
        )
    shares = iter(shares)
    greet(place, corners=True)
    wait(first_in)

    for t in range(3):
        for z in range(PLANES):
            if t == 0:
                act_in[z].wait()
            if t == 0 and z == PLANES - 1:
                next_in = [
                    load(gb_h, gb), load(wdn_h, ga_s), load(slope_h, slope), load(low_t_h, left),
                ]
            starts = [D * z + 384 * y + 128 * t for y in range(2)]
            pair = [acts[:, start : start + 128] for start in starts]
            part = dot(wup[:, 0:rows_all], jnp.concatenate(pair, axis=1)).astype(bf16)
            for y in range(2):
                own = part[:, 128 * y : 128 * y + 128].reshape(8, 2, 48, 128)
                gd_s[:, z, y, :, :, 128 * t : 128 * t + 128] = own
            engine.tick(0.6)
        reduce.launch(next(shares))

    mid_in = [
        load(wup_h, wup), load(gr2_h, gr2), load(xhat_h, wide), load(rstd_h, rstd),
        load(norm_h, norm_s), load(sums_h, norm_v),
    ]
    late_in = [
        load(state_h, state_s),
        load(trig_h.at[ds((place.x * 2 + place.c) * PIECE, PIECE, PIECE), :], trig_s),
    ]
    for at, src in enumerate((q_h, k_h, v_h, att_h)):
        late_in.append(load(src, acts.at[:, D * at : D * at + D]))
    wait(next_in)
    for at in range(12):
        cols = slice(256 * at, 256 * at + 256)
        down_rows = ga_s[at // 3].reshape(D, D)[256 * (at % 3) : 256 * (at % 3) + 256]
        for part in range(0, rows_all, PIECE):
            span = slice(part, part + PIECE)
            grad = dot_nt(gb[span, :], down_rows) * slope[span, cols].astype(f32)
            slope[span, cols] = grad.astype(bf16)
        up = dot(left[...], slope[:, cols]).astype(bf16)
        gu_s[0, :, :, :, :, cols] = up.reshape(PLANES, 2, 2, 48, tile)
        engine.tick(1.4)
        if at % 4 == 3:
            reduce.launch(next(shares))
    att_t_in = load(att_t_h, left)
    wait(mid_in)
    gain_one = norm_s[0:1, :]
    norm_v[2:4, :] = norm_v[0:2, :]
    norm_v[0:2, :] = jnp.zeros((2, D), f32)

    def first_back(t, carry):
        cols = ds(t * tile, tile, tile)
        for part in range(0, rows_all, PIECE):
            span = slice(part, part + PIECE)
            gr2[span, cols] += dot_nt(slope[span, :], wup[cols, :])
        return carry

    def norm_part(t, carry):
        rows = ds(t * 128, 128, 128)
        unit, grad = wide[rows, :], gr2[rows, :]
        norm_v[0:1, :] += jnp.sum(grad * unit, axis=0, keepdims=True)
        norm_v[1:2, :] += jnp.sum(grad, axis=0, keepdims=True)
        grad = norm_back(grad * gain_one, unit, rstd[rows, 0:1])
        gr2[rows, :] = grad
        gb[rows, :] = grad.astype(bf16)
        return carry

    for part in range(3):
        lax.fori_loop(part, part + 1, first_back, 0)
        engine.tick(2.2)
    wo_in = load(wo_h, wup.at[:, 3 * D : 4 * D])
    wqkv_in = load(wqkv_h, wup.at[:, 0 : 3 * D])
    for part in range(0, rows_all // 128, 4):
        lax.fori_loop(part, part + 4, norm_part, 0)
        engine.tick(0.8)
    norms = Total(place, engine, "norms", norm_v, norm_w, norm_z, t_send, t_recv)
    rden_in = load(rden_h, wide)
    att_t_in.wait()

    def outer(unit, column, grad):
        part = dot(left[...], grad).astype(bf16)
        part = part.reshape(PLANES, 2, 2, 48, 256)
        ga_s[unit, :, :, :, :, column : column + 256] = part
        engine.tick(0.6)

    for t in range(3):
        outer(3, 256 * t, gb[:, 256 * t : 256 * t + 256])
    reduce.launch(next(shares))
    x_t_in = load(x_t_h, left)
    wait(late_in)
    rden_in.wait()
    wo_in.wait()
    square = (2 * PAIR, PAIR)
    row_half = (lax.broadcasted_iota(jnp.int32, square, 0) & (PAIR - 1)) < HEAD
    by_head = (row_half == first_half(square)).astype(f32).astype(bf16)

    def split(i, carry):
        g, t = i // 3, lax.rem(i, 3)
        rows = ds(g * PIECE, PIECE, PIECE)
        grad = dot_nt(gb[rows, :], wup[ds(t * tile, tile, tile), 3 * D : 4 * D])
        for pair in range(2):
            base = t * tile + pair * PAIR
            cols, num_cols = ds(base, PAIR, PAIR), ds(3 * D + base, PAIR, PAIR)
            mine = grad[:, pair * PAIR : pair * PAIR + PAIR]
            recip = wide[rows, cols]
            along = mine * acts[rows, num_cols].astype(f32)
            high = along.astype(bf16)
            rest = (along - high.astype(f32)).astype(bf16)
            gden = -dot(jnp.concatenate([high, rest], axis=1), by_head) * recip
            high = gden.astype(bf16).astype(f32)
            lane = lane_in_head(gden.shape)
            both = jnp.where(lane == 0, high, jnp.where(lane == 1, gden - high, 0.0))
            acts[rows, num_cols] = both.astype(bf16)
            slope[rows, num_cols] = (mine * recip).astype(bf16)
        return carry

    for part in range(0, blocks // 2, 2):
        lax.fori_loop(part, part + 2, split, 0)
        engine.tick(1.6)

    def column_of(b, group):
        return ds(group * D + lax.rem(b, 6) * PAIR, PAIR, PAIR)

    def local(b, carry):
        rows, cols = block_of(b)
        queries = turned(acts[rows, cols], trig_s[...])
        state = dot_tn(queries, slope[rows, column_of(b, 3)])
        cross = dot_tn(acts[rows, column_of(b, 3)], queries)
        shape = (PAIR, 2 * PAIR)
        kept = jnp.where(top_half(shape) == pair_mask(shape), cross, 0.0)
        totals = jnp.broadcast_to(jnp.sum(kept, axis=0, keepdims=True), (16, 2 * PAIR))
        st_own[b] = squeeze_state(state, totals).astype(bf16)
        return carry

    for part in range(0, blocks, 4):
        lax.fori_loop(part, part + 4, local, 0)
        engine.tick(1.5)
    state = StateSum(place, engine, s_send, s_recv, st_own, st_twin, st_chip, st_prior, True)

    def soft_slope(feature):
        return 1.0 - jnp.exp(-feature.astype(f32))

    def take(b):
        rows, cols = block_of(b)
        num, den = slope[rows, column_of(b, 3)], acts[rows, column_of(b, 3)]
        q, k, v = (acts[rows, column_of(b, group)] for group in range(3))
        return jnp.concatenate([num, den], axis=1), num, q, k, v

    def query_grad(i, carry):
        marks = [2 * i, 2 * i + 1]
        taken = [take(b) + (state_s[b],) for b in marks]
        outs = []
        for own, _, q, k, v, packed in taken:
            grad = causal_product(own, with_ones(v), turned(k, trig_s[...]), tri_s)
            grad = (grad + dot_nt(own, spread_state(packed))) * trig_s[...]
            outs.append(((grad[:, :PAIR] + grad[:, PAIR:]) * soft_slope(q)).astype(bf16))
        for b, out in zip(marks, outs):
            slope[block_of(b)] = out
        return carry

    for part in range(blocks // 2):
        lax.fori_loop(part, part + 1, query_grad, 0)
        engine.tick(2.6)
    x_t_in.wait()
    for t in range(3):
        outer(0, 256 * t, slope[:, 256 * t : 256 * t + 256])
    reduce.launch(next(shares))
    engine.until("state")

    def key_pair(t):
        def body(g, carry):
            marks = [g * 6 + 2 * t, g * 6 + 2 * t + 1]
            taken = [take(b) + (state.total(b).astype(bf16),) for b in marks]
            outs = []
            for own, num, q, k, v, packed in taken:
                queries, keys = turned(q, trig_s[...]), turned(k, trig_s[...])
                spread = spread_state(packed)
                grad = causal_transposed(own, with_ones(v), queries, tri_s)
                one = (lane_in_head(v.shape) == 0).astype(f32).astype(bf16)
                grad = (grad + dot_nt(jnp.concatenate([v, one], axis=1), spread)) * trig_s[...]
                grad = (grad[:, :PAIR] + grad[:, PAIR:]) * soft_slope(k)
                grad_v = causal_transposed(queries, keys, num, tri_s)
                grad_v = grad_v + dot(keys, spread[:, :PAIR])
                outs.append((grad.astype(bf16), grad_v.astype(bf16)))
            for b, (grad, grad_v) in zip(marks, outs):
                rows, _ = block_of(b)
                slope[rows, column_of(b, 1)] = grad
                slope[rows, column_of(b, 2)] = grad_v
            return carry

        return body

    for t in range(3):
        for part in range(blocks // 6):
            lax.fori_loop(part, part + 1, key_pair(t), 0)
            engine.tick(4.4)
        for j in (1, 2):
            outer(j, 256 * t, slope[:, D * j + 256 * t : D * j + 256 * t + 256])
        reduce.launch(next(shares))
    wqkv_in.wait()

    def input_grad(t, carry):
        cols = ds(t * tile, tile, tile)
        for part in range(0, rows_all, PIECE):
            span = slice(part, part + PIECE)
            gr2[span, cols] += dot_nt(slope[span, 0 : 3 * D], wup[cols, 0 : 3 * D])
        return carry

    for part in range(3):
        lax.fori_loop(part, part + 1, input_grad, 0)
        engine.tick(1.8)
    stores = [
        pltpu.make_async_copy(gr2, input_o, load_sem.at[count[0]]),
        pltpu.make_async_copy(norm_v, norm_o, load_sem.at[count[0] + 1]),
    ]
    engine.until("norms")
    for copy in stores:
        copy.start()
    engine.until(*[("sum", k) for k in range(SHARES)])
    squares = Total(place, engine, "squares", sq_v, sq_w, sq_z, u_send, u_recv)
    engine.until("squares")
    stores.append(pltpu.make_async_copy(sq_v, square_o, load_sem.at[count[0] + 2]))
    stores[2].start()
    engine.rest()
    wait(stores)
    reduce.drain()
    norms.drain()
    squares.drain()
    state.drain()


def share_plan():
    plan = [("down", 0, 8, 128 * t, 128) for t in range(3)]
    plan += [("up", 0, 1, FF // 3 * t, FF // 3) for t in range(3)]
    plan += [("attn", 3, 1, 0, D), ("attn", 0, 1, 0, D)]
    plan += [("attn", 1, 2, 256 * t, 256) for t in range(3)]
    return [
        part + (part[0] == "down", 1 if at % 2 else 2, at in (2,)) for at, part in enumerate(plan)
    ]


SHARES = 11


def backward_call(s, norm_params, seq_count):
    rows = s["q"].shape[0]
    blocks = rows // PIECE * 6
    trig = turning_table(seq_count)
    names = (
        "wqkv", "wo", "wup", "q", "k", "v", "att", "rden", "xhat", "rstd", "x_t", "att_t",
        "low_t", "act", "slope", "gb", "gb_t", "gr2", "state", "sums",
    )
    wdn = s["wdn"].reshape(4, PLANES, 2, 2, 48, D)
    shapes = [
        ((rows, D), f32),
        ((4, 2, 48, D), bf16), ((1, 2, 48, FF), bf16), ((8, 2, 48, FF // 8), bf16),
        ((8, D), f32), ((8, 128), f32),
    ]
    vmem = [
        ((D, FF), bf16), ((rows, FF), bf16), ((rows, FF), bf16), ((rows, D), f32),
        ((rows, D), bf16), ((D, rows), bf16), ((rows, D), f32), ((rows, 128), f32),
        ((4, PLANES, 2, 2, 48, D), bf16), ((8, PLANES, 2, 2, 48, FF // 8), bf16),
        ((1, PLANES, 2, 2, 48, FF), bf16),
        ((4, D), f32), ((PIECE, 2 * PAIR), f32), ((PIECE, PIECE // 2), bf16),
        ((blocks, 144, PAIR), bf16), ((blocks, 144, PAIR), bf16), ((blocks, 144, PAIR), bf16),
        ((blocks, 144, PAIR), bf16), ((blocks, 144, PAIR), bf16),
        ((8, D), f32), ((8, 8, D), f32), ((PLANES, 8, D), f32),
        ((8, 128), f32), ((8, 8, 128), f32), ((PLANES, 8, 128), f32),
    ]
    for _, _, units, _, width, by_units, early, z_first in share_plan():
        count, part = (units // 2, width) if by_units else (units, width // 2)
        if z_first:
            vmem += [
                ((units, PLANES, 2, 48, width), bf16), ((count, 48, part), bf16),
                ((units, 48, width), bf16), ((16, 128), bf16), ((16, 128), bf16),
                ((units, 3, 2, 48, width), bf16), ((units, 2, 48, width), bf16),
            ]
            continue
        vmem += [
            ((units, PLANES, 2, 48, width), bf16), ((count, PLANES, 48, part), bf16),
            ((count, PLANES, 48, part), bf16), ((count, early, 48, part), bf16),
            ((count, PLANES - early, 48, part), bf16), ((count, 3, 48, part), bf16),
            ((units, 2, 48, width), bf16),
        ]
    dma = pltpu.SemaphoreType.DMA
    sems = [(36,), (SHARES,), (SHARES, 12), (SHARES, 12), (3,), (3,), (10,), (10,), (10,), (10,)]
    hbm = pl.BlockSpec(memory_space=pl.ANY)
    return pl.pallas_call(
        backward_kernel,
        out_shape=[jax.ShapeDtypeStruct(*shape) for shape in shapes],
        in_specs=[hbm] * 23,
        out_specs=[hbm] * len(shapes),
        scratch_shapes=[pltpu.VMEM(*shape) for shape in vmem] + [dma(shape) for shape in sems],
        compiler_params=pltpu.CompilerParams(
            collective_id=1, has_side_effects=True, vmem_limit_bytes=VMEM_BYTES
        ),
        name="backward_reduce",
    )(*[s[name] for name in names], wdn, norm_params, trig)


def adam_step(weight, grad, first, second, rate, outs):
    first_new = beta_one * first + (1.0 - beta_one) * grad
    second_new = beta_two * second + (1.0 - beta_two) * grad * grad
    first_hat = first_new * (1.0 / (1.0 - beta_one**STEP))
    second_hat = second_new * (1.0 / (1.0 - beta_two**STEP))
    step = first_hat / (jnp.sqrt(second_hat) + epsilon) + weight_decay * weight
    for ref, value in zip(outs, (grad, weight - rate * step, first_new, second_new)):
        ref[...] = value.reshape(ref.shape)


def update_kernel(
    out_rate, steps,
    layer_h, input_h, attn_r, up_r, down_r, norm_r, square_r,
    attn_w, up_w, down_w, norm_w, attn_m, up_m, down_m, norm_m, attn_v, up_v, down_v, norm_v,
    layer_o, input_o, attn_g, up_g, down_g, norm_g, grad_norm_o,
    attn_n, up_n, down_n, norm_n, attn_f, up_f, down_f, norm_f, attn_s, up_s, down_s, norm_s,
    grad_s, turned_s, layer_s, input_s, copy_sem,
):
    norm_raw = norm_r[0:4, :]
    pairs = [(layer_h, layer_s, layer_o), (input_h, input_s, input_o)]
    inward = [
        pltpu.make_async_copy(src, mid, copy_sem.at[at]) for at, (src, mid, _) in enumerate(pairs)
    ]
    outward = [
        pltpu.make_async_copy(mid, dst, copy_sem.at[2 + at])
        for at, (_, mid, dst) in enumerate(pairs)
    ]

    @pl.when(pl.program_id(0) == 0)
    def _():
        for copy in inward:
            copy.start()
        turned_s[...] = down_r[...].T.astype(f32)

    grad_norm = jnp.sqrt(
        jnp.sum(square_r[...], keepdims=True) + jnp.sum(norm_raw * norm_raw, keepdims=True)
    )
    clip = clip_limit / jnp.maximum(grad_norm, clip_limit)
    grad_norm_o[...] = grad_norm
    down_rate = learn_rate * math.sqrt(D / FF)
    grad = up_r[...].astype(f32) * clip
    adam_step(up_w[...], grad, up_m[...], up_v[...], learn_rate, (up_g, up_n, up_f, up_s))
    rows = down_w.shape[0]
    grad = turned_s[ds(pl.program_id(0) * rows, rows, rows), :] * clip
    outs = (down_g, down_n, down_f, down_s)
    adam_step(down_w[...], grad, down_m[...], down_v[...], down_rate, outs)
    count = attn_w.shape[0]
    shape = (4 * count, D)
    for j in range(4):
        part = attn_r[j].astype(f32)
        for t in range(D // 128):
            span = pl.ds(4 * count * t + j, count, stride=4)
            grad_s[span, :] = part[:, 128 * t : 128 * t + 128]
    grad = jnp.concatenate(
        [grad_s[4 * count * t : 4 * count * (t + 1), :] for t in range(D // 128)], axis=1
    )
    row = lax.broadcasted_iota(jnp.int32, shape, 0)
    rate = jnp.where((row & 3) == 3, learn_rate * out_rate, learn_rate)
    flat = [ref[...].reshape(shape) for ref in (attn_w, attn_m, attn_v)]
    outs = (attn_g, attn_n, attn_f, attn_s)
    adam_step(flat[0], grad * clip, flat[1], flat[2], rate, outs)
    outs = (norm_g, norm_n, norm_f, norm_s)
    adam_step(norm_w[...], norm_raw * clip, norm_m[...], norm_v[...], gain_rate, outs)

    @pl.when(pl.program_id(0) == 1)
    def _():
        for taken, given in zip(inward, outward):
            taken.wait()
            given.start()

    @pl.when(pl.program_id(0) == steps - 1)
    def _():
        for copy in outward:
            copy.wait()


def update_call(layer_output, input_grad, raw, norm_raw, square, weights, firsts, seconds, length):
    steps = 6
    thin, thick = weights[0].shape[0], weights[2].shape[0]
    a, u, d = thin // steps, thin // steps, thick // steps
    attn = pl.BlockSpec((a, 4, D), lambda t: (t, 0, 0))
    up = pl.BlockSpec((u, FF), lambda t: (t, 0))
    down = pl.BlockSpec((d, D), lambda t: (t, 0))
    whole = lambda rows, cols: pl.BlockSpec((rows, cols), lambda t: (0, 0))
    norm = whole(4, D)
    kinds = [attn, up, down, norm]
    shapes = [jax.ShapeDtypeStruct(w.shape, f32) for w in weights]
    one = jax.ShapeDtypeStruct((1, 1), f32)
    hbm = pl.BlockSpec(memory_space=pl.ANY)
    through = [jax.ShapeDtypeStruct(v.shape, v.dtype) for v in (layer_output, input_grad)]
    return pl.pallas_call(
        functools.partial(update_kernel, math.sqrt(length // 8), steps),
        grid=(steps,),
        in_specs=[hbm, hbm, pl.BlockSpec((4, a, D), lambda t: (0, t, 0)), up, whole(D, thick)]
        + [whole(8, D), whole(8, 128)]
        + kinds * 3,
        out_specs=[hbm, hbm] + kinds + [whole(1, 1)] + kinds * 3,
        out_shape=through + shapes + [one] + shapes * 3,
        scratch_shapes=[
            pltpu.VMEM((4 * a * D // 128, 128), f32), pltpu.VMEM((thick, D), f32),
            pltpu.VMEM(layer_output.shape, bf16), pltpu.VMEM(input_grad.shape, f32),
            pltpu.SemaphoreType.DMA((4,)),
        ],
        compiler_params=pltpu.CompilerParams(vmem_limit_bytes=VMEM_BYTES),
        name="adamw_update",
    )(layer_output, input_grad, *raw, norm_raw, square, *weights, *firsts, *seconds)


def prefix(part, axis, combine, identity):
    place = lax.axis_index(axis)
    gathered = jax.tree.map(lambda a: lax.all_gather(a, axis), part)
    state = jax.tree.map(lambda a, e: jnp.zeros_like(a) + jnp.asarray(e, a.dtype), part, identity)

    def prefix_one(step, state):
        return combine(
            state, jax.tree.map(lambda a: lax.dynamic_index_in_dim(a, step, 0, False), gathered)
        )

    return lax.fori_loop(0, place, prefix_one, state)


def carried_in(shard, axis, join, neutral):
    count = lax.axis_size(axis)
    place = lax.axis_index(axis)
    ahead = count - 1 - place
    gathered = jax.tree.map(
        lambda a, kind: lax.all_gather(a.astype(kind), axis),
        shard,
        jax.tree.map(lambda a: jnp.bfloat16 if a.dtype == jnp.float32 else a.dtype, shard),
    )
    state = jax.tree.map(lambda a, e: jnp.zeros_like(a) + jnp.asarray(e, a.dtype), shard, neutral)

    def carried_one(step, state):
        source = count - 1 - step
        return join(
            state,
            jax.tree.map(
                lambda a, own: lax.dynamic_index_in_dim(a, source, 0, False).astype(own.dtype),
                gathered,
                shard,
            ),
        )

    return lax.fori_loop(0, ahead, carried_one, state)


def add_states(earlier, later):
    return jax.tree.map(jnp.add, earlier, later)


def layer_norm(values, gain_row, bias_row):
    centered = values - jnp.mean(values, axis=-1, keepdims=True)
    spread = jnp.mean(centered * centered, axis=-1, keepdims=True)
    return centered * lax.rsqrt(spread + norm_eps) * gain_row + bias_row


def piece_scores(query_cos, query_sin, key_cos, key_sin, causal):
    scores = jnp.einsum("ihe,jhe->hij", query_cos, key_cos, preferred_element_type=jnp.float32)
    scores = scores + jnp.einsum(
        "ihe,jhe->hij", query_sin, key_sin, preferred_element_type=jnp.float32
    )
    return jnp.where(causal[None], scores, 0.0)


def adamw(weight, gradient, first_moment, second, step_rate):
    first_new = beta_one * first_moment + (1.0 - beta_one) * gradient
    second_new = beta_two * second + (1.0 - beta_two) * gradient * gradient
    first_hat = first_new / (1.0 - beta_one**STEP)
    second_hat = second_new / (1.0 - beta_two**STEP)
    weight_new = weight - step_rate * (
        first_hat / (jnp.sqrt(second_hat) + epsilon) + weight_decay * weight
    )
    return (weight_new, first_new, second_new)


def plain_shards(
    layer_input,
    cotangent,
    attn_master,
    up_master,
    down_master,
    norm_params,
    attn_first,
    up_first,
    down_first,
    norm_first,
    attn_second,
    up_second,
    down_second,
    norm_second,
):
    groups, piece_rows, model_width = layer_input.shape
    head_count = model_width // HEAD
    length = piece_rows * lax.axis_size("seq")
    rows_all = groups * piece_rows
    attn_full, up_full, down_full = (
        lax.all_gather(attn_master.astype(jnp.bfloat16), "dp", axis=0, tiled=True),
        lax.all_gather(up_master.astype(jnp.bfloat16), "dp", axis=0, tiled=True),
        lax.all_gather(down_master.astype(jnp.bfloat16), "dp", axis=0, tiled=True),
    )
    project_in = attn_full[:, :3, :].reshape(model_width, 3 * model_width)
    out_weight = attn_full[:, 3, :]
    tokens = layer_input.reshape(rows_all, model_width)
    projected = jnp.dot(tokens, project_in, preferred_element_type=jnp.float32)
    query_pre = projected[:, :model_width]
    key_pre = projected[:, model_width : 2 * model_width]
    value_pre = projected[:, 2 * model_width :]
    position = (lax.axis_index("seq") * piece_rows + jnp.arange(piece_rows)).astype(jnp.float32)
    phase_angle = math.pi / 2 * position / length
    cosine_weight = jnp.tile(jnp.cos(phase_angle), groups)[:, None]
    sine_weight = jnp.tile(jnp.sin(phase_angle), groups)[:, None]
    query_feat = jax.nn.softplus(query_pre)
    key_feat = jax.nn.softplus(key_pre)
    shape_four = (groups, piece_rows, head_count, HEAD)
    query_cos = (query_feat * cosine_weight).astype(jnp.bfloat16).reshape(shape_four)
    query_sin = (query_feat * sine_weight).astype(jnp.bfloat16).reshape(shape_four)
    key_cos = (key_feat * cosine_weight).astype(jnp.bfloat16).reshape(shape_four)
    key_sin = (key_feat * sine_weight).astype(jnp.bfloat16).reshape(shape_four)
    values = value_pre.astype(jnp.bfloat16).reshape(shape_four)
    local_state = (
        jnp.stack(
            [
                jnp.einsum("gjhe,gjhf->ghef", key_cos, values, preferred_element_type=jnp.float32),
                jnp.einsum("gjhe,gjhf->ghef", key_sin, values, preferred_element_type=jnp.float32),
            ],
            axis=1,
        ),
        jnp.stack(
            [
                jnp.sum(key_cos, axis=1, dtype=jnp.float32),
                jnp.sum(key_sin, axis=1, dtype=jnp.float32),
            ],
            axis=1,
        ),
    )
    identity = jax.tree.map(jnp.zeros_like, local_state)
    prior_state, prior_total = prefix(
        (local_state[0], local_state[1]), "seq", add_states, (identity[0], identity[1])
    )
    causal = jnp.arange(piece_rows)[:, None] >= jnp.arange(piece_rows)[None, :]
    attended_list = []
    denominator_list = []
    for group_index in range(groups):
        scores = piece_scores(
            query_cos[group_index],
            query_sin[group_index],
            key_cos[group_index],
            key_sin[group_index],
            causal,
        )
        qcos_wide = query_cos[group_index].astype(jnp.float32)
        qsin_wide = query_sin[group_index].astype(jnp.float32)
        numerator = jnp.einsum(
            "hij,jhe->ihe",
            scores.astype(jnp.bfloat16),
            values[group_index],
            preferred_element_type=jnp.float32,
        )
        numerator = numerator + jnp.einsum(
            "ihe,hef->ihf", qcos_wide, prior_state[group_index, 0], precision=highest
        )
        numerator = numerator + jnp.einsum(
            "ihe,hef->ihf", qsin_wide, prior_state[group_index, 1], precision=highest
        )
        denominator = jnp.sum(scores, axis=-1).T
        denominator = denominator + jnp.einsum(
            "ihe,he->ih", qcos_wide, prior_total[group_index, 0], precision=highest
        )
        denominator = denominator + jnp.einsum(
            "ihe,he->ih", qsin_wide, prior_total[group_index, 1], precision=highest
        )
        attended_list.append(numerator / denominator[:, :, None])
        denominator_list.append(denominator)
    attended = jnp.stack(attended_list)
    attended_low = attended.reshape(rows_all, model_width).astype(jnp.bfloat16)
    branch_one = jnp.dot(attended_low, out_weight, preferred_element_type=jnp.float32)
    residual_one = tokens.astype(jnp.float32) + branch_one
    first_norm, norm_one_back = jax.vjp(layer_norm, residual_one, norm_params[0], norm_params[1])
    first_low = first_norm.astype(jnp.bfloat16)
    hidden = jnp.dot(first_low, up_full, preferred_element_type=jnp.float32)
    activated, gelu_back = jax.vjp(jax.nn.gelu, hidden)
    activated_low = activated.astype(jnp.bfloat16)
    branch_two = jnp.dot(activated_low, down_full, preferred_element_type=jnp.float32)
    result, norm_two_back = jax.vjp(
        layer_norm, first_norm + branch_two, norm_params[2], norm_params[3]
    )
    layer_output = result.astype(jnp.bfloat16).reshape(groups, piece_rows, model_width)
    grad_residual_two, grad_gain_two, grad_bias_two = norm_two_back(
        cotangent.reshape(rows_all, model_width).astype(jnp.float32)
    )
    grad_branch_two = grad_residual_two.astype(jnp.bfloat16)
    grad_down = jnp.einsum(
        "nf,nd->fd", activated_low, grad_branch_two, preferred_element_type=jnp.float32
    )
    grad_activated = jnp.einsum(
        "nd,fd->nf", grad_branch_two, down_full, preferred_element_type=jnp.float32
    )
    grad_hidden = gelu_back(grad_activated)[0].astype(jnp.bfloat16)
    grad_up = jnp.einsum("nd,nf->df", first_low, grad_hidden, preferred_element_type=jnp.float32)
    grad_first = grad_residual_two + jnp.einsum(
        "nf,df->nd", grad_hidden, up_full, preferred_element_type=jnp.float32
    )
    grad_residual_one, grad_gain_one, grad_bias_one = norm_one_back(grad_first)
    grad_branch_one = grad_residual_one.astype(jnp.bfloat16)
    grad_out_weight = jnp.einsum(
        "nd,ne->de", attended_low, grad_branch_one, preferred_element_type=jnp.float32
    )
    grad_attended = jnp.einsum(
        "ne,de->nd", grad_branch_one, out_weight, preferred_element_type=jnp.float32
    ).reshape(shape_four)
    grad_qcos_list = []
    grad_qsin_list = []
    grad_kcos_list = []
    grad_ksin_list = []
    grad_values_list = []
    prior_grad_state = []
    prior_grad_total = []
    for group_index in range(groups):
        denominator = denominator_list[group_index]
        grad_numerator = (grad_attended[group_index] / denominator[:, :, None]).astype(jnp.bfloat16)
        grad_denominator = (
            -jnp.sum(grad_attended[group_index] * attended[group_index], axis=-1) / denominator
        )
        scores = piece_scores(
            query_cos[group_index],
            query_sin[group_index],
            key_cos[group_index],
            key_sin[group_index],
            causal,
        )
        grad_scores = (
            jnp.einsum(
                "ihe,jhe->hij",
                grad_numerator,
                values[group_index],
                preferred_element_type=jnp.float32,
            )
            + grad_denominator.T[:, :, None]
        )
        grad_scores = jnp.where(causal[None], grad_scores, 0.0).astype(jnp.bfloat16)
        grad_numerator_wide = grad_numerator.astype(jnp.float32)
        grad_qcos = jnp.einsum(
            "hij,jhe->ihe", grad_scores, key_cos[group_index], preferred_element_type=jnp.float32
        )
        grad_qcos = grad_qcos + jnp.einsum(
            "ihf,hef->ihe", grad_numerator_wide, prior_state[group_index, 0], precision=highest
        )
        grad_qcos = grad_qcos + grad_denominator[:, :, None] * prior_total[group_index, 0][None]
        grad_qsin = jnp.einsum(
            "hij,jhe->ihe", grad_scores, key_sin[group_index], preferred_element_type=jnp.float32
        )
        grad_qsin = grad_qsin + jnp.einsum(
            "ihf,hef->ihe", grad_numerator_wide, prior_state[group_index, 1], precision=highest
        )
        grad_qsin = grad_qsin + grad_denominator[:, :, None] * prior_total[group_index, 1][None]
        grad_qcos_list.append(grad_qcos)
        grad_qsin_list.append(grad_qsin)
        grad_kcos_list.append(
            jnp.einsum(
                "hij,ihe->jhe",
                grad_scores,
                query_cos[group_index],
                preferred_element_type=jnp.float32,
            )
        )
        grad_ksin_list.append(
            jnp.einsum(
                "hij,ihe->jhe",
                grad_scores,
                query_sin[group_index],
                preferred_element_type=jnp.float32,
            )
        )
        grad_values_list.append(
            jnp.einsum(
                "hij,ihe->jhe",
                scores.astype(jnp.bfloat16),
                grad_numerator,
                preferred_element_type=jnp.float32,
            )
        )
        prior_grad_state.append(
            jnp.stack(
                [
                    jnp.einsum(
                        "ihe,ihf->hef",
                        query_cos[group_index],
                        grad_numerator,
                        preferred_element_type=jnp.float32,
                    ),
                    jnp.einsum(
                        "ihe,ihf->hef",
                        query_sin[group_index],
                        grad_numerator,
                        preferred_element_type=jnp.float32,
                    ),
                ]
            )
        )
        prior_grad_total.append(
            jnp.stack(
                [
                    jnp.einsum(
                        "ihe,ih->he",
                        query_cos[group_index].astype(jnp.float32),
                        grad_denominator,
                        precision=highest,
                    ),
                    jnp.einsum(
                        "ihe,ih->he",
                        query_sin[group_index].astype(jnp.float32),
                        grad_denominator,
                        precision=highest,
                    ),
                ]
            )
        )
    later_state, later_total = carried_in(
        (jnp.stack(prior_grad_state), jnp.stack(prior_grad_total)),
        "seq",
        add_states,
        (identity[0], identity[1]),
    )
    values_wide = values.astype(jnp.float32)
    kcos_wide = key_cos.astype(jnp.float32)
    ksin_wide = key_sin.astype(jnp.float32)
    grad_kcos = (
        jnp.stack(grad_kcos_list)
        + jnp.einsum("gjhf,ghef->gjhe", values_wide, later_state[:, 0], precision=highest)
        + later_total[:, 0][:, None]
    )
    grad_ksin = (
        jnp.stack(grad_ksin_list)
        + jnp.einsum("gjhf,ghef->gjhe", values_wide, later_state[:, 1], precision=highest)
        + later_total[:, 1][:, None]
    )
    grad_values = jnp.stack(grad_values_list)
    grad_values = grad_values + jnp.einsum(
        "gjhe,ghef->gjhf", kcos_wide, later_state[:, 0], precision=highest
    )
    grad_values = grad_values + jnp.einsum(
        "gjhe,ghef->gjhf", ksin_wide, later_state[:, 1], precision=highest
    )
    grad_query = (
        jnp.stack(grad_qcos_list).reshape(rows_all, model_width) * cosine_weight
        + jnp.stack(grad_qsin_list).reshape(rows_all, model_width) * sine_weight
    )
    grad_keys = (
        grad_kcos.reshape(rows_all, model_width) * cosine_weight
        + grad_ksin.reshape(rows_all, model_width) * sine_weight
    )
    grad_projected = jnp.concatenate(
        [
            (grad_query * jax.nn.sigmoid(query_pre)).astype(jnp.bfloat16),
            (grad_keys * jax.nn.sigmoid(key_pre)).astype(jnp.bfloat16),
            grad_values.reshape(rows_all, model_width).astype(jnp.bfloat16),
        ],
        axis=1,
    )
    input_grad = grad_residual_one + jnp.einsum(
        "nk,dk->nd", grad_projected, project_in, preferred_element_type=jnp.float32
    )
    input_grad = input_grad.reshape(groups, piece_rows, model_width)
    grad_in = jnp.einsum("nd,nk->dk", tokens, grad_projected, preferred_element_type=jnp.float32)
    grad_attn = jnp.concatenate(
        [grad_in.reshape(model_width, 3, model_width), grad_out_weight[:, None, :]], axis=1
    )
    norm_grad_local = jnp.stack([grad_gain_one, grad_bias_one, grad_gain_two, grad_bias_two])
    norm_grad_raw = lax.psum(norm_grad_local, ("dp", "seq"))
    row_blocks = (
        lax.psum_scatter(
            grad_attn.astype(jnp.bfloat16), "dp", scatter_dimension=0, tiled=True
        ).astype(jnp.float32),
        lax.psum_scatter(
            grad_up.astype(jnp.bfloat16), "dp", scatter_dimension=0, tiled=True
        ).astype(jnp.float32),
        lax.psum_scatter(
            grad_down.astype(jnp.bfloat16), "dp", scatter_dimension=0, tiled=True
        ).astype(jnp.float32),
    )
    shard_attn, shard_up, shard_down = (
        lax.psum(row_blocks[0].astype(jnp.bfloat16), "seq").astype(jnp.float32),
        lax.psum(row_blocks[1].astype(jnp.bfloat16), "seq").astype(jnp.float32),
        lax.psum(row_blocks[2].astype(jnp.bfloat16), "seq").astype(jnp.float32),
    )
    local_square = (
        jnp.sum(shard_attn * shard_attn)
        + jnp.sum(shard_up * shard_up)
        + jnp.sum(shard_down * shard_down)
    )
    square = lax.psum(local_square, "dp") + jnp.sum(norm_grad_raw * norm_grad_raw)
    grad_norm = jnp.sqrt(square)
    clip_scale = clip_limit / jnp.maximum(grad_norm, clip_limit)
    attn_grad = shard_attn * clip_scale
    up_grad = shard_up * clip_scale
    down_grad = shard_down * clip_scale
    norm_grad = norm_grad_raw * clip_scale
    attn_rate = (
        learn_rate * jnp.array([1.0, 1.0, 1.0, math.sqrt(length // 8)], jnp.float32)[None, :, None]
    )
    attn_new, attn_first_new, attn_second_new = adamw(
        attn_master, attn_grad, attn_first, attn_second, attn_rate
    )
    up_new, up_first_new, up_second_new = adamw(up_master, up_grad, up_first, up_second, learn_rate)
    down_new, down_first_new, down_second_new = adamw(
        down_master, down_grad, down_first, down_second, learn_rate * math.sqrt(D / FF)
    )
    norm_new, norm_first_new, norm_second_new = adamw(
        norm_params, norm_grad, norm_first, norm_second, gain_rate
    )
    return (
        layer_output,
        input_grad,
        attn_grad,
        up_grad,
        down_grad,
        norm_grad,
        grad_norm,
        attn_new,
        up_new,
        down_new,
        norm_new,
        attn_first_new,
        up_first_new,
        down_first_new,
        norm_first_new,
        attn_second_new,
        up_second_new,
        down_second_new,
        norm_second_new,
    )


def fused_shards(
    layer_input, cotangent, attn_master, up_master, down_master, norm_params,
    attn_first, up_first, down_first, norm_first,
    attn_second, up_second, down_second, norm_second,
):
    groups, piece_rows, model_width = layer_input.shape
    seq_count = lax.axis_size("seq")
    rows = groups * piece_rows
    weights = (attn_master, up_master, down_master, norm_params)
    saved = forward_call(
        layer_input.reshape(rows, model_width), cotangent.reshape(rows, model_width),
        *weights, seq_count,
    )
    input_grad, attn, up, down, norm_raw, square = backward_call(saved, norm_params, seq_count)
    raw = (attn.reshape(4, -1, D), up.reshape(-1, FF), down.reshape(D, -1))
    layer_output, input_grad, *outs = update_call(
        saved["out"], input_grad, raw, norm_raw, square, weights,
        (attn_first, up_first, down_first, norm_first),
        (attn_second, up_second, down_second, norm_second), piece_rows * seq_count,
    )
    return (
        layer_output.reshape(layer_input.shape), input_grad.reshape(layer_input.shape),
        *outs[:4], outs[4].reshape(()), *outs[5:],
    )


def shards(*args):
    groups, piece_rows, model_width = args[0].shape
    planes = lax.axis_size("dp") // 2
    if piece_rows == PIECE and planes == PLANES and lax.axis_size("seq") == 4:
        return fused_shards(*args)
    return plain_shards(*args)


def solution(mesh):
    in_specs = (
        P("dp", "seq", None),
        P("dp", "seq", None),
        P("dp", None, None),
        P("dp", None),
        P("dp", None),
        P(),
        P("dp", None, None),
        P("dp", None),
        P("dp", None),
        P(),
        P("dp", None, None),
        P("dp", None),
        P("dp", None),
        P(),
    )
    out_specs = (
        P("dp", "seq", None),
        P("dp", "seq", None),
        P("dp", None, None),
        P("dp", None),
        P("dp", None),
        P(),
        P(),
        P("dp", None, None),
        P("dp", None),
        P("dp", None),
        P(),
        P("dp", None, None),
        P("dp", None),
        P("dp", None),
        P(),
        P("dp", None, None),
        P("dp", None),
        P("dp", None),
        P(),
    )
    return jax.shard_map(shards, mesh=mesh, in_specs=in_specs, out_specs=out_specs, check_vma=False)
```

```python
import functools
import math

import jax
import jax.numpy as jnp
import numpy as np
from jax import lax
from jax.experimental import pallas as pl
from jax.experimental.pallas import tpu as pltpu
from jax.sharding import PartitionSpec as P

D = 768
HEAD = 64
FF = 3072
STEP = 5


highest = lax.Precision.HIGHEST
beta_one = 0.5
beta_two = 0.5
learn_rate = 0.02
gain_rate = 0.2
epsilon = 1e-08
weight_decay = 0.01
norm_eps = 1e-05
clip_limit = 1.0


MESH = pl.DeviceIdType.MESH
f32, bf16 = jnp.float32, jnp.bfloat16
PIECE = 512
PAIR = 2 * HEAD
PLANES = 4
VMEM_BYTES = 63 * 1024 * 1024


def dot(left, right):
    return jnp.dot(left, right, preferred_element_type=f32)


def dot_nt(left, right):
    return lax.dot_general(left, right, (((1,), (1,)), ((), ())), preferred_element_type=f32)


def dot_tn(left, right):
    return lax.dot_general(left, right, (((0,), (0,)), ((), ())), preferred_element_type=f32)


def first_half(shape):
    return lax.broadcasted_iota(jnp.int32, shape, 1) < HEAD


def top_half(shape):
    return lax.broadcasted_iota(jnp.int32, shape, 0) < HEAD


def own_head(value, head):
    mask = first_half(value.shape)
    zero = jnp.zeros_like(value)
    return jnp.where(mask, value, zero) if head == 0 else jnp.where(mask, zero, value)


def two_heads(first, second):
    return jnp.where(first_half(first.shape), first, second)


def pair_mask(shape):
    return (lax.broadcasted_iota(jnp.int32, shape, 1) & (PAIR - 1)) < HEAD


def stack_heads(value):
    mask, zero = pair_mask(value.shape), jnp.zeros_like(value)
    return jnp.concatenate([jnp.where(mask, value, zero), jnp.where(mask, zero, value)], axis=0)


def join_heads(stacked):
    first, second = stacked[: stacked.shape[0] // 2], stacked[stacked.shape[0] // 2 :]
    return jnp.where(pair_mask(first.shape), first, second)


def side_by_side(wide):
    half = wide.shape[1] // 2
    return jnp.concatenate([wide[:, :half], wide[:, half:]], axis=0)


def fill_triangles(tri_s):
    half = tri_s.shape[1]
    row = lax.broadcasted_iota(jnp.int32, (half, half), 0)
    col = lax.broadcasted_iota(jnp.int32, (half, half), 1)
    tri_s[0:half] = (row >= col).astype(f32).astype(bf16)
    tri_s[half:] = (row <= col).astype(f32).astype(bf16)


def causal_product(own, other, right, tri_s):
    half = PIECE // 2
    tri = jnp.concatenate([tri_s[0:half], tri_s[0:half]], axis=0)
    tops, lows = stack_heads(own[0:half]), stack_heads(own[half:])
    first = dot_nt(jnp.concatenate([tops, lows], axis=0), other[0:half]).astype(bf16)
    near = dot_nt(lows, other[half:]).astype(bf16) * tri
    first = jnp.concatenate([first[:PIECE] * tri, first[PIECE:]], axis=0)
    out = dot(first, right[0:half])
    low = out[PIECE:] + dot(near, right[half:])
    return jnp.concatenate([join_heads(out[:PIECE]), join_heads(low)], axis=0)


def causal_transposed(own, other, right, tri_s):
    half = PIECE // 2
    tri = jnp.concatenate([tri_s[half:], tri_s[half:]], axis=1)
    top = dot_nt(other[0:half], stack_heads(own[0:half])).astype(bf16) * tri
    low = dot_nt(other, stack_heads(own[half:])).astype(bf16)
    low = jnp.concatenate([low[0:half], low[half:] * tri], axis=0)
    out = dot(side_by_side(low), right[half:])
    more = dot(side_by_side(top), right[0:half])
    first = jnp.concatenate([out[0:half] + more[0:half], out[half:PIECE]], axis=0)
    second = jnp.concatenate([out[PIECE : PIECE + half] + more[half:], out[PIECE + half :]], axis=0)
    return jnp.where(pair_mask(first.shape), first, second)


def with_ones(value):
    return jnp.concatenate([value, jnp.ones_like(value)], axis=1)


def turned(value, trig):
    wide = value.astype(f32)
    cos, sin = trig[:, :PAIR], trig[:, PAIR:]
    return jnp.concatenate([(wide * cos).astype(bf16), (wide * sin).astype(bf16)], axis=1)


def squeeze_state(state, totals):
    cos = two_heads(state[0:HEAD], state[HEAD : 2 * HEAD])
    sin = two_heads(state[2 * HEAD : 3 * HEAD], state[3 * HEAD :])
    row = lax.broadcasted_iota(jnp.int32, (16, PAIR), 0)
    sums = jnp.where(row == 0, totals[:, :PAIR], totals[:, PAIR:])
    return jnp.concatenate([cos, sin, sums], axis=0)


def spread_state(packed):
    cos, sin = packed[0:HEAD], packed[HEAD:PAIR]
    state = jnp.concatenate(
        [own_head(cos, 0), own_head(cos, 1), own_head(sin, 0), own_head(sin, 1)], axis=0
    )
    row = lax.broadcasted_iota(jnp.int32, (16, PAIR), 0)
    sums = packed[PAIR:]
    ones = jnp.ones((16, PAIR), bf16)
    blocks = []
    for kind in range(2):
        column = dot_tn(jnp.where(row == kind, sums, jnp.zeros_like(sums)), ones).astype(bf16)
        blocks += [own_head(column[0:HEAD], 0), own_head(column[HEAD:], 1)]
    return jnp.concatenate([state, jnp.concatenate(blocks, axis=0)], axis=1)


def normed(value):
    centered = value - jnp.mean(value, axis=-1, keepdims=True)
    rstd = lax.rsqrt(jnp.mean(centered * centered, axis=-1, keepdims=True) + norm_eps)
    return centered * rstd, rstd


def norm_back(grad, unit, rstd):
    mean = jnp.mean(grad, axis=-1, keepdims=True)
    along = jnp.mean(grad * unit, axis=-1, keepdims=True)
    return rstd * (grad - mean - unit * along)


class Place:
    def __init__(self):
        dp, seq = lax.axis_index("dp"), lax.axis_index("seq")
        self.z, self.y, self.x, self.c = dp // 2, dp % 2, seq // 2, seq % 2
        self.shard = dp

    def device(self, z=None, y=None, x=None, c=None):
        z = self.z if z is None else z
        y = self.y if y is None else y
        x = self.x if x is None else x
        c = self.c if c is None else c
        return {"dp": z * 2 + y, "seq": x * 2 + c}

    def plane(self, shift):
        return lax.rem(self.z + shift + PLANES, PLANES)

    def across_y(self):
        return self.device(y=1 - self.y)

    def across_x(self):
        return self.device(x=1 - self.x)

    def across_c(self):
        return self.device(c=1 - self.c)

    def neighbours(self):
        planes = [self.device(z=self.plane(step)) for step in range(1, PLANES)]
        return planes + [self.across_y(), self.across_x(), self.across_c()]

    def corners(self):
        y, x, c = 1 - self.y, 1 - self.x, 1 - self.c
        return [
            self.device(x=x, c=c), self.device(y=y, c=c),
            self.device(y=y, x=x), self.device(y=y, x=x, c=c),
        ]

    def in_plane(self):
        return (self.y * 2 + self.x) * 2 + self.c


def greet(place, corners=False):
    barrier = pltpu.get_barrier_semaphore()
    peers = place.neighbours() + (place.corners() if corners else [])
    for peer in peers:
        pl.semaphore_signal(barrier, inc=1, device_id=peer, device_id_type=MESH)
    pl.semaphore_wait(barrier, len(peers))


class Engine:
    RATES = {"x": 30e3, "y": 30e3, "z": 23e3, "c": 200e3}

    def __init__(self, scale=1.0):
        self.now, self.free, self.scale = 0.0, dict.fromkeys(self.RATES, 0.0), scale
        self.eta, self.tasks, self.done = {}, [], set()

    def sent(self, key, link, size):
        self.now += 0.04
        start = max(self.now, self.free[link])
        self.free[link] = start + size / self.RATES[link]
        self.eta[key] = self.free[link] + 1.5

    def add(self, needs, act, mark=None, cost=0.05):
        self.tasks.append((needs, act, mark, cost))

    def due(self, task):
        return max((self.eta.get(key, math.inf) for key in task[0]), default=0.0)

    def run(self, task):
        self.tasks.remove(task)
        self.now = max(self.now, self.due(task)) + task[3]
        task[1]()
        if task[2] is not None:
            self.done.add(task[2])

    def tick(self, cost):
        self.now += self.scale * cost
        while self.tasks:
            task = min(self.tasks, key=self.due)
            if self.due(task) > self.now:
                return
            self.run(task)

    def until(self, *marks):
        while not self.done.issuperset(marks):
            self.run(min(self.tasks, key=self.due))

    def rest(self):
        while self.tasks:
            self.run(min(self.tasks, key=self.due))


class Gather:
    def __init__(self, place, engine, chunks, send, recv, ready):
        self.place, self.engine, self.chunks = place, engine, chunks
        self.send, self.recv, self.sent, self.ready = send, recv, [], ready
        for k in range(len(chunks)):
            self.plan(k)

    def piece(self, k, z, y, x, c):
        ref, stride, base, height, column, width = self.chunks[k]
        row = (z * 2 + y) * stride + base + c * height
        return ref.at[
            pl.ds(pl.multiple_of(row, 16), height),
            pl.ds(pl.multiple_of(column + x * width, 128), width),
        ]

    def copy(self, k, index, ref, device):
        return pltpu.make_async_remote_copy(
            src_ref=ref,
            dst_ref=ref,
            send_sem=self.send.at[k, index],
            recv_sem=self.recv.at[k, index],
            device_id=device,
            device_id_type=MESH,
        )

    def push(self, k, index, ref, device, link):
        copy = self.copy(k, index, ref, device)
        copy.start()
        self.sent.append(copy)
        self.engine.sent((k, index), link, 2 * self.chunks[k][3] * self.chunks[k][5])

    def pull(self, k, index, ref):
        self.copy(k, index, ref, self.place.across_c()).wait_recv()

    def twin(self, k, index, ref):
        self.push(k, 14 + index, ref, self.place.across_c(), "c")

    def begin(self, k):
        p = self.place
        self.ready(k)
        own = self.piece(k, p.z, p.y, p.x, p.c)
        for step in (1, 3, 2):
            self.push(k, step - 1, own, p.device(z=p.plane(step)), "z")
        self.push(k, 3, own, p.across_y(), "y")
        other = self.piece(k, p.z, p.y, 1 - p.x, p.c)
        self.push(k, 10, other, p.across_y(), "y")
        self.push(k, 7, other, p.device(z=p.plane(1)), "z")

    def from_plane(self, k, step):
        p = self.place
        ref = self.piece(k, p.plane(-step), p.y, p.x, p.c)
        self.pull(k, step - 1, ref)
        self.push(k, 3 + step, ref, p.across_y(), "y")
        if step != 1:
            self.push(k, 6 + step, ref, p.across_x(), "x")
        self.twin(k, step - 1, ref)

    def by_y(self, k):
        return (1, 3) if k == 6 else ()

    def from_y(self, k, step):
        p = self.place
        ref = self.piece(k, p.plane(-step), 1 - p.y, p.x, p.c)
        self.pull(k, 3 + step, ref)
        if step and step not in self.by_y(k):
            self.push(k, 10 + step, ref, p.across_x(), "x")
        self.twin(k, 3 + step, ref)

    def from_x(self, k, step):
        p = self.place
        ref = self.piece(k, p.plane(-step), p.y, 1 - p.x, p.c)
        self.pull(k, 6 + step, ref)
        if step in self.by_y(k):
            self.push(k, 10 + step, ref, p.across_y(), "y")
        self.twin(k, 6 + step, ref)

    def corner(self, k, step):
        p = self.place
        ref = self.piece(k, p.plane(-step), 1 - p.y, 1 - p.x, p.c)
        self.pull(k, 10 + step, ref)
        self.twin(k, 10 + step, ref)

    def finish(self, k):
        p = self.place
        far = 1 - p.c
        for step in range(PLANES):
            z = p.plane(-step)
            if step:
                self.pull(k, 14 + step - 1, self.piece(k, z, p.y, p.x, far))
                self.pull(k, 20 + step, self.piece(k, z, p.y, 1 - p.x, far))
            self.pull(k, 17 + step, self.piece(k, z, 1 - p.y, p.x, far))
            self.pull(k, 24 + step, self.piece(k, z, 1 - p.y, 1 - p.x, far))

    def plan(self, k):
        before = [(k - 2, at) for at in range(3)] if k > 1 else []
        add = self.engine.add
        add(before, functools.partial(self.begin, k))
        for step in (1, 3, 2):
            add([(k, step - 1)], functools.partial(self.from_plane, k, step))
            add([(k, 6 + step)], functools.partial(self.from_x, k, step))
        for step in (0, 1, 3, 2):
            add([(k, 3 + step)], functools.partial(self.from_y, k, step))
            add([(k, 10 + step)], functools.partial(self.corner, k, step))
        add([(k, 14 + at) for at in range(14)], functools.partial(self.finish, k), k, 0.3)

    def drain(self):
        for copy in self.sent:
            copy.wait_send()


def ds(start, size, unit):
    return pl.ds(pl.multiple_of(start, unit), size)


def turn_over(source, target):
    for at in range(0, source.shape[0], 256):
        target[:, at : at + 256] = source[at : at + 256, :].T


def block_of(b):
    return ds((b // 6) * PIECE, PIECE, PIECE), ds(lax.rem(b, 6) * PAIR, PAIR, PAIR)


def forward_kernel(
    x_h, cot_h, attn_h, up_h, down_h, norm_h, trig_h,
    wqkv_o, wo_o, wup_o, wdn_o, q_o, k_o, v_o, att_o, rden_o, xhat_o, rstd_o, xt_o, att_t_o,
    low_t_o, act_o, slope_o, gb_o, gb_t_o, gr2_o, out_o, state_o, sums_o,
    wqkv, wo, wup, wdn, attn_st, up_st, down_st, x_s, cot_s, norm_s, trig_s, tri_s,
    q_s, k_s, v_s, num_s, den_s, att_s, xhat_s, rstd_s, low_s, act_s, slope_a, slope_b, hid_a, hid_b, out_s,
    x_t_s, att_t_s, low_t_s, sums_s, st_own, st_twin, st_chip, st_prior,
    load_sem, store_sem, tile_sem, g_send, g_recv, st_send, st_recv,
):
    place = Place()
    shard, x, c = place.shard, place.x, place.c
    groups = x_s.shape[0] // PIECE
    blocks = groups * 6
    loads = []
    for at, (src, dst) in enumerate(
        [
            (attn_h, attn_st), (up_h, up_st), (down_h, down_st), (x_h, x_s), (norm_h, norm_s),
            (trig_h.at[ds((x * 2 + c) * PIECE, PIECE, PIECE), :], trig_s), (cot_h, cot_s),
        ]
    ):
        copy = pltpu.make_async_copy(src, dst, load_sem.at[at])
        copy.start()
        loads.append(copy)
    stores = []

    def store(src, dst):
        copy = pltpu.make_async_copy(src, dst, store_sem.at[len(stores)])
        copy.start()
        stores.append(copy)

    thin, thick = attn_st.shape[0], down_st.shape[0]
    chunks = [
        (wqkv, thin, 0, thin // 2, D, D),
        (wqkv, thin, 0, thin // 2, 0, D // 2),
        (wo, thin, 0, thin // 2, 0, D // 2),
        (wup, thin, 0, thin // 2, 0, FF // 4),
        (wup, thin, 0, thin // 2, FF // 2, FF // 4),
        (wdn, thick, 0, thick // 2, 0, D // 3),
        (wdn, thick, 0, thick // 2, 2 * D // 3, D // 6),
    ]
    def ready(k):
        narrow = ds(shard * thin, thin, 32)
        if k == 0:
            loads[0].wait()
            for j in (1, 2):
                wqkv[narrow, j * D : (j + 1) * D] = attn_st[:, j, :].astype(bf16)
        elif k == 1:
            wqkv[narrow, 0:D] = attn_st[:, 0, :].astype(bf16)
        elif k == 2:
            wo[narrow, :] = attn_st[:, 3, :].astype(bf16)
        elif k == 3:
            loads[1].wait()
            wup[narrow, :] = up_st[...].astype(bf16)
        elif k == 5:
            loads[2].wait()
            wdn[ds(shard * thick, thick, 128), :] = down_st[...].astype(bf16)

    engine = Engine()
    gather = Gather(place, engine, chunks, g_send, g_recv, ready)
    greet(place)
    engine.tick(0.0)
    fill_triangles(tri_s)
    for copy in loads[3:6]:
        copy.wait()
    turn_over(x_s, x_t_s)
    store(x_t_s, xt_o)
    engine.tick(3.0)
    engine.until(0)

    hidden = (hid_a, hid_b)

    def chain(products, finish, cost):
        hidden[0][...] = products[0]()
        for t in range(len(products)):
            if t + 1 < len(products):
                hidden[(t + 1) % 2][...] = products[t + 1]()
            finish(t, hidden[t % 2])
            engine.tick(cost)

    def project(parts):
        tiles = [(target, column, t, soft) for target, column, soft in parts for t in range(3)]

        def product(target, column, t, soft):
            return dot(x_s[...], wqkv[:, column + 256 * t : column + 256 * t + 256])

        def finish(at, pre):
            target, _, t, soft = tiles[at]
            pre = pre[...]
            if soft:
                pre = jnp.maximum(pre, 0.0) + jnp.log1p(jnp.exp(-jnp.abs(pre)))
            target[:, 256 * t : 256 * t + 256] = pre.astype(bf16)

        chain([functools.partial(product, *tile) for tile in tiles], finish, 0.7)

    project([(k_s, D, True), (v_s, 2 * D, False)])

    def local(b, carry):
        rows, cols = ds((b // 6) * PIECE, PIECE, PIECE), ds(lax.rem(b, 6) * PAIR, PAIR, PAIR)
        keys = turned(k_s[rows, cols], trig_s[...])
        state = dot_tn(keys, v_s[rows, cols])
        totals = dot(jnp.ones((16, PIECE), bf16), keys)
        st_own[b] = squeeze_state(state, totals).astype(bf16)
        return carry

    for part in range(0, blocks, 4):
        lax.fori_loop(part, part + 4, local, 0)
        engine.tick(1.4)
    state = StateSum(place, engine, st_send, st_recv, st_own, st_twin, st_chip, st_prior, False)
    engine.tick(0.0)
    engine.until(1)
    project([(q_s, 0, True)])
    store(wqkv, wqkv_o)
    store(q_s, q_o)
    store(k_s, k_o)
    store(v_s, v_o)

    def intra(i, carry):
        spots = [block_of(2 * i), block_of(2 * i + 1)]
        taken = [(q_s[at], k_s[at], v_s[at]) for at in spots]
        outs = [
            causal_product(
                turned(q, trig_s[...]), turned(k, trig_s[...]), with_ones(v), tri_s
            )
            for q, k, v in taken
        ]
        for at, out in zip(spots, outs):
            num_s[at] = out[:, :PAIR]
            den_s[at] = out[:, PAIR:]
        return carry

    for part in range(blocks // 2):
        lax.fori_loop(part, part + 1, intra, 0)
        engine.tick(1.6)
    engine.until("state")

    def inter(i, carry):
        spots = [block_of(2 * i), block_of(2 * i + 1)]
        states = [state.total(2 * i + at).astype(bf16) for at in range(2)]
        taken = [(q_s[at], num_s[at], den_s[at]) for at in spots]
        outs = []
        for (q, num, den), packed in zip(taken, states):
            more = dot(turned(q, trig_s[...]), spread_state(packed))
            recip = 1.0 / (den + more[:, PAIR:])
            outs.append((((num + more[:, :PAIR]) * recip).astype(bf16), recip))
        for at, (attended, recip) in zip(spots, outs):
            att_s[at] = attended
            den_s[at] = recip
        for at, packed in enumerate(states):
            st_chip[2 * i + at] = packed
        return carry

    for part in range(0, blocks // 2, 2):
        lax.fori_loop(part, part + 2, inter, 0)
        engine.tick(1.6)
    store(att_s, att_o)
    store(den_s, rden_o)
    turn_over(att_s, att_t_s)
    store(att_t_s, att_t_o)
    store(st_chip, state_o)
    engine.tick(1.0)
    engine.until(2)
    store(wo, wo_o)

    gain_one, bias_one = norm_s[0:1, :], norm_s[1:2, :]
    tile = 256

    def join(t, carry):
        cols = ds(t * tile, tile, tile)
        xhat_s[:, cols] = x_s[:, cols].astype(f32) + dot(att_s[...], wo[:, cols])
        return carry

    def join_norm(t, carry):
        rows = ds(t * tile, tile, tile)
        unit, rstd = normed(xhat_s[rows, :])
        xhat_s[rows, :] = unit
        rstd_s[rows, :] = jnp.broadcast_to(rstd, (tile, 128))
        low_s[rows, :] = (unit * gain_one + bias_one).astype(bf16)
        return carry

    for t in range(D // tile):
        lax.fori_loop(t, t + 1, join, 0)
        engine.tick(0.7)
    for part in range(x_s.shape[0] // tile):
        lax.fori_loop(part, part + 1, join_norm, 0)
        engine.tick(0.4)
    store(xhat_s, xhat_o)
    store(rstd_s, rstd_o)
    turn_over(low_s, low_t_s)
    store(low_t_s, low_t_o)
    engine.tick(1.0)
    engine.until(3)

    slopes, scale = (slope_a, slope_b), math.sqrt(2.0 / math.pi)

    def slope_copy(t):
        return pltpu.make_async_copy(
            slopes[t % 2], slope_o.at[:, 256 * t : 256 * t + 256], tile_sem.at[t % 2]
        )

    def expand(t, value):
        if t >= 2:
            slope_copy(t - 2).wait()
        value = value[...]
        squared = value * value
        curve = jnp.tanh(value * (scale + (scale * 0.044715) * squared))
        half = 0.5 + 0.5 * curve
        active = value * half
        slope = half + active * (1.0 - curve) * (scale + (3.0 * scale * 0.044715) * squared)
        act_s[:, 256 * t : 256 * t + 256] = active.astype(bf16)
        if t % 3 == 2:
            span = slice(256 * t - 512, 256 * t + 256)
            store(act_s.at[:, span], act_o.at[:, span])
        slopes[t % 2][...] = slope.astype(bf16)
        slope_copy(t).start()

    def raised(t):
        if t == 6:
            engine.until(4)
            store(wup, wup_o)
        return dot(low_s[...], wup[:, 256 * t : 256 * t + 256])

    chain([functools.partial(raised, t) for t in range(FF // 256)], expand, 1.1)
    loads[6].wait()
    sums_s[...] = jnp.zeros_like(sums_s)
    gain_two, bias_two = norm_s[2:3, :], norm_s[3:4, :]

    def contract(t):
        cols = slice(tile * t, tile * t + tile)
        num_s[:, cols] = dot(act_s[...], wdn[:, cols])
        engine.tick(2.5)

    engine.until(5)
    store(wdn.at[:, 0 : 2 * tile], wdn_o.at[:, 0 : 2 * tile])
    contract(0)
    contract(1)
    engine.until(6)
    store(wdn.at[:, 2 * tile :], wdn_o.at[:, 2 * tile :])
    contract(2)

    def contract_norm(t, carry):
        rows = ds(t * tile, tile, tile)
        unit, rstd = normed(xhat_s[rows, :] * gain_one + bias_one + num_s[rows, :])
        out_s[rows, :] = (unit * gain_two + bias_two).astype(bf16)
        cot = cot_s[rows, :].astype(f32)
        sums_s[0:1, :] += jnp.sum(cot * unit, axis=0, keepdims=True)
        sums_s[1:2, :] += jnp.sum(cot, axis=0, keepdims=True)
        grad = norm_back(cot * gain_two, unit, rstd)
        num_s[rows, :] = grad
        low_s[rows, :] = grad.astype(bf16)
        return carry

    stores[0].wait()
    for t in range(x_s.shape[0] // tile):
        span = slice(tile * t, tile * t + tile)
        lax.fori_loop(t, t + 1, contract_norm, 0)
        x_t_s[:, span] = low_s[span, :].T
        store(num_s.at[span, :], gr2_o.at[span, :])
        store(low_s.at[span, :], gb_o.at[span, :])
        store(out_s.at[span, :], out_o.at[span, :])
    store(x_t_s, gb_t_o)
    store(sums_s, sums_o)
    for copy in stores[1:] + [slope_copy(10), slope_copy(11)]:
        copy.wait()
    gather.drain()
    state.drain()


def forward_call(tokens, cotangent, attn_master, up_master, down_master, norm_params, seq_count):
    rows = tokens.shape[0]
    blocks = rows // PIECE * 6
    thin, thick = attn_master.shape[0], down_master.shape[0]
    trig = turning_table(seq_count)
    shapes = dict(
        wqkv=((D, 3 * D), bf16), wo=((D, D), bf16), wup=((D, FF), bf16), wdn=((FF, D), bf16),
        q=((rows, D), bf16), k=((rows, D), bf16), v=((rows, D), bf16), att=((rows, D), bf16),
        rden=((rows, D), f32), xhat=((rows, D), f32), rstd=((rows, 128), f32),
        x_t=((D, rows), bf16), att_t=((D, rows), bf16), low_t=((D, rows), bf16),
        act=((rows, FF), bf16), slope=((rows, FF), bf16), gb=((rows, D), bf16),
        gb_t=((D, rows), bf16),
        gr2=((rows, D), f32), out=((rows, D), bf16), state=((blocks, 144, PAIR), bf16),
        sums=((8, D), f32),
    )
    out_shape = [jax.ShapeDtypeStruct(s, d) for s, d in shapes.values()]
    hbm = pl.BlockSpec(memory_space=pl.ANY)
    scratch = [
        pltpu.VMEM((D, 3 * D), bf16), pltpu.VMEM((D, D), bf16),
        pltpu.VMEM((D, FF), bf16), pltpu.VMEM((FF, D), bf16),
        pltpu.VMEM((thin, 4, D), f32), pltpu.VMEM((thin, FF), f32), pltpu.VMEM((thick, D), f32),
        pltpu.VMEM((rows, D), bf16), pltpu.VMEM((rows, D), bf16), pltpu.VMEM((4, D), f32),
        pltpu.VMEM((PIECE, 2 * PAIR), f32), pltpu.VMEM((PIECE, PIECE // 2), bf16),
        pltpu.VMEM((rows, D), bf16), pltpu.VMEM((rows, D), bf16), pltpu.VMEM((rows, D), bf16),
        pltpu.VMEM((rows, D), f32), pltpu.VMEM((rows, D), f32), pltpu.VMEM((rows, D), bf16),
        pltpu.VMEM((rows, D), f32), pltpu.VMEM((rows, 128), f32), pltpu.VMEM((rows, D), bf16),
        pltpu.VMEM((rows, FF), bf16), pltpu.VMEM((rows, 256), bf16),
        pltpu.VMEM((rows, 256), bf16), pltpu.VMEM((rows, 256), f32),
        pltpu.VMEM((rows, 256), f32), pltpu.VMEM((rows, D), bf16),
        pltpu.VMEM((D, rows), bf16), pltpu.VMEM((D, rows), bf16), pltpu.VMEM((D, rows), bf16),
        pltpu.VMEM((8, D), f32),
        pltpu.VMEM((blocks, 144, PAIR), bf16), pltpu.VMEM((blocks, 144, PAIR), bf16),
        pltpu.VMEM((blocks, 144, PAIR), bf16), pltpu.VMEM((blocks, 144, PAIR), bf16),
        pltpu.SemaphoreType.DMA((8,)), pltpu.SemaphoreType.DMA((40,)),
        pltpu.SemaphoreType.DMA((2,)),
        pltpu.SemaphoreType.DMA((7, 28)), pltpu.SemaphoreType.DMA((7, 28)),
        pltpu.SemaphoreType.DMA((3,)), pltpu.SemaphoreType.DMA((3,)),
    ]
    return dict(
        zip(
            shapes,
            pl.pallas_call(
                forward_kernel,
                out_shape=out_shape,
                in_specs=[hbm] * 7,
                out_specs=[hbm] * len(out_shape),
                scratch_shapes=scratch,
                compiler_params=pltpu.CompilerParams(
                    collective_id=0, has_side_effects=True, vmem_limit_bytes=VMEM_BYTES
                ),
                name="gather_forward",
            )(
                tokens, cotangent, attn_master, up_master, down_master, norm_params,
                trig,
            ),
        )
    )


def turning_table(seq_count):
    length = seq_count * PIECE
    angle = math.pi / 2 * np.arange(length, dtype=np.float64) / length
    trig = np.repeat(np.stack([np.cos(angle), np.sin(angle)], axis=1), PAIR, axis=1)
    return jnp.asarray(trig, f32)


class Share:
    def __init__(self, grad, first, units, column, width, by_units, early, z_first, bufs, out):
        self.grad, self.first, self.units = grad, first, units
        self.column, self.width, self.by_units, self.early = column, width, by_units, early
        self.count = units // 2 if by_units else units
        self.half = width if by_units else width // 2
        self.twin, self.from_x, self.from_y, self.via_x, self.via_y, self.planes, self.final = bufs
        self.out, self.z_first = out, z_first

    def side(self, x):
        if self.by_units:
            return x * self.count, slice(0, self.width)
        return 0, ds(x * self.half, self.half, 128)

    def part(self, x):
        first, lanes = self.side(x)
        return pl.ds(first, self.count), lanes


class Reduce:
    def __init__(self, place, engine, send, recv, store_sem, squares):
        self.place, self.engine, self.send, self.recv = place, engine, send, recv
        self.store_sem, self.squares = store_sem, squares
        self.sent, self.stored, self.count = [], [], 0

    def copy(self, k, index, src, dst, device):
        return pltpu.make_async_remote_copy(
            src_ref=src, dst_ref=dst, send_sem=self.send.at[k, index],
            recv_sem=self.recv.at[k, index], device_id=device, device_id_type=MESH,
        )

    def push(self, k, index, src, dst, device, link):
        copy = self.copy(k, index, src, dst, device)
        copy.start()
        self.sent.append((k, index, copy))
        self.engine.sent(("part", k, index), link, 2 * math.prod(dst.shape))

    def settle(self, parts):
        for k, index, copy in list(self.sent):
            if k in parts and index == 0:
                copy.wait_send()
                self.sent.remove((k, index, copy))

    def pull(self, k, index, dst):
        self.copy(k, index, dst, dst, self.place.across_c()).wait_recv()

    def launch(self, share):
        k = self.count
        self.count += 1
        src = share.grad.at[
            share.first : share.first + share.units, :, :, 1 - self.place.c, :,
            share.column : share.column + share.width,
        ]
        self.push(k, 0, src, share.twin, self.place.across_c(), "c")
        middle = [
            ((1, 2), self.fold_corner, None, 0.3),
            ((3, 4, 5, 6), self.fold_square, None, 0.4),
            ((7, 8, 9), self.fold_planes, "sum", 0.3),
        ]
        if share.z_first:
            middle = [
                ((1, 2, 3), self.first_planes, None, 0.3),
                ((4,), self.then_y, None, 0.1),
                ((5,), self.then_x, "sum", 0.1),
            ]
        for needs, act, mark, cost in [
            ((0,), self.fold_core, "core", 0.5),
            *middle,
            ((10,), self.share_x, None, 0.05),
            ((11,), self.share_c, "whole", 0.05),
        ]:
            keys = [("part", k, at) for at in needs]
            self.engine.add(keys, functools.partial(act, k, share), (mark, k), cost)

    def fold_core(self, k, s):
        p = self.place
        self.pull(k, 0, s.twin)
        own = s.grad[s.first : s.first + s.units, :, :, p.c, :, s.column : s.column + s.width]
        s.twin[...] = (s.twin[...].astype(f32) + own.astype(f32)).astype(bf16)
        e, oy, t = s.early, 1 - p.y, s.twin
        if s.z_first:
            for step in (1, 3, 2):
                z = p.plane(step)
                self.push(k, step, t.at[:, z], s.planes.at[:, step - 1], p.device(z=z), "z")
            return
        (mine, near), (theirs, far) = s.part(p.x), s.part(1 - p.x)
        self.push(k, 1, t.at[theirs, 0:e, oy, :, far], s.via_x, p.across_x(), "x")
        self.push(k, 2, t.at[theirs, e:PLANES, oy, :, far], s.via_y, p.across_y(), "y")
        self.push(
            k, 3, t.at[theirs, 0:e, p.y, :, far], s.from_x.at[:, 0:e], p.across_x(), "x"
        )
        self.push(
            k, 4, t.at[mine, e:PLANES, oy, :, near], s.from_y.at[:, e:PLANES], p.across_y(), "y"
        )

    def fold_corner(self, k, s):
        p, e, t, oy = self.place, s.early, s.twin, 1 - self.place.y
        (mine, near), (theirs, far) = s.part(p.x), s.part(1 - p.x)
        self.pull(k, 1, s.via_x)
        at = (mine, slice(0, e), oy, slice(None), near)
        t[at] = (t[at].astype(f32) + s.via_x[...].astype(f32)).astype(bf16)
        self.push(k, 5, t.at[mine, 0:e, oy, :, near], s.from_y.at[:, 0:e], p.across_y(), "y")
        self.pull(k, 2, s.via_y)
        at = (theirs, slice(e, PLANES), p.y, slice(None), far)
        t[at] = (t[at].astype(f32) + s.via_y[...].astype(f32)).astype(bf16)
        self.push(
            k, 6, t.at[theirs, e:PLANES, p.y, :, far], s.from_x.at[:, e:PLANES], p.across_x(), "x"
        )

    def fold_square(self, k, s):
        p, e, t = self.place, s.early, s.twin
        mine, near = s.part(p.x)
        self.pull(k, 3, s.from_x.at[:, 0:e])
        self.pull(k, 4, s.from_y.at[:, e:PLANES])
        self.pull(k, 5, s.from_y.at[:, 0:e])
        self.pull(k, 6, s.from_x.at[:, e:PLANES])
        at = (mine, slice(None), p.y, slice(None), near)
        total = t[at].astype(f32) + s.from_x[...].astype(f32) + s.from_y[...].astype(f32)
        t[at] = total.astype(bf16)
        for step in (1, 3, 2):
            z = p.plane(step)
            self.push(
                k, 6 + step, t.at[mine, z, p.y, :, near], s.planes.at[:, step - 1],
                p.device(z=z), "z",
            )

    def fold_planes(self, k, s):
        p = self.place
        mine, near = s.part(p.x)
        for step in (1, 3, 2):
            self.pull(k, 6 + step, s.planes.at[:, step - 1])
        total = s.twin[mine, p.z, p.y, :, near].astype(f32)
        for step in range(3):
            total = total + s.planes[:, step].astype(f32)
        self.own_sum(k, s, total.astype(bf16))

    def first_planes(self, k, s):
        p, t = self.place, s.twin
        for step in (1, 3, 2):
            self.pull(k, step, s.planes.at[:, step - 1])
        total = t[:, p.z].astype(f32)
        for step in range(3):
            total = total + s.planes[:, step].astype(f32)
        t[:, p.z] = total.astype(bf16)
        self.push(k, 4, t.at[:, p.z, 1 - p.y], s.from_y, p.across_y(), "y")

    def then_y(self, k, s):
        p, t = self.place, s.twin
        theirs, far = s.part(1 - p.x)
        self.pull(k, 4, s.from_y)
        total = t[:, p.z, p.y].astype(f32) + s.from_y[...].astype(f32)
        t[:, p.z, p.y] = total.astype(bf16)
        self.push(k, 5, t.at[theirs, p.z, p.y, :, far], s.from_x, p.across_x(), "x")

    def then_x(self, k, s):
        p = self.place
        mine, near = s.part(p.x)
        self.pull(k, 5, s.from_x)
        total = s.twin[mine, p.z, p.y, :, near].astype(f32) + s.from_x[...].astype(f32)
        self.own_sum(k, s, total.astype(bf16))

    def own_sum(self, k, s, total):
        p = self.place
        mine, near = s.part(p.x)
        s.final[mine, p.c, :, near] = total
        wide = total.astype(f32).reshape(s.count * 48, s.half)
        for lane in range(0, s.half, 128):
            part = wide[:, lane : lane + 128]
            self.squares[...] += jnp.sum((part * part).reshape(-1, 8, 128), axis=0)
        piece = s.final.at[mine, p.c, :, near]
        self.push(k, 10, piece, piece, p.across_x(), "x")

    def share_x(self, k, s):
        p = self.place
        theirs, far = s.part(1 - p.x)
        self.pull(k, 10, s.final.at[theirs, p.c, :, far])
        half = s.final.at[:, p.c]
        self.push(k, 11, half, half, p.across_c(), "c")

    def share_c(self, k, s):
        self.pull(k, 11, s.final.at[:, 1 - self.place.c])
        if s.out is not None:
            copy = pltpu.make_async_copy(s.final, s.out, self.store_sem.at[k])
            copy.start()
            self.stored.append(copy)

    def drain(self):
        for _, _, copy in self.sent:
            copy.wait_send()
        for copy in self.stored:
            copy.wait()


class Total:
    def __init__(self, place, engine, name, value, near, planes, send, recv):
        self.place, self.engine, self.name = place, engine, name
        self.value, self.near, self.planes = value, near, planes
        self.send, self.recv, self.sent = send, recv, []
        y, x, c = 1 - place.y, 1 - place.x, 1 - place.c
        peers = [place.across_c(), place.across_x(), place.across_y()] + place.corners()
        flips = [(0, 0, 1), (0, 1, 0), (1, 0, 0), (0, 1, 1), (1, 0, 1), (1, 1, 0), (1, 1, 1)]
        self.slots = [
            ((y if flip[0] else place.y) * 2 + (x if flip[1] else place.x)) * 2
            + (c if flip[2] else place.c)
            for flip in flips
        ]
        own = near.at[place.in_plane()]
        near[place.in_plane()] = value[...]
        for at, peer in enumerate(peers):
            self.push(at, own, peer, "cxyxyxy"[at])
        engine.add([(name, at) for at in range(7)], self.across)

    def copy(self, index, ref, device):
        return pltpu.make_async_remote_copy(
            src_ref=ref, dst_ref=ref, send_sem=self.send.at[index],
            recv_sem=self.recv.at[index], device_id=device, device_id_type=MESH,
        )

    def push(self, index, ref, device, link):
        copy = self.copy(index, ref, device)
        copy.start()
        self.sent.append(copy)
        self.engine.sent((self.name, index), link, 4 * math.prod(ref.shape))

    def across(self):
        p = self.place
        for at, slot in enumerate(self.slots):
            self.copy(at, self.near.at[slot], p.across_c()).wait_recv()
        total = self.near[0]
        for at in range(1, 8):
            total = total + self.near[at]
        self.planes[p.z] = total
        for step in (1, 3, 2):
            self.push(6 + step, self.planes.at[p.z], p.device(z=p.plane(step)), "z")
        self.engine.add([(self.name, at) for at in (7, 8, 9)], self.end, self.name)

    def end(self):
        for step in (1, 3, 2):
            own = self.planes.at[self.place.plane(-step)]
            self.copy(6 + step, own, self.place.across_c()).wait_recv()
        self.value[...] = (self.planes[0] + self.planes[1]) + (self.planes[2] + self.planes[3])

    def drain(self):
        for copy in self.sent:
            copy.wait_send()


class StateSum:
    def __init__(self, place, engine, send, recv, own, twin, chip, prior, late):
        self.x, self.c, self.engine = place.x, place.c, engine
        self.own, self.twin, self.chip, self.prior = own, twin, chip, prior
        self.giver, self.taker = (1, 0) if late else (0, 1)
        half = own.shape[0] // 2
        self.size = math.prod(own.shape)
        mine, other = ds(place.c * half, half, 1), ds((1 - place.c) * half, half, 1)

        def copy(index, src, dst, device):
            return pltpu.make_async_remote_copy(
                src_ref=src, dst_ref=dst, send_sem=send.at[index], recv_sem=recv.at[index],
                device_id=device, device_id_type=MESH,
            )

        self.swap = copy(0, own, twin, place.across_c())
        self.over = copy(1, chip.at[mine], prior.at[mine], place.across_x())
        self.pass_on = copy(2, prior.at[mine], prior.at[mine], place.across_c())
        self.taken = copy(2, prior.at[other], prior.at[other], place.across_c())
        self.swap.start()
        engine.sent("swap", "c", 2 * self.size)
        engine.add(["swap"], self.join, None, 0.5)
        engine.add(["over"], self.forward)
        engine.add(["pass"], self.end, "state")

    def join(self):
        self.swap.wait_recv()
        self.chip[...] = (self.own[...].astype(f32) + self.twin[...].astype(f32)).astype(bf16)

        @pl.when(self.x == self.giver)
        def _():
            self.over.start()

        self.engine.sent("over", "x", self.size)

    def forward(self):
        @pl.when(self.x == self.taker)
        def _():
            self.over.wait_recv()
            self.pass_on.start()

        self.engine.sent("pass", "c", self.size)

    def end(self):
        @pl.when(self.x == self.taker)
        def _():
            self.taken.wait_recv()

        @pl.when(self.x == self.giver)
        def _():
            self.over.wait_send()

    def drain(self):
        self.swap.wait_send()

        @pl.when(self.x == self.taker)
        def _():
            self.pass_on.wait_send()

    def total(self, b):
        far = jnp.where(self.x == self.taker, self.prior[b].astype(f32), 0.0)
        return far + jnp.where(self.c == self.taker, self.twin[b].astype(f32), 0.0)


def lane_in_head(shape):
    return lax.broadcasted_iota(jnp.int32, shape, 1) & (HEAD - 1)


def backward_kernel(
    wqkv_h, wo_h, wup_h, q_h, k_h, v_h, att_h, rden_h, xhat_h, rstd_h, x_t_h, att_t_h,
    low_t_h, act_h, slope_h, gb_h, gb_t_h, gr2_h, state_h, sums_h, wdn_h, norm_h, trig_h,
    input_o, attn_o, up_o, down_o, norm_o, square_o,
    wup, acts, slope, gr2, gb, left, wide, rstd, ga_s, gd_s, gu_s,
    norm_s, trig_s, tri_s, state_s, st_own, st_twin, st_chip, st_prior,
    norm_v, norm_w, norm_z, sq_v, sq_w, sq_z,
    *rest,
):
    bufs = rest[: 7 * SHARES]
    load_sem, store_sem, r_send, r_recv, s_send, s_recv = rest[7 * SHARES : 7 * SHARES + 6]
    t_send, t_recv, u_send, u_recv = rest[7 * SHARES + 6 :]
    place = Place()
    rows_all = gr2.shape[0]
    blocks = state_s.shape[0]
    tile = 256
    count = [0]

    def load(src, dst):
        copy = pltpu.make_async_copy(src, dst, load_sem.at[count[0]])
        count[0] += 1
        copy.start()
        return copy

    def wait(copies):
        for copy in copies:
            copy.wait()

    first_in = [load(gb_t_h, wup.at[:, 0:rows_all])]
    act_in = [load(act_h.at[:, D * z : D * z + D], acts.at[:, D * z : D * z + D]) for z in range(4)]
    sq_v[...] = jnp.zeros_like(sq_v)
    fill_triangles(tri_s)
    engine = Engine(0.65)
    reduce = Reduce(place, engine, r_send, r_recv, store_sem, sq_v)
    shares = []
    for at, (kind, first, units, column, width, by_units, early, z_first) in enumerate(share_plan()):
        grad, out = {"down": (gd_s, down_o), "up": (gu_s, up_o), "attn": (ga_s, attn_o)}[kind]
        cut = None
        if kind != "down":
            cut = out.at[first : first + units, :, :, column : column + width]
        mine = bufs[7 * at : 7 * at + 7]
        shares.append(
            Share(grad, first, units, column, width, by_units, early, z_first, mine, cut)
        )
    downs = shares[:3]
    shares = iter(shares)
    greet(place, corners=True)
    wait(first_in)

    for t in range(3):
        for z in range(PLANES):
            if t == 0:
                act_in[z].wait()
            if t == 0 and z == PLANES - 1:
                next_in = [
                    load(gb_h, gb), load(wdn_h, ga_s), load(slope_h, slope), load(low_t_h, left),
                ]
            starts = [D * z + 384 * y + 128 * t for y in range(2)]
            pair = [acts[:, start : start + 128] for start in starts]
            part = dot(wup[:, 0:rows_all], jnp.concatenate(pair, axis=1)).astype(bf16)
            for y in range(2):
                own = part[:, 128 * y : 128 * y + 128].reshape(8, 2, 48, 128)
                gd_s[:, z, y, :, :, 128 * t : 128 * t + 128] = own
            engine.tick(0.6)
        reduce.launch(next(shares))

    mid_in = [
        load(wup_h, wup), load(gr2_h, gr2), load(xhat_h, wide), load(rstd_h, rstd),
        load(norm_h, norm_s), load(sums_h, norm_v),
    ]
    late_in = [
        load(state_h, state_s),
        load(trig_h.at[ds((place.x * 2 + place.c) * PIECE, PIECE, PIECE), :], trig_s),
    ]
    for at, src in enumerate((q_h, k_h, v_h, att_h)):
        late_in.append(load(src, acts.at[:, D * at : D * at + D]))
    wait(next_in)
    for at in range(12):
        cols = slice(256 * at, 256 * at + 256)
        down_rows = ga_s[at // 3].reshape(D, D)[256 * (at % 3) : 256 * (at % 3) + 256]
        for part in range(0, rows_all, PIECE):
            span = slice(part, part + PIECE)
            grad = dot_nt(gb[span, :], down_rows) * slope[span, cols].astype(f32)
            slope[span, cols] = grad.astype(bf16)
        up = dot(left[...], slope[:, cols]).astype(bf16)
        gu_s[0, :, :, :, :, cols] = up.reshape(PLANES, 2, 2, 48, tile)
        engine.tick(1.4)
        if at % 4 == 3:
            reduce.launch(next(shares))
    att_t_in = load(att_t_h, left)
    wait(mid_in)
    gain_one = norm_s[0:1, :]
    norm_v[2:4, :] = norm_v[0:2, :]
    norm_v[0:2, :] = jnp.zeros((2, D), f32)

    def first_back(t, carry):
        cols = ds(t * tile, tile, tile)
        for part in range(0, rows_all, PIECE):
            span = slice(part, part + PIECE)
            gr2[span, cols] += dot_nt(slope[span, :], wup[cols, :])
        return carry

    def norm_part(t, carry):
        rows = ds(t * 128, 128, 128)
        unit, grad = wide[rows, :], gr2[rows, :]
        norm_v[0:1, :] += jnp.sum(grad * unit, axis=0, keepdims=True)
        norm_v[1:2, :] += jnp.sum(grad, axis=0, keepdims=True)
        grad = norm_back(grad * gain_one, unit, rstd[rows, 0:1])
        gr2[rows, :] = grad
        gb[rows, :] = grad.astype(bf16)
        return carry

    for part in range(3):
        lax.fori_loop(part, part + 1, first_back, 0)
        engine.tick(2.2)
    wo_in = load(wo_h, wup.at[:, 3 * D : 4 * D])
    wqkv_in = load(wqkv_h, wup.at[:, 0 : 3 * D])
    for part in range(0, rows_all // 128, 4):
        lax.fori_loop(part, part + 4, norm_part, 0)
        engine.tick(0.8)
    norms = Total(place, engine, "norms", norm_v, norm_w, norm_z, t_send, t_recv)
    rden_in = load(rden_h, wide)
    att_t_in.wait()

    def outer(unit, column, grad):
        part = dot(left[...], grad).astype(bf16)
        part = part.reshape(PLANES, 2, 2, 48, 256)
        ga_s[unit, :, :, :, :, column : column + 256] = part
        engine.tick(0.6)

    for t in range(3):
        outer(3, 256 * t, gb[:, 256 * t : 256 * t + 256])
    reduce.launch(next(shares))
    x_t_in = load(x_t_h, left)
    wait(late_in)
    rden_in.wait()
    wo_in.wait()
    square = (2 * PAIR, PAIR)
    row_half = (lax.broadcasted_iota(jnp.int32, square, 0) & (PAIR - 1)) < HEAD
    by_head = (row_half == first_half(square)).astype(f32).astype(bf16)

    def split(i, carry):
        g, t = i // 3, lax.rem(i, 3)
        rows = ds(g * PIECE, PIECE, PIECE)
        grad = dot_nt(gb[rows, :], wup[ds(t * tile, tile, tile), 3 * D : 4 * D])
        for pair in range(2):
            base = t * tile + pair * PAIR
            cols, num_cols = ds(base, PAIR, PAIR), ds(3 * D + base, PAIR, PAIR)
            mine = grad[:, pair * PAIR : pair * PAIR + PAIR]
            recip = wide[rows, cols]
            along = mine * acts[rows, num_cols].astype(f32)
            high = along.astype(bf16)
            rest = (along - high.astype(f32)).astype(bf16)
            gden = -dot(jnp.concatenate([high, rest], axis=1), by_head) * recip
            high = gden.astype(bf16).astype(f32)
            lane = lane_in_head(gden.shape)
            both = jnp.where(lane == 0, high, jnp.where(lane == 1, gden - high, 0.0))
            acts[rows, num_cols] = both.astype(bf16)
            slope[rows, num_cols] = (mine * recip).astype(bf16)
        return carry

    for part in range(0, blocks // 2, 2):
        lax.fori_loop(part, part + 2, split, 0)
        engine.tick(1.6)

    def column_of(b, group):
        return ds(group * D + lax.rem(b, 6) * PAIR, PAIR, PAIR)

    def local(b, carry):
        rows, cols = block_of(b)
        queries = turned(acts[rows, cols], trig_s[...])
        state = dot_tn(queries, slope[rows, column_of(b, 3)])
        cross = dot_tn(acts[rows, column_of(b, 3)], queries)
        shape = (PAIR, 2 * PAIR)
        kept = jnp.where(top_half(shape) == pair_mask(shape), cross, 0.0)
        totals = jnp.broadcast_to(jnp.sum(kept, axis=0, keepdims=True), (16, 2 * PAIR))
        st_own[b] = squeeze_state(state, totals).astype(bf16)
        return carry

    for part in range(0, blocks, 4):
        lax.fori_loop(part, part + 4, local, 0)
        engine.tick(1.5)
    state = StateSum(place, engine, s_send, s_recv, st_own, st_twin, st_chip, st_prior, True)

    def soft_slope(feature):
        return 1.0 - jnp.exp(-feature.astype(f32))

    def take(b):
        rows, cols = block_of(b)
        num, den = slope[rows, column_of(b, 3)], acts[rows, column_of(b, 3)]
        q, k, v = (acts[rows, column_of(b, group)] for group in range(3))
        return jnp.concatenate([num, den], axis=1), num, q, k, v

    def query_grad(i, carry):
        marks = [2 * i, 2 * i + 1]
        taken = [take(b) + (state_s[b],) for b in marks]
        outs = []
        for own, _, q, k, v, packed in taken:
            grad = causal_product(own, with_ones(v), turned(k, trig_s[...]), tri_s)
            grad = (grad + dot_nt(own, spread_state(packed))) * trig_s[...]
            outs.append(((grad[:, :PAIR] + grad[:, PAIR:]) * soft_slope(q)).astype(bf16))
        for b, out in zip(marks, outs):
            slope[block_of(b)] = out
        return carry

    for part in range(blocks // 2):
        lax.fori_loop(part, part + 1, query_grad, 0)
        engine.tick(2.6)
    x_t_in.wait()
    for t in range(3):
        outer(0, 256 * t, slope[:, 256 * t : 256 * t + 256])
    reduce.launch(next(shares))
    engine.until("state")

    def key_pair(t):
        def body(g, carry):
            marks = [g * 6 + 2 * t, g * 6 + 2 * t + 1]
            taken = [take(b) + (state.total(b).astype(bf16),) for b in marks]
            outs = []
            for own, num, q, k, v, packed in taken:
                queries, keys = turned(q, trig_s[...]), turned(k, trig_s[...])
                spread = spread_state(packed)
                grad = causal_transposed(own, with_ones(v), queries, tri_s)
                one = (lane_in_head(v.shape) == 0).astype(f32).astype(bf16)
                grad = (grad + dot_nt(jnp.concatenate([v, one], axis=1), spread)) * trig_s[...]
                grad = (grad[:, :PAIR] + grad[:, PAIR:]) * soft_slope(k)
                grad_v = causal_transposed(queries, keys, num, tri_s)
                grad_v = grad_v + dot(keys, spread[:, :PAIR])
                outs.append((grad.astype(bf16), grad_v.astype(bf16)))
            for b, (grad, grad_v) in zip(marks, outs):
                rows, _ = block_of(b)
                slope[rows, column_of(b, 1)] = grad
                slope[rows, column_of(b, 2)] = grad_v
            return carry

        return body

    for t in range(3):
        for part in range(blocks // 6):
            lax.fori_loop(part, part + 1, key_pair(t), 0)
            engine.tick(4.4)
        for j in (1, 2):
            outer(j, 256 * t, slope[:, D * j + 256 * t : D * j + 256 * t + 256])
        reduce.launch(next(shares))
    wqkv_in.wait()

    def input_grad(t, carry):
        cols = ds(t * tile, tile, tile)
        for part in range(0, rows_all, PIECE):
            span = slice(part, part + PIECE)
            gr2[span, cols] += dot_nt(slope[span, 0 : 3 * D], wup[cols, 0 : 3 * D])
        return carry

    for part in range(3):
        lax.fori_loop(part, part + 1, input_grad, 0)
        engine.tick(1.8)
    stores = [
        pltpu.make_async_copy(gr2, input_o, load_sem.at[count[0]]),
        pltpu.make_async_copy(norm_v, norm_o, load_sem.at[count[0] + 1]),
    ]
    engine.until("norms", ("whole", 0), ("whole", 1), ("whole", 2))
    for at, share in enumerate(downs):
        span = slice(128 * at, 128 * at + 128)
        gb[span, :] = share.final[...].reshape(D, 128).T
    stores.append(
        pltpu.make_async_copy(gb.at[0 : FF // 8, :], down_o, load_sem.at[count[0] + 3])
    )
    for copy in stores:
        copy.start()
    engine.until(*[("sum", k) for k in range(SHARES)])
    squares = Total(place, engine, "squares", sq_v, sq_w, sq_z, u_send, u_recv)
    engine.until("squares")
    stores.append(pltpu.make_async_copy(sq_v, square_o, load_sem.at[count[0] + 2]))
    stores[-1].start()
    engine.rest()
    wait(stores)
    reduce.drain()
    norms.drain()
    squares.drain()
    state.drain()


def share_plan():
    plan = [("down", 0, 8, 128 * t, 128) for t in range(3)]
    plan += [("up", 0, 1, FF // 3 * t, FF // 3) for t in range(3)]
    plan += [("attn", 3, 1, 0, D), ("attn", 0, 1, 0, D)]
    plan += [("attn", 1, 2, 256 * t, 256) for t in range(3)]
    return [
        part + (part[0] == "down", 1 if at in (1, 3, 5, 7, 9) else 2, at in (2,)) for at, part in enumerate(plan)
    ]


SHARES = 11


def backward_call(s, norm_params, seq_count):
    rows = s["q"].shape[0]
    blocks = rows // PIECE * 6
    trig = turning_table(seq_count)
    names = (
        "wqkv", "wo", "wup", "q", "k", "v", "att", "rden", "xhat", "rstd", "x_t", "att_t",
        "low_t", "act", "slope", "gb", "gb_t", "gr2", "state", "sums",
    )
    wdn = s["wdn"].reshape(4, PLANES, 2, 2, 48, D)
    shapes = [
        ((rows, D), f32),
        ((4, 2, 48, D), bf16), ((1, 2, 48, FF), bf16), ((FF // 8, D), bf16),
        ((8, D), f32), ((8, 128), f32),
    ]
    vmem = [
        ((D, FF), bf16), ((rows, FF), bf16), ((rows, FF), bf16), ((rows, D), f32),
        ((rows, D), bf16), ((D, rows), bf16), ((rows, D), f32), ((rows, 128), f32),
        ((4, PLANES, 2, 2, 48, D), bf16), ((8, PLANES, 2, 2, 48, FF // 8), bf16),
        ((1, PLANES, 2, 2, 48, FF), bf16),
        ((4, D), f32), ((PIECE, 2 * PAIR), f32), ((PIECE, PIECE // 2), bf16),
        ((blocks, 144, PAIR), bf16), ((blocks, 144, PAIR), bf16), ((blocks, 144, PAIR), bf16),
        ((blocks, 144, PAIR), bf16), ((blocks, 144, PAIR), bf16),
        ((8, D), f32), ((8, 8, D), f32), ((PLANES, 8, D), f32),
        ((8, 128), f32), ((8, 8, 128), f32), ((PLANES, 8, 128), f32),
    ]
    for _, _, units, _, width, by_units, early, z_first in share_plan():
        count, part = (units // 2, width) if by_units else (units, width // 2)
        if z_first:
            vmem += [
                ((units, PLANES, 2, 48, width), bf16), ((count, 48, part), bf16),
                ((units, 48, width), bf16), ((16, 128), bf16), ((16, 128), bf16),
                ((units, 3, 2, 48, width), bf16), ((units, 2, 48, width), bf16),
            ]
            continue
        vmem += [
            ((units, PLANES, 2, 48, width), bf16), ((count, PLANES, 48, part), bf16),
            ((count, PLANES, 48, part), bf16), ((count, early, 48, part), bf16),
            ((count, PLANES - early, 48, part), bf16), ((count, 3, 48, part), bf16),
            ((units, 2, 48, width), bf16),
        ]
    dma = pltpu.SemaphoreType.DMA
    sems = [(36,), (SHARES,), (SHARES, 12), (SHARES, 12), (3,), (3,), (10,), (10,), (10,), (10,)]
    hbm = pl.BlockSpec(memory_space=pl.ANY)
    return pl.pallas_call(
        backward_kernel,
        out_shape=[jax.ShapeDtypeStruct(*shape) for shape in shapes],
        in_specs=[hbm] * 23,
        out_specs=[hbm] * len(shapes),
        scratch_shapes=[pltpu.VMEM(*shape) for shape in vmem] + [dma(shape) for shape in sems],
        compiler_params=pltpu.CompilerParams(
            collective_id=1, has_side_effects=True, vmem_limit_bytes=VMEM_BYTES
        ),
        name="backward_reduce",
    )(*[s[name] for name in names], wdn, norm_params, trig)


def adam_step(weight, grad, first, second, rate, outs):
    first_new = beta_one * first + (1.0 - beta_one) * grad
    second_new = beta_two * second + (1.0 - beta_two) * grad * grad
    first_hat = first_new * (1.0 / (1.0 - beta_one**STEP))
    second_hat = second_new * (1.0 / (1.0 - beta_two**STEP))
    step = first_hat / (jnp.sqrt(second_hat) + epsilon) + weight_decay * weight
    for ref, value in zip(outs, (grad, weight - rate * step, first_new, second_new)):
        ref[...] = value.reshape(ref.shape)


def update_kernel(
    out_rate, steps,
    layer_h, input_h, attn_r, up_r, down_r, norm_r, square_r,
    attn_w, up_w, down_w, norm_w, attn_m, up_m, down_m, norm_m, attn_v, up_v, down_v, norm_v,
    layer_o, input_o, attn_g, up_g, down_g, norm_g, grad_norm_o,
    attn_n, up_n, down_n, norm_n, attn_f, up_f, down_f, norm_f, attn_s, up_s, down_s, norm_s,
    grad_s, layer_s, input_s, copy_sem,
):
    norm_raw = norm_r[0:4, :]
    pairs = [(layer_h, layer_s, layer_o), (input_h, input_s, input_o)]
    inward = [
        pltpu.make_async_copy(src, mid, copy_sem.at[at]) for at, (src, mid, _) in enumerate(pairs)
    ]
    outward = [
        pltpu.make_async_copy(mid, dst, copy_sem.at[2 + at])
        for at, (_, mid, dst) in enumerate(pairs)
    ]

    @pl.when(pl.program_id(0) == 0)
    def _():
        for copy in inward:
            copy.start()

    grad_norm = jnp.sqrt(
        jnp.sum(square_r[...], keepdims=True) + jnp.sum(norm_raw * norm_raw, keepdims=True)
    )
    clip = clip_limit / jnp.maximum(grad_norm, clip_limit)
    grad_norm_o[...] = grad_norm
    down_rate = learn_rate * math.sqrt(D / FF)
    grad = up_r[...].astype(f32) * clip
    adam_step(up_w[...], grad, up_m[...], up_v[...], learn_rate, (up_g, up_n, up_f, up_s))
    grad = down_r[...].astype(f32) * clip
    outs = (down_g, down_n, down_f, down_s)
    adam_step(down_w[...], grad, down_m[...], down_v[...], down_rate, outs)
    count = attn_w.shape[0]
    shape = (4 * count, D)
    for j in range(4):
        part = attn_r[j].astype(f32)
        for t in range(D // 128):
            span = pl.ds(4 * count * t + j, count, stride=4)
            grad_s[span, :] = part[:, 128 * t : 128 * t + 128]
    grad = jnp.concatenate(
        [grad_s[4 * count * t : 4 * count * (t + 1), :] for t in range(D // 128)], axis=1
    )
    row = lax.broadcasted_iota(jnp.int32, shape, 0)
    rate = jnp.where((row & 3) == 3, learn_rate * out_rate, learn_rate)
    flat = [ref[...].reshape(shape) for ref in (attn_w, attn_m, attn_v)]
    outs = (attn_g, attn_n, attn_f, attn_s)
    adam_step(flat[0], grad * clip, flat[1], flat[2], rate, outs)
    outs = (norm_g, norm_n, norm_f, norm_s)
    adam_step(norm_w[...], norm_raw * clip, norm_m[...], norm_v[...], gain_rate, outs)

    @pl.when(pl.program_id(0) == 1)
    def _():
        for taken, given in zip(inward, outward):
            taken.wait()
            given.start()

    @pl.when(pl.program_id(0) == steps - 1)
    def _():
        for copy in outward:
            copy.wait()


def update_call(layer_output, input_grad, raw, norm_raw, square, weights, firsts, seconds, length):
    steps = 6
    thin, thick = weights[0].shape[0], weights[2].shape[0]
    a, u, d = thin // steps, thin // steps, thick // steps
    attn = pl.BlockSpec((a, 4, D), lambda t: (t, 0, 0))
    up = pl.BlockSpec((u, FF), lambda t: (t, 0))
    down = pl.BlockSpec((d, D), lambda t: (t, 0))
    whole = lambda rows, cols: pl.BlockSpec((rows, cols), lambda t: (0, 0))
    norm = whole(4, D)
    kinds = [attn, up, down, norm]
    shapes = [jax.ShapeDtypeStruct(w.shape, f32) for w in weights]
    one = jax.ShapeDtypeStruct((1, 1), f32)
    hbm = pl.BlockSpec(memory_space=pl.ANY)
    through = [jax.ShapeDtypeStruct(v.shape, v.dtype) for v in (layer_output, input_grad)]
    return pl.pallas_call(
        functools.partial(update_kernel, math.sqrt(length // 8), steps),
        grid=(steps,),
        in_specs=[hbm, hbm, pl.BlockSpec((4, a, D), lambda t: (0, t, 0)), up, down]
        + [whole(8, D), whole(8, 128)]
        + kinds * 3,
        out_specs=[hbm, hbm] + kinds + [whole(1, 1)] + kinds * 3,
        out_shape=through + shapes + [one] + shapes * 3,
        scratch_shapes=[
            pltpu.VMEM((4 * a * D // 128, 128), f32),
            pltpu.VMEM(layer_output.shape, bf16), pltpu.VMEM(input_grad.shape, f32),
            pltpu.SemaphoreType.DMA((4,)),
        ],
        compiler_params=pltpu.CompilerParams(vmem_limit_bytes=VMEM_BYTES),
        name="adamw_update",
    )(layer_output, input_grad, *raw, norm_raw, square, *weights, *firsts, *seconds)


def prefix(part, axis, combine, identity):
    place = lax.axis_index(axis)
    gathered = jax.tree.map(lambda a: lax.all_gather(a, axis), part)
    state = jax.tree.map(lambda a, e: jnp.zeros_like(a) + jnp.asarray(e, a.dtype), part, identity)

    def prefix_one(step, state):
        return combine(
            state, jax.tree.map(lambda a: lax.dynamic_index_in_dim(a, step, 0, False), gathered)
        )

    return lax.fori_loop(0, place, prefix_one, state)


def carried_in(shard, axis, join, neutral):
    count = lax.axis_size(axis)
    place = lax.axis_index(axis)
    ahead = count - 1 - place
    gathered = jax.tree.map(
        lambda a, kind: lax.all_gather(a.astype(kind), axis),
        shard,
        jax.tree.map(lambda a: jnp.bfloat16 if a.dtype == jnp.float32 else a.dtype, shard),
    )
    state = jax.tree.map(lambda a, e: jnp.zeros_like(a) + jnp.asarray(e, a.dtype), shard, neutral)

    def carried_one(step, state):
        source = count - 1 - step
        return join(
            state,
            jax.tree.map(
                lambda a, own: lax.dynamic_index_in_dim(a, source, 0, False).astype(own.dtype),
                gathered,
                shard,
            ),
        )

    return lax.fori_loop(0, ahead, carried_one, state)


def add_states(earlier, later):
    return jax.tree.map(jnp.add, earlier, later)


def layer_norm(values, gain_row, bias_row):
    centered = values - jnp.mean(values, axis=-1, keepdims=True)
    spread = jnp.mean(centered * centered, axis=-1, keepdims=True)
    return centered * lax.rsqrt(spread + norm_eps) * gain_row + bias_row


def piece_scores(query_cos, query_sin, key_cos, key_sin, causal):
    scores = jnp.einsum("ihe,jhe->hij", query_cos, key_cos, preferred_element_type=jnp.float32)
    scores = scores + jnp.einsum(
        "ihe,jhe->hij", query_sin, key_sin, preferred_element_type=jnp.float32
    )
    return jnp.where(causal[None], scores, 0.0)


def adamw(weight, gradient, first_moment, second, step_rate):
    first_new = beta_one * first_moment + (1.0 - beta_one) * gradient
    second_new = beta_two * second + (1.0 - beta_two) * gradient * gradient
    first_hat = first_new / (1.0 - beta_one**STEP)
    second_hat = second_new / (1.0 - beta_two**STEP)
    weight_new = weight - step_rate * (
        first_hat / (jnp.sqrt(second_hat) + epsilon) + weight_decay * weight
    )
    return (weight_new, first_new, second_new)


def plain_shards(
    layer_input,
    cotangent,
    attn_master,
    up_master,
    down_master,
    norm_params,
    attn_first,
    up_first,
    down_first,
    norm_first,
    attn_second,
    up_second,
    down_second,
    norm_second,
):
    groups, piece_rows, model_width = layer_input.shape
    head_count = model_width // HEAD
    length = piece_rows * lax.axis_size("seq")
    rows_all = groups * piece_rows
    attn_full, up_full, down_full = (
        lax.all_gather(attn_master.astype(jnp.bfloat16), "dp", axis=0, tiled=True),
        lax.all_gather(up_master.astype(jnp.bfloat16), "dp", axis=0, tiled=True),
        lax.all_gather(down_master.astype(jnp.bfloat16), "dp", axis=0, tiled=True),
    )
    project_in = attn_full[:, :3, :].reshape(model_width, 3 * model_width)
    out_weight = attn_full[:, 3, :]
    tokens = layer_input.reshape(rows_all, model_width)
    projected = jnp.dot(tokens, project_in, preferred_element_type=jnp.float32)
    query_pre = projected[:, :model_width]
    key_pre = projected[:, model_width : 2 * model_width]
    value_pre = projected[:, 2 * model_width :]
    position = (lax.axis_index("seq") * piece_rows + jnp.arange(piece_rows)).astype(jnp.float32)
    phase_angle = math.pi / 2 * position / length
    cosine_weight = jnp.tile(jnp.cos(phase_angle), groups)[:, None]
    sine_weight = jnp.tile(jnp.sin(phase_angle), groups)[:, None]
    query_feat = jax.nn.softplus(query_pre)
    key_feat = jax.nn.softplus(key_pre)
    shape_four = (groups, piece_rows, head_count, HEAD)
    query_cos = (query_feat * cosine_weight).astype(jnp.bfloat16).reshape(shape_four)
    query_sin = (query_feat * sine_weight).astype(jnp.bfloat16).reshape(shape_four)
    key_cos = (key_feat * cosine_weight).astype(jnp.bfloat16).reshape(shape_four)
    key_sin = (key_feat * sine_weight).astype(jnp.bfloat16).reshape(shape_four)
    values = value_pre.astype(jnp.bfloat16).reshape(shape_four)
    local_state = (
        jnp.stack(
            [
                jnp.einsum("gjhe,gjhf->ghef", key_cos, values, preferred_element_type=jnp.float32),
                jnp.einsum("gjhe,gjhf->ghef", key_sin, values, preferred_element_type=jnp.float32),
            ],
            axis=1,
        ),
        jnp.stack(
            [
                jnp.sum(key_cos, axis=1, dtype=jnp.float32),
                jnp.sum(key_sin, axis=1, dtype=jnp.float32),
            ],
            axis=1,
        ),
    )
    identity = jax.tree.map(jnp.zeros_like, local_state)
    prior_state, prior_total = prefix(
        (local_state[0], local_state[1]), "seq", add_states, (identity[0], identity[1])
    )
    causal = jnp.arange(piece_rows)[:, None] >= jnp.arange(piece_rows)[None, :]
    attended_list = []
    denominator_list = []
    for group_index in range(groups):
        scores = piece_scores(
            query_cos[group_index],
            query_sin[group_index],
            key_cos[group_index],
            key_sin[group_index],
            causal,
        )
        qcos_wide = query_cos[group_index].astype(jnp.float32)
        qsin_wide = query_sin[group_index].astype(jnp.float32)
        numerator = jnp.einsum(
            "hij,jhe->ihe",
            scores.astype(jnp.bfloat16),
            values[group_index],
            preferred_element_type=jnp.float32,
        )
        numerator = numerator + jnp.einsum(
            "ihe,hef->ihf", qcos_wide, prior_state[group_index, 0], precision=highest
        )
        numerator = numerator + jnp.einsum(
            "ihe,hef->ihf", qsin_wide, prior_state[group_index, 1], precision=highest
        )
        denominator = jnp.sum(scores, axis=-1).T
        denominator = denominator + jnp.einsum(
            "ihe,he->ih", qcos_wide, prior_total[group_index, 0], precision=highest
        )
        denominator = denominator + jnp.einsum(
            "ihe,he->ih", qsin_wide, prior_total[group_index, 1], precision=highest
        )
        attended_list.append(numerator / denominator[:, :, None])
        denominator_list.append(denominator)
    attended = jnp.stack(attended_list)
    attended_low = attended.reshape(rows_all, model_width).astype(jnp.bfloat16)
    branch_one = jnp.dot(attended_low, out_weight, preferred_element_type=jnp.float32)
    residual_one = tokens.astype(jnp.float32) + branch_one
    first_norm, norm_one_back = jax.vjp(layer_norm, residual_one, norm_params[0], norm_params[1])
    first_low = first_norm.astype(jnp.bfloat16)
    hidden = jnp.dot(first_low, up_full, preferred_element_type=jnp.float32)
    activated, gelu_back = jax.vjp(jax.nn.gelu, hidden)
    activated_low = activated.astype(jnp.bfloat16)
    branch_two = jnp.dot(activated_low, down_full, preferred_element_type=jnp.float32)
    result, norm_two_back = jax.vjp(
        layer_norm, first_norm + branch_two, norm_params[2], norm_params[3]
    )
    layer_output = result.astype(jnp.bfloat16).reshape(groups, piece_rows, model_width)
    grad_residual_two, grad_gain_two, grad_bias_two = norm_two_back(
        cotangent.reshape(rows_all, model_width).astype(jnp.float32)
    )
    grad_branch_two = grad_residual_two.astype(jnp.bfloat16)
    grad_down = jnp.einsum(
        "nf,nd->fd", activated_low, grad_branch_two, preferred_element_type=jnp.float32
    )
    grad_activated = jnp.einsum(
        "nd,fd->nf", grad_branch_two, down_full, preferred_element_type=jnp.float32
    )
    grad_hidden = gelu_back(grad_activated)[0].astype(jnp.bfloat16)
    grad_up = jnp.einsum("nd,nf->df", first_low, grad_hidden, preferred_element_type=jnp.float32)
    grad_first = grad_residual_two + jnp.einsum(
        "nf,df->nd", grad_hidden, up_full, preferred_element_type=jnp.float32
    )
    grad_residual_one, grad_gain_one, grad_bias_one = norm_one_back(grad_first)
    grad_branch_one = grad_residual_one.astype(jnp.bfloat16)
    grad_out_weight = jnp.einsum(
        "nd,ne->de", attended_low, grad_branch_one, preferred_element_type=jnp.float32
    )
    grad_attended = jnp.einsum(
        "ne,de->nd", grad_branch_one, out_weight, preferred_element_type=jnp.float32
    ).reshape(shape_four)
    grad_qcos_list = []
    grad_qsin_list = []
    grad_kcos_list = []
    grad_ksin_list = []
    grad_values_list = []
    prior_grad_state = []
    prior_grad_total = []
    for group_index in range(groups):
        denominator = denominator_list[group_index]
        grad_numerator = (grad_attended[group_index] / denominator[:, :, None]).astype(jnp.bfloat16)
        grad_denominator = (
            -jnp.sum(grad_attended[group_index] * attended[group_index], axis=-1) / denominator
        )
        scores = piece_scores(
            query_cos[group_index],
            query_sin[group_index],
            key_cos[group_index],
            key_sin[group_index],
            causal,
        )
        grad_scores = (
            jnp.einsum(
                "ihe,jhe->hij",
                grad_numerator,
                values[group_index],
                preferred_element_type=jnp.float32,
            )
            + grad_denominator.T[:, :, None]
        )
        grad_scores = jnp.where(causal[None], grad_scores, 0.0).astype(jnp.bfloat16)
        grad_numerator_wide = grad_numerator.astype(jnp.float32)
        grad_qcos = jnp.einsum(
            "hij,jhe->ihe", grad_scores, key_cos[group_index], preferred_element_type=jnp.float32
        )
        grad_qcos = grad_qcos + jnp.einsum(
            "ihf,hef->ihe", grad_numerator_wide, prior_state[group_index, 0], precision=highest
        )
        grad_qcos = grad_qcos + grad_denominator[:, :, None] * prior_total[group_index, 0][None]
        grad_qsin = jnp.einsum(
            "hij,jhe->ihe", grad_scores, key_sin[group_index], preferred_element_type=jnp.float32
        )
        grad_qsin = grad_qsin + jnp.einsum(
            "ihf,hef->ihe", grad_numerator_wide, prior_state[group_index, 1], precision=highest
        )
        grad_qsin = grad_qsin + grad_denominator[:, :, None] * prior_total[group_index, 1][None]
        grad_qcos_list.append(grad_qcos)
        grad_qsin_list.append(grad_qsin)
        grad_kcos_list.append(
            jnp.einsum(
                "hij,ihe->jhe",
                grad_scores,
                query_cos[group_index],
                preferred_element_type=jnp.float32,
            )
        )
        grad_ksin_list.append(
            jnp.einsum(
                "hij,ihe->jhe",
                grad_scores,
                query_sin[group_index],
                preferred_element_type=jnp.float32,
            )
        )
        grad_values_list.append(
            jnp.einsum(
                "hij,ihe->jhe",
                scores.astype(jnp.bfloat16),
                grad_numerator,
                preferred_element_type=jnp.float32,
            )
        )
        prior_grad_state.append(
            jnp.stack(
                [
                    jnp.einsum(
                        "ihe,ihf->hef",
                        query_cos[group_index],
                        grad_numerator,
                        preferred_element_type=jnp.float32,
                    ),
                    jnp.einsum(
                        "ihe,ihf->hef",
                        query_sin[group_index],
                        grad_numerator,
                        preferred_element_type=jnp.float32,
                    ),
                ]
            )
        )
        prior_grad_total.append(
            jnp.stack(
                [
                    jnp.einsum(
                        "ihe,ih->he",
                        query_cos[group_index].astype(jnp.float32),
                        grad_denominator,
                        precision=highest,
                    ),
                    jnp.einsum(
                        "ihe,ih->he",
                        query_sin[group_index].astype(jnp.float32),
                        grad_denominator,
                        precision=highest,
                    ),
                ]
            )
        )
    later_state, later_total = carried_in(
        (jnp.stack(prior_grad_state), jnp.stack(prior_grad_total)),
        "seq",
        add_states,
        (identity[0], identity[1]),
    )
    values_wide = values.astype(jnp.float32)
    kcos_wide = key_cos.astype(jnp.float32)
    ksin_wide = key_sin.astype(jnp.float32)
    grad_kcos = (
        jnp.stack(grad_kcos_list)
        + jnp.einsum("gjhf,ghef->gjhe", values_wide, later_state[:, 0], precision=highest)
        + later_total[:, 0][:, None]
    )
    grad_ksin = (
        jnp.stack(grad_ksin_list)
        + jnp.einsum("gjhf,ghef->gjhe", values_wide, later_state[:, 1], precision=highest)
        + later_total[:, 1][:, None]
    )
    grad_values = jnp.stack(grad_values_list)
    grad_values = grad_values + jnp.einsum(
        "gjhe,ghef->gjhf", kcos_wide, later_state[:, 0], precision=highest
    )
    grad_values = grad_values + jnp.einsum(
        "gjhe,ghef->gjhf", ksin_wide, later_state[:, 1], precision=highest
    )
    grad_query = (
        jnp.stack(grad_qcos_list).reshape(rows_all, model_width) * cosine_weight
        + jnp.stack(grad_qsin_list).reshape(rows_all, model_width) * sine_weight
    )
    grad_keys = (
        grad_kcos.reshape(rows_all, model_width) * cosine_weight
        + grad_ksin.reshape(rows_all, model_width) * sine_weight
    )
    grad_projected = jnp.concatenate(
        [
            (grad_query * jax.nn.sigmoid(query_pre)).astype(jnp.bfloat16),
            (grad_keys * jax.nn.sigmoid(key_pre)).astype(jnp.bfloat16),
            grad_values.reshape(rows_all, model_width).astype(jnp.bfloat16),
        ],
        axis=1,
    )
    input_grad = grad_residual_one + jnp.einsum(
        "nk,dk->nd", grad_projected, project_in, preferred_element_type=jnp.float32
    )
    input_grad = input_grad.reshape(groups, piece_rows, model_width)
    grad_in = jnp.einsum("nd,nk->dk", tokens, grad_projected, preferred_element_type=jnp.float32)
    grad_attn = jnp.concatenate(
        [grad_in.reshape(model_width, 3, model_width), grad_out_weight[:, None, :]], axis=1
    )
    norm_grad_local = jnp.stack([grad_gain_one, grad_bias_one, grad_gain_two, grad_bias_two])
    norm_grad_raw = lax.psum(norm_grad_local, ("dp", "seq"))
    row_blocks = (
        lax.psum_scatter(
            grad_attn.astype(jnp.bfloat16), "dp", scatter_dimension=0, tiled=True
        ).astype(jnp.float32),
        lax.psum_scatter(
            grad_up.astype(jnp.bfloat16), "dp", scatter_dimension=0, tiled=True
        ).astype(jnp.float32),
        lax.psum_scatter(
            grad_down.astype(jnp.bfloat16), "dp", scatter_dimension=0, tiled=True
        ).astype(jnp.float32),
    )
    shard_attn, shard_up, shard_down = (
        lax.psum(row_blocks[0].astype(jnp.bfloat16), "seq").astype(jnp.float32),
        lax.psum(row_blocks[1].astype(jnp.bfloat16), "seq").astype(jnp.float32),
        lax.psum(row_blocks[2].astype(jnp.bfloat16), "seq").astype(jnp.float32),
    )
    local_square = (
        jnp.sum(shard_attn * shard_attn)
        + jnp.sum(shard_up * shard_up)
        + jnp.sum(shard_down * shard_down)
    )
    square = lax.psum(local_square, "dp") + jnp.sum(norm_grad_raw * norm_grad_raw)
    grad_norm = jnp.sqrt(square)
    clip_scale = clip_limit / jnp.maximum(grad_norm, clip_limit)
    attn_grad = shard_attn * clip_scale
    up_grad = shard_up * clip_scale
    down_grad = shard_down * clip_scale
    norm_grad = norm_grad_raw * clip_scale
    attn_rate = (
        learn_rate * jnp.array([1.0, 1.0, 1.0, math.sqrt(length // 8)], jnp.float32)[None, :, None]
    )
    attn_new, attn_first_new, attn_second_new = adamw(
        attn_master, attn_grad, attn_first, attn_second, attn_rate
    )
    up_new, up_first_new, up_second_new = adamw(up_master, up_grad, up_first, up_second, learn_rate)
    down_new, down_first_new, down_second_new = adamw(
        down_master, down_grad, down_first, down_second, learn_rate * math.sqrt(D / FF)
    )
    norm_new, norm_first_new, norm_second_new = adamw(
        norm_params, norm_grad, norm_first, norm_second, gain_rate
    )
    return (
        layer_output,
        input_grad,
        attn_grad,
        up_grad,
        down_grad,
        norm_grad,
        grad_norm,
        attn_new,
        up_new,
        down_new,
        norm_new,
        attn_first_new,
        up_first_new,
        down_first_new,
        norm_first_new,
        attn_second_new,
        up_second_new,
        down_second_new,
        norm_second_new,
    )


def fused_shards(
    layer_input, cotangent, attn_master, up_master, down_master, norm_params,
    attn_first, up_first, down_first, norm_first,
    attn_second, up_second, down_second, norm_second,
):
    groups, piece_rows, model_width = layer_input.shape
    seq_count = lax.axis_size("seq")
    rows = groups * piece_rows
    weights = (attn_master, up_master, down_master, norm_params)
    saved = forward_call(
        layer_input.reshape(rows, model_width), cotangent.reshape(rows, model_width),
        *weights, seq_count,
    )
    input_grad, attn, up, down, norm_raw, square = backward_call(saved, norm_params, seq_count)
    raw = (attn.reshape(4, -1, D), up.reshape(-1, FF), down)
    layer_output, input_grad, *outs = update_call(
        saved["out"], input_grad, raw, norm_raw, square, weights,
        (attn_first, up_first, down_first, norm_first),
        (attn_second, up_second, down_second, norm_second), piece_rows * seq_count,
    )
    return (
        layer_output.reshape(layer_input.shape), input_grad.reshape(layer_input.shape),
        *outs[:4], outs[4].reshape(()), *outs[5:],
    )


def shards(*args):
    groups, piece_rows, model_width = args[0].shape
    planes = lax.axis_size("dp") // 2
    if piece_rows == PIECE and planes == PLANES and lax.axis_size("seq") == 4:
        return fused_shards(*args)
    return plain_shards(*args)


def solution(mesh):
    in_specs = (
        P("dp", "seq", None),
        P("dp", "seq", None),
        P("dp", None, None),
        P("dp", None),
        P("dp", None),
        P(),
        P("dp", None, None),
        P("dp", None),
        P("dp", None),
        P(),
        P("dp", None, None),
        P("dp", None),
        P("dp", None),
        P(),
    )
    out_specs = (
        P("dp", "seq", None),
        P("dp", "seq", None),
        P("dp", None, None),
        P("dp", None),
        P("dp", None),
        P(),
        P(),
        P("dp", None, None),
        P("dp", None),
        P("dp", None),
        P(),
        P("dp", None, None),
        P("dp", None),
        P("dp", None),
        P(),
        P("dp", None, None),
        P("dp", None),
        P("dp", None),
        P(),
    )
    return jax.shard_map(shards, mesh=mesh, in_specs=in_specs, out_specs=out_specs, check_vma=False)
```
